128 devices in a mesh: dp: 32 (over x, y, core), seq: 4 (over z).
Axes of the slice: x: 4, y: 4, z: 4, core: 2. Of those that a mesh axis runs over, the one named last changes fastest.
Arguments:
- tokens: bfloat16 [32, 512, 1280], P('dp', 'seq'), may hold values from -6 to 6
- segment_ids: int32 [32, 512], P('dp', 'seq'), may hold values from 0 to 7, never falling along the last dimension, each value on 1 to 384 neighbouring positions
- expert_ids: int32 [32, 512, 2], P('dp', 'seq'), may hold values from 0 to 31, all different within a row; in each aligned block of 128 rows (0 to 127, 128 to 255, ..., all dimensions but the last counted through in order) at most 9 rows name the same one
- gate_values: float32 [32, 512, 2], P('dp', 'seq'), may hold values from 0.2 to 1
- ln_attn: float32 [1280], replicated, may hold values from 0.4 to 1.6
- w_qkv: bfloat16 [1280, 3840], replicated, may hold values from -1 to 1
- w_attn_out: bfloat16 [1280, 1280], replicated, may hold values from -0.15625 to 0.15625
- ln_expert: float32 [1280], replicated, may hold values from 0.4 to 1.6
- w_in: bfloat16 [32, 1280, 5120], P('dp', None, 'seq'), may hold values from -0.15625 to 0.15625
- w_out: bfloat16 [32, 5120, 1280], P('dp', 'seq'), may hold values from -0.078125 to 0.078125
Outputs:
- encoded: bfloat16 [32, 512, 1280], P('dp', 'seq')
The draws below stay inside these ranges and needn't reach their ends.
Inputs may be any that keep to these rules, and one draw needn't show every extreme that they name: `segment_ids`: segment numbers never fall along a pack; each image holds 1 to 384 patches and one image of each pack exactly 384. `expert_ids`: a patch's two experts differ; among the patches of one device no expert is named more than 9 times, a bound that some block reaches.
All inputs are finite; a program needn't handle non-finite values.
Results may differ from the reference program's by a relative error of at most 0.009.
Values may be sent and summed in bfloat16 or wider, within the bound.
A program may use at most 128 MiB of HBM per device.

```python
import math
import jax
import jax.numpy as jnp
import numpy as np
from jax import lax

D = 1280
HEADS = 16
HEAD_DIM = 80
FF = 5120
TOP = 2
EXPERTS = 32
TOK_DEV = 128
PACK_LEN = 512
PACKS = 32
BLOCKS = 128
CAP = 9
SEGS = 8
SEG_MOST = 384


def draw_w_qkv(key, part):
    key = jax.random.fold_in(key, 7)
    key_base, key_noise, key_value = jax.random.split(key, 3)
    base = jax.random.normal(key_base, (D, D), jnp.float32) * D ** (-0.5)
    noise = jax.random.normal(key_noise, (D, D), jnp.float32) * D ** (-0.5)
    value = jax.random.normal(key_value, (D, D), jnp.float32) * D ** (-0.5)
    query_part = base
    key_part = noise
    whole = jnp.concatenate([query_part, key_part, value], axis=1)
    return jnp.clip(whole, -1.0, 1.0).astype(jnp.bfloat16)


def steps_of(key, extent, shards, smallest, high):
    level, own = 1.0, jax.random.fold_in(key, 6)
    for dim, shards_of in shards:
        heights = jnp.exp(jax.random.uniform(jax.random.fold_in(own, dim), (shards_of,), jnp.float32, smallest / len(shards), high / len(shards)))
        level = level * jnp.repeat(heights, extent[dim] // shards_of).reshape([-1 if axis == dim else 1 for axis in range(len(extent))])
    return level


def profile(amount, total, most, lean):
    loads = [(1 << 20) // math.isqrt(standing ** lean) + 1 for standing in range(2, amount + 1)]
    rest, given = total - most - (amount - 1), [1] * (amount - 1)
    while rest > 0:
        free = [i for i in range(amount - 1) if given[i] < most]
        mass, left = sum([loads[i] for i in free]), rest
        for i in free:
            addition = min(most - given[i], max(1, left * loads[i] // mass), rest)
            given[i] = given[i] + addition
            rest = rest - addition
    return np.array([most] + given)


def ragged_sizes(key, count, total, bound, slope):
    if count == 2:
        one = jax.random.randint(key, (), max(1, total - bound), min(bound, total - 1) + 1)
        return jnp.stack([one, total - one])
    sizes = jnp.asarray(profile(count, total, bound, slope), jnp.int32)
    pairs = (count - 1) // 2
    source_of, receiver = sizes[1:1 + 2 * pairs:2], sizes[2:2 + 2 * pairs:2]
    room = jnp.minimum(source_of - 1, bound - receiver)
    shifted = jax.random.randint(jax.random.fold_in(key, 1), (pairs,), 0, 1 << 20) % (room + 1)
    sizes = sizes.at[1:1 + 2 * pairs:2].set(source_of - shifted).at[2:2 + 2 * pairs:2].set(receiver + shifted)
    return sizes[jax.random.permutation(jax.random.fold_in(key, 2), count)]


def shared_out(stream_key, own, number, rows, count, top, bound, slope):
    sequence = jax.random.permutation(stream_key, count)
    crowded, common = shares(count, rows * top, bound, slope, True), shares(count, rows * top, bound, slope, False)
    places = jnp.arange(count)

    def named(sizes, rotation):
        used = int((sizes > 0).sum())
        fixed = max(1, used // 4)
        shifted = fixed + (places - fixed + rotation * (used - fixed)) % max(1, count - fixed)
        return jnp.zeros((count,), jnp.int32).at[sequence[jnp.where(places < fixed, places, shifted)]].set(jnp.asarray(sizes, jnp.int32))

    sizes = jnp.where(number % 4 == 0, named(crowded, number // 4), named(common, number - number // 4 - 1))
    mixed = jax.random.permutation(jax.random.fold_in(own, 3), count)
    giver, taker = mixed[0:count // 2 * 2:2], mixed[1:count // 2 * 2:2]
    room = jnp.minimum(sizes[giver] - 1, bound - sizes[taker]) // 2
    room = jnp.where((giver == sequence[0]) | (taker == sequence[0]) | (sizes[taker] == 0), 0, jnp.maximum(room, 0))
    shifted = jax.random.randint(jax.random.fold_in(own, 4), (count // 2,), 0, 1 << 20) % (room + 1)
    sizes = sizes.at[giver].add(-shifted).at[taker].add(shifted)
    members = jnp.searchsorted(jnp.cumsum(sizes), jnp.arange(rows * top), side="right").astype(jnp.int32)
    listing = members.reshape(top, rows).T
    listing = listing[jax.random.permutation(jax.random.fold_in(own, 1), rows)]
    rotation = jax.random.randint(jax.random.fold_in(own, 2), (rows, 1), 0, top)
    return jnp.take_along_axis(listing, (jnp.arange(top)[None, :] + rotation) % top, axis=1)


def shares(number_of, total, most, slope, full):
    portions = [(1 << 20) // math.isqrt(grade ** slope) + 1 for grade in range(1, number_of + 1)]
    largest = most if full else min(most, max(-(-total // number_of), total * portions[0] // sum(portions)))
    least = 1 if total - largest >= number_of - 1 else 0
    holding, surplus = [largest] + [least] * (number_of - 1), total - largest - least * (number_of - 1)
    while surplus > 0:
        free = [i for i in range(1, number_of) if holding[i] < largest] or [i for i in range(1, number_of) if holding[i] < most]
        pool, remaining = sum([portions[i] for i in free]), surplus
        for i in free:
            more = min(most - holding[i], max(1, remaining * portions[i] // pool), surplus)
            holding[i] = holding[i] + more
            surplus = surplus - more
    return np.array(holding)


def centred(rng, dims, scale, reach, pieces=(), kind=jnp.bfloat16):
    drawn = scale * jax.random.normal(rng, dims, jnp.float32)
    if pieces:
        drawn = drawn * steps_of(rng, dims, pieces, -0.22, 0.18)
    return jnp.clip(drawn, -reach, reach).astype(kind)


def setup_inputs(seed: int = 0) -> dict:
    seeds = jax.random.split(jax.random.key(seed), 11)
    tokens = centred(seeds[0], (PACKS, PACK_LEN, D), 1.0, 6.0, ((0, 32), (1, 4)))
    segment_ids = jax.vmap(lambda own: jnp.searchsorted(jnp.cumsum(ragged_sizes(own, SEGS, PACK_LEN, SEG_MOST, 2)), jnp.arange(PACK_LEN), side="right"))(jax.random.split(seeds[1], PACKS)).reshape((PACKS, PACK_LEN)).astype(jnp.int32)
    expert_ids_keys = jax.random.split(jax.random.fold_in(seeds[2], 1), PACKS * PACK_LEN // TOK_DEV)
    expert_ids_turns = jax.random.permutation(jax.random.fold_in(seeds[2], 3), PACKS * PACK_LEN // TOK_DEV)
    expert_ids = jax.vmap(lambda own, number: shared_out(jax.random.fold_in(seeds[2], 2), own, number, TOK_DEV, EXPERTS, TOP, CAP, 2))(expert_ids_keys, expert_ids_turns).reshape((PACKS, PACK_LEN, TOP))
    gate_values = jnp.clip(0.2 + 0.8 * jax.random.uniform(seeds[3], (PACKS, PACK_LEN, TOP), jnp.float32) ** steps_of(seeds[3], (PACKS, PACK_LEN, TOP), ((0, 32), (1, 4)), -0.2, 0.2), 0.2, 1.0)
    ln_attn = jnp.clip(1.0 + 0.12 * jax.random.normal(seeds[4], (D,), jnp.float32), 0.4, 1.6)
    w_qkv = draw_w_qkv(jax.random.fold_in(seeds[10], 71), 0)
    w_attn_out = centred(seeds[6], (D, D), D ** -0.5, 0.15625)
    ln_expert = jnp.clip(1.0 + 0.12 * jax.random.normal(seeds[7], (D,), jnp.float32), 0.4, 1.6)
    w_in = centred(seeds[8], (EXPERTS, D, FF), D ** -0.5, 0.15625, ((0, 32), (2, 4)))
    w_out = centred(seeds[9], (EXPERTS, FF, D), FF ** -0.5, 0.078125, ((0, 32), (1, 4)))
    return dict(tokens=tokens, segment_ids=segment_ids, expert_ids=expert_ids, gate_values=gate_values, ln_attn=ln_attn, w_qkv=w_qkv, w_attn_out=w_attn_out, ln_expert=ln_expert, w_in=w_in, w_out=w_out)


epsilon = 1e-06

def normalize(rows, gain):
    mean = lax.optimization_barrier(jnp.mean(rows, axis=-1, keepdims=True))
    centered = rows - mean
    spread = lax.optimization_barrier(jnp.mean(centered * centered, axis=-1, keepdims=True))
    return centered * lax.rsqrt(spread + epsilon) * gain

def reference(tokens, segment_ids, expert_ids, gate_values, ln_attn, w_qkv, w_attn_out, ln_expert, w_in, w_out):
    scale = HEAD_DIM ** (-0.5)

    def pack_attention(operands):
        patches, segments = operands
        length = patches.shape[0]
        attn_in = normalize(patches.astype(jnp.float32), ln_attn).astype(jnp.bfloat16)
        qkv = jnp.dot(attn_in, w_qkv, preferred_element_type=jnp.float32).astype(jnp.bfloat16)
        queries = qkv[:, :D].reshape(length, HEADS, HEAD_DIM).astype(jnp.float32)
        keys = qkv[:, D:2 * D].reshape(length, HEADS, HEAD_DIM).astype(jnp.float32)
        values = qkv[:, 2 * D:].reshape(length, HEADS, HEAD_DIM).astype(jnp.float32)
        scores = jnp.einsum('qhd,khd->hqk', queries, keys) * scale
        allowed = (segments[:, None] == segments[None, :])[None]
        scores = jnp.where(allowed, scores, -1e+30)
        largest = lax.optimization_barrier(jnp.max(scores, axis=-1, keepdims=True))
        weights = jnp.where(allowed, jnp.exp(scores - largest), 0.0)
        totals = lax.optimization_barrier(jnp.sum(weights, axis=-1))
        rounded = lax.optimization_barrier(weights.astype(jnp.bfloat16)).astype(jnp.float32)
        context = jnp.einsum('hqk,khd->hqd', rounded, values) / totals[..., None]
        context = context.transpose(1, 0, 2).reshape(length, D).astype(jnp.bfloat16)
        return patches.astype(jnp.float32) + jnp.dot(context, w_attn_out, preferred_element_type=jnp.float32)
    middle = lax.map(pack_attention, (tokens, segment_ids))
    rows = middle.reshape(BLOCKS, TOK_DEV, D)
    expert_in = normalize(rows, ln_expert).astype(jnp.bfloat16)
    chosen = expert_ids.reshape(BLOCKS, TOK_DEV * TOP).astype(jnp.int32)

    def place(operands):
        block_rows, block_ids = operands
        onehot = (block_ids[:, None] == jnp.arange(EXPERTS, dtype=jnp.int32)[None, :]).astype(jnp.int32)
        slots = lax.optimization_barrier(jnp.sum((jnp.cumsum(onehot, axis=0) - onehot) * onehot, axis=1)).astype(jnp.int32)
        targets = (block_ids * CAP + slots).astype(jnp.int32)
        buffer = jnp.zeros((EXPERTS * CAP, D), jnp.bfloat16).at[targets].set(jnp.repeat(block_rows, TOP, axis=0))
        return (buffer, targets)
    buffers, targets = lax.map(place, (expert_in, chosen))
    per_expert = buffers.reshape(BLOCKS, EXPERTS, CAP, D).transpose(1, 0, 2, 3).reshape(EXPERTS, BLOCKS * CAP, D)

    def run_expert(operands):
        slot_rows, first, second = operands
        hidden = jax.nn.gelu(jnp.dot(slot_rows, first, preferred_element_type=jnp.float32)).astype(jnp.bfloat16)
        return jnp.dot(hidden, second, preferred_element_type=jnp.float32).astype(jnp.bfloat16)
    outputs = lax.map(run_expert, (per_expert, w_in, w_out))
    returned = outputs.reshape(EXPERTS, BLOCKS, CAP, D).transpose(1, 0, 2, 3).reshape(BLOCKS, EXPERTS * CAP, D)
    picked = jnp.take_along_axis(returned, targets[:, :, None], axis=1).astype(jnp.float32)
    picked = picked.reshape(BLOCKS, TOK_DEV, TOP, D)
    mixed = lax.optimization_barrier(jnp.sum(picked * gate_values.reshape(BLOCKS, TOK_DEV, TOP)[..., None], axis=2))
    return (rows + mixed).astype(jnp.bfloat16).reshape(PACKS, PACK_LEN, D)
```

```python
import functools

import jax
import jax.numpy as jnp
from jax import lax
from jax.experimental import pallas as pl
from jax.experimental.pallas import tpu as pltpu
from jax.sharding import PartitionSpec as P

F32 = jnp.float32
BF16 = jnp.bfloat16
I32 = jnp.int32
MESH = pl.DeviceIdType.MESH

D = 1280
HEADS = 16
HEAD = 80
TOK = 128
CAP = 9
NE = 32
COL = 256
NC = D // COL
MSG = 48
HALF = 16
CR = HALF * CAP
ALL = NE * MSG
EPS = 1e-06
NEG = -1e30

GROUPS = (((0, 1, 2), 0), ((3,), 128), ((4, 5), 256), ((6, 7), 384))


def normalize(rows, gain):
    mean = jnp.mean(rows, axis=-1, keepdims=True)
    centered = rows - mean
    spread = jnp.mean(centered * centered, axis=-1, keepdims=True)
    return centered * lax.rsqrt(spread + EPS) * gain


def gelu(x):
    return 0.5 * x * (1.0 + jnp.tanh(0.7978845608028654 * (x + 0.044715 * (x * x * x))))


def iota(shape, dim):
    return lax.broadcasted_iota(I32, shape, dim)


def dot(a, b):
    return jnp.dot(a, b, preferred_element_type=F32)


def cols(j):
    return pl.ds(pl.multiple_of(j * COL, COL), COL)


def kernel(
    tok, seg, eid, gate, lna, lne, wqkv_h, wao_h, win_h, wout_h, out,
    wqkv, wao, win, wout, xn, segs, q, k, v, ctx, ctxb, mid, xp, g, send, rcv, a, hid,
    part, keep, own, stage, back, rst, pack, ret, pick, unp, pkm, gcol,
    w_sem, as_sem, ar_sem, ss_sem, sr_sem, ds_sem, dr_sem, zs_sem, zr_sem, bs_sem, br_sem,
    es_sem, er_sem,
):
    d = lax.axis_index("dp")
    z = lax.axis_index("seq")
    zl = lax.rem(z + 3, 4)
    zr = lax.rem(z + 1, 4)
    zo = lax.rem(z + 2, 4)
    x, y, c = d // 8, lax.rem(d // 2, 4), lax.rem(d, 2)

    def shifted(j, sign):
        dx, dy, dc = j // 8, lax.rem(j // 2, 4), lax.rem(j, 2)
        if sign < 0:
            dx, dy = 4 - dx, 4 - dy
        return lax.rem(x + dx, 4) * 8 + lax.rem(y + dy, 4) * 2 + lax.rem(c + dc, 2)

    def rows48(j):
        return pl.ds(pl.multiple_of(j * MSG, MSG), MSG)

    loads = []
    for i in range(3):
        part_of = pl.ds(i * D, D)
        loads.append(pltpu.make_async_copy(wqkv_h.at[:, part_of], wqkv.at[:, part_of], w_sem.at[i]))
    loads.append(pltpu.make_async_copy(wao_h, wao, w_sem.at[3]))
    loads.append(pltpu.make_async_copy(win_h, win, w_sem.at[4]))
    loads.append(pltpu.make_async_copy(wout_h, wout, w_sem.at[5]))
    for load in loads:
        load.start()

    barrier = pltpu.get_barrier_semaphore()
    for other in (zl, zr, zo):
        pl.semaphore_signal(barrier, inc=1, device_id=(d, other), device_id_type=MESH)

    def greet(j, _):
        pl.semaphore_signal(barrier, inc=1, device_id=(shifted(j, 1), z), device_id_type=MESH)
        return 0

    lax.fori_loop(1, NE, greet, 0)
    xn[pl.ds(0, TOK), :] = normalize(tok[...].astype(F32), lna[...]).astype(BF16)
    segs[0] = jnp.broadcast_to(seg[...], (8, TOK))
    pl.semaphore_wait(barrier, NE - 1 + 3)

    def remote(src, dst, s_sem, r_sem, dev):
        return pltpu.make_async_remote_copy(
            src_ref=src, dst_ref=dst, send_sem=s_sem, recv_sem=r_sem,
            device_id=dev, device_id_type=MESH,
        )

    right, left, across = (d, zr), (d, zl), (d, zo)

    def xrows(slot, half):
        return xn.at[pl.ds(slot * TOK + half * 64, 64), :]

    seg_copies = [
        remote(segs.at[0], segs.at[1], ss_sem.at[0], sr_sem.at[0], right),
        remote(segs.at[0], segs.at[2], ss_sem.at[1], sr_sem.at[1], left),
        remote(segs.at[0], segs.at[3], ss_sem.at[2], sr_sem.at[2], across),
    ]
    r0 = remote(xrows(0, 0), xrows(1, 0), as_sem.at[0], ar_sem.at[0], right)
    r1 = remote(xrows(0, 1), xrows(1, 1), as_sem.at[1], ar_sem.at[1], right)
    l1 = remote(xrows(0, 1), xrows(2, 1), as_sem.at[2], ar_sem.at[2], left)
    l0 = remote(xrows(0, 0), xrows(2, 0), as_sem.at[3], ar_sem.at[3], left)
    ro = remote(xrows(1, 0), xrows(3, 0), as_sem.at[4], ar_sem.at[4], right)
    lo = remote(xrows(2, 1), xrows(3, 1), as_sem.at[5], ar_sem.at[5], left)
    r0.start()
    l1.start()
    r1.start()
    l0.start()
    for copy in seg_copies:
        copy.start()

    e0, e1 = eid[0:1, :], eid[1:2, :]
    ei = iota((NE, TOK), 0)
    named = jnp.where((ei == e0) | (ei == e1), 1.0, 0.0).astype(BF16)
    before = jnp.where(iota((TOK, TOK), 0) < iota((TOK, TOK), 1), 1.0, 0.0).astype(BF16)
    count = dot(named, before)
    s0 = jnp.sum(jnp.where(ei == e0, count, 0.0), axis=0, keepdims=True)
    s1 = jnp.sum(jnp.where(ei == e1, count, 0.0), axis=0, keepdims=True)
    t0 = e0.astype(F32) * MSG + s0
    t1 = e1.astype(F32) * MSG + s1
    ri = iota((TOK, TOK), 0)
    square = jnp.where(
        ri == 0, t0, jnp.where(ri == 1, t1, jnp.where(ri == 2, gate[0:1, :], gate[1:2, :]))
    )
    gcol[...] = jnp.transpose(square)
    t0, t1 = t0.astype(I32), t1.astype(I32)

    def make_g(i, _):
        rows = pl.ds(pl.multiple_of(i * 256, 256), 256)
        r = iota((256, TOK), 0) + i * 256
        for cc in range(NC):
            hit = (r == t0 + CAP * cc) | (r == t1 + CAP * cc)
            g[rows, cc * TOK : (cc + 1) * TOK] = jnp.where(hit, 1.0, 0.0).astype(BF16)
        return 0

    lax.fori_loop(0, ALL // 256, make_g, 0)

    for load in loads[:3]:
        load.wait()

    def own_q(j, _):
        q[:, cols(j)] = dot(xn[pl.ds(0, TOK), :], wqkv[:, cols(j)]).astype(BF16)
        return 0

    lax.fori_loop(0, NC, own_q, 0)

    def keys_values(first, number):
        rows = pl.ds(first, number)

        def step(j, _):
            k[rows, cols(j)] = dot(xn[rows, :], wqkv[:, cols(j + NC)]).astype(BF16)
            v[rows, cols(j)] = dot(xn[rows, :], wqkv[:, cols(j + 2 * NC)]).astype(BF16)
            return 0

        lax.fori_loop(0, NC, step, 0)

    keys_values(0, TOK)
    r0.wait_recv()
    ro.start()
    l1.wait_recv()
    lo.start()

    i = iota((CR, HALF * MSG), 0)
    r = iota((CR, HALF * MSG), 1)
    at = i + (MSG - CAP) * lax.shift_right_logical(i * 57, 9)
    for cc in range(NC):
        unp[pl.ds(cc * CR, CR), :] = jnp.where(r == at + CAP * cc, 1.0, 0.0).astype(BF16)
    i = iota((HALF * MSG, CR), 1)
    r = iota((HALF * MSG, CR), 0)
    at = i + (MSG - CAP) * lax.shift_right_logical(i * 57, 9)
    for cc in range(NC):
        pkm[cc] = jnp.where(r == at + CAP * cc, 1.0, 0.0).astype(BF16)

    r1.wait_recv()
    l0.wait_recv()
    keys_values(TOK, 2 * TOK)

    ri = iota((TOK, ALL), 1)
    c0, c1 = gcol[:, 0:1].astype(I32), gcol[:, 1:2].astype(I32)

    def make_pick(cc, _):
        base = pl.multiple_of(cc * 256, 256)
        pick[pl.ds(base, TOK), :] = jnp.where(ri == c0 + CAP * cc, 1.0, 0.0).astype(BF16)
        pick[pl.ds(base + TOK, TOK), :] = jnp.where(ri == c1 + CAP * cc, 1.0, 0.0).astype(BF16)
        return 0

    lax.fori_loop(0, NC, make_pick, 0)

    for copy in seg_copies:
        copy.wait_recv()
    eight = iota((8, TOK), 0)
    kinds = [jnp.where(eight == segs[s], 1.0, 0.0).astype(BF16) for s in range(4)]
    key_kind = jnp.concatenate(kinds, axis=1)
    same = lax.dot_general(kinds[0], key_kind, (((0,), (0,)), ((), ())), preferred_element_type=F32)
    bias = jnp.where(same > 0.5, 0.0, NEG)

    ro.wait_recv()
    lo.wait_recv()
    keys_values(3 * TOK, TOK)

    scale = HEAD ** (-0.5)
    ctx[...] = jnp.zeros((TOK, D), F32)
    for half in range(2):
        for heads, at in GROUPS:
            window = pl.ds(half * 640 + at, COL)
            lane = iota((TOK, COL), 1) + at
            masks = [(lane >= h * HEAD) & (lane < (h + 1) * HEAD) for h in heads]
            qw = q[:, window]
            zero = jnp.zeros_like(qw)
            stacked = jnp.concatenate([jnp.where(m, qw, zero) for m in masks], axis=0)
            scores = lax.dot_general(
                stacked, k[:, window], (((1,), (1,)), ((), ())), preferred_element_type=F32
            )
            probs, sums = [], []
            for n in range(len(heads)):
                s = scores[n * TOK : (n + 1) * TOK, :] * scale + bias
                w = jnp.exp(s - jnp.max(s, axis=-1, keepdims=True))
                sums.append(jnp.sum(w, axis=-1, keepdims=True))
                probs.append(w.astype(BF16))
            mixed = dot(jnp.concatenate(probs, axis=0), v[:, window])
            total = ctx[:, window]
            for n, m in enumerate(masks):
                total = jnp.where(m, mixed[n * TOK : (n + 1) * TOK, :] / sums[n], total)
            ctx[:, window] = total
    ctxb[...] = ctx[...].astype(BF16)

    loads[3].wait()

    def project(j, _):
        mid[:, cols(j)] = tok[:, cols(j)].astype(F32) + dot(ctxb[...], wao[:, cols(j)])
        return 0

    lax.fori_loop(0, NC, project, 0)
    expert_in = normalize(mid[...], lne[...]).astype(BF16)
    for cc in range(NC):
        xp[pl.ds(cc * TOK, TOK), :] = expert_in[:, cc * COL : (cc + 1) * COL]

    def fill(i, _):
        rows = pl.ds(pl.multiple_of(i * 256, 256), 256)
        send[rows, :] = dot(g[rows, :], xp[...]).astype(BF16)
        return 0

    lax.fori_loop(0, ALL // 256, fill, 0)

    def to_expert(j, _):
        dest = shifted(j, 1)
        remote(
            send.at[rows48(dest), :], rcv.at[rows48(j), :], ds_sem, dr_sem.at[j // HALF], (dest, z)
        ).start()
        return 0

    lax.fori_loop(1, NE, to_expert, 0)
    rcv[pl.ds(0, MSG), :] = send[rows48(d), :]

    loads[4].wait()
    loads[5].wait()

    def chunk(slot, half):
        return a.at[slot, half]

    def unpack(half):
        first, number = (MSG, (HALF - 1) * MSG) if half == 0 else (HALF * MSG, HALF * MSG)
        got = rcv.at[pl.ds(first, number), :]
        remote(got, got, ds_sem, dr_sem.at[half], right).wait_recv()
        for cc in range(NC):
            piece = dot(unp[pl.ds(cc * CR, CR), :], rcv[pl.ds(half * HALF * MSG, HALF * MSG), :])
            a[0, half, :, cc * COL : (cc + 1) * COL] = piece.astype(BF16)

    zc = {}
    for half in range(2):
        zc["r", half] = remote(chunk(0, half), chunk(1, half), zs_sem.at[half], zr_sem.at[half], right)
        zc["l", half] = remote(
            chunk(0, half), chunk(2, half), zs_sem.at[2 + half], zr_sem.at[2 + half], left
        )
    zc["ro"] = remote(chunk(1, 0), chunk(3, 0), zs_sem.at[4], zr_sem.at[4], right)
    zc["lo"] = remote(chunk(2, 1), chunk(3, 1), zs_sem.at[5], zr_sem.at[5], left)

    def expert(slot, half, store):
        def first(j, _):
            hid[:, cols(j)] = gelu(dot(a[slot, half], win[:, cols(j)])).astype(BF16)
            return 0

        lax.fori_loop(0, NC, first, 0)

        def second(j, _):
            store(cols(j), dot(hid[...], wout[:, cols(j)]))
            return 0

        lax.fori_loop(0, NC, second, 0)

    def into_own(half):
        def store(at, value):
            own[half, :, at] = value

        return store

    def into_part(n):
        def store(at, value):
            part[n, :, at] = value.astype(BF16)

        return store

    def into_keep(n):
        def store(at, value):
            keep[n, :, at] = value

        return store

    b_left0 = remote(part.at[0], back.at[2], bs_sem.at[0], br_sem.at[0], left)
    b_right1 = remote(part.at[1], back.at[1], bs_sem.at[1], br_sem.at[1], right)
    b_across0 = remote(part.at[2], stage.at[0], bs_sem.at[2], br_sem.at[2], right)
    b_across1 = remote(part.at[3], stage.at[1], bs_sem.at[3], br_sem.at[3], left)
    b_right0 = remote(part.at[4], back.at[0], bs_sem.at[4], br_sem.at[4], right)
    b_left1 = remote(part.at[5], back.at[3], bs_sem.at[5], br_sem.at[5], left)

    unpack(0)
    zc["r", 0].start()
    zc["l", 0].start()
    unpack(1)
    zc["l", 1].start()
    zc["r", 1].start()
    expert(0, 0, into_own(0))
    zc["r", 0].wait_recv()
    zc["ro"].start()
    expert(0, 1, into_own(1))
    zc["l", 1].wait_recv()
    zc["lo"].start()
    expert(1, 0, into_part(0))
    b_left0.start()
    zc["r", 1].wait_recv()
    expert(1, 1, into_keep(1))
    expert(2, 1, into_part(1))
    b_right1.start()
    zc["l", 0].wait_recv()
    expert(2, 0, into_keep(0))
    zc["ro"].wait_recv()
    expert(3, 0, into_part(2))
    b_across0.start()
    zc["lo"].wait_recv()
    expert(3, 1, into_part(3))
    b_across1.start()
    b_across0.wait_recv()
    part[4] = (keep[0] + stage[0].astype(F32)).astype(BF16)
    b_right0.start()
    b_across1.wait_recv()
    part[5] = (keep[1] + stage[1].astype(F32)).astype(BF16)
    b_left1.start()

    b_left0.wait_recv()
    b_right1.wait_recv()
    for half in range(2):
        if half == 0:
            b_right0.wait_recv()
        else:
            b_left1.wait_recv()
        for cc in range(NC):
            at = slice(cc * COL, (cc + 1) * COL)
            full = own[half, :, at] + back[half, :, at].astype(F32) + back[2 + half, :, at].astype(F32)
            rst[pl.ds(cc * CR, CR), :] = full.astype(BF16)
        packed = dot(pkm[0], rst[pl.ds(0, CR), :])
        for cc in range(1, NC):
            packed += dot(pkm[cc], rst[pl.ds(cc * CR, CR), :])
        pack[pl.ds(half * HALF * MSG, HALF * MSG), :] = packed.astype(BF16)

        def to_patch(j, _):
            dest = shifted(j, -1)
            remote(pack.at[rows48(j), :], ret.at[rows48(d), :], es_sem, er_sem, (dest, z)).start()
            return 0

        lax.fori_loop(max(1, half * HALF), (half + 1) * HALF, to_patch, 0)
    ret[rows48(d), :] = pack[pl.ds(0, MSG), :]

    others = ret.at[pl.ds(0, (NE - 1) * MSG), :]
    remote(others, others, es_sem, er_sem, right).wait_recv()
    g0, g1 = gcol[:, 2:3], gcol[:, 3:4]

    def final(cc, _):
        both = dot(pick[pl.ds(pl.multiple_of(cc * 256, 256), 256), :], ret[...])
        out[:, cols(cc)] = (mid[:, cols(cc)] + g0 * both[:TOK] + g1 * both[TOK:]).astype(BF16)
        return 0

    lax.fori_loop(0, NC, final, 0)

    for copy in seg_copies + [r0, r1, l0, l1, ro, lo] + list(zc.values()):
        copy.wait_send()
    for copy in (b_left0, b_right1, b_across0, b_across1, b_right0, b_left1):
        copy.wait_send()
    gone = send.at[pl.ds(0, (NE - 1) * MSG), :]
    remote(gone, gone, ds_sem, dr_sem.at[0], right).wait_send()
    gone = pack.at[pl.ds(0, (NE - 1) * MSG), :]
    remote(gone, gone, es_sem, er_sem, right).wait_send()


def layer(tok, seg, eid, gate, lna, lne, wqkv, wao, win, wout):
    vm = pl.BlockSpec(memory_space=pltpu.VMEM)
    hbm = pl.BlockSpec(memory_space=pl.ANY)
    V = pltpu.VMEM
    dma = pltpu.SemaphoreType.DMA
    return pl.pallas_call(
        kernel,
        out_shape=jax.ShapeDtypeStruct((TOK, D), BF16),
        in_specs=[vm] * 6 + [hbm] * 4,
        out_specs=vm,
        scratch_shapes=[
            V((D, 3 * D), BF16),
            V((D, D), BF16),
            V((D, D), BF16),
            V((D, D), BF16),
            V((4 * TOK, D), BF16),
            V((4, 8, TOK), I32),
            V((TOK, D), BF16),
            V((4 * TOK, D), BF16),
            V((4 * TOK, D), BF16),
            V((TOK, D), F32),
            V((TOK, D), BF16),
            V((TOK, D), F32),
            V((NC * TOK, COL), BF16),
            V((ALL, NC * TOK), BF16),
            V((ALL, COL), BF16),
            V((ALL, COL), BF16),
            V((4, 2, CR, D), BF16),
            V((CR, D), BF16),
            V((6, CR, D), BF16),
            V((2, CR, D), F32),
            V((2, CR, D), F32),
            V((2, CR, D), BF16),
            V((4, CR, D), BF16),
            V((NC * CR, COL), BF16),
            V((ALL, COL), BF16),
            V((ALL, COL), BF16),
            V((2 * NC * TOK, ALL), BF16),
            V((NC * CR, HALF * MSG), BF16),
            V((NC, HALF * MSG, CR), BF16),
            V((TOK, TOK), F32),
            dma((6,)),
            dma((6,)),
            dma((6,)),
            dma((3,)),
            dma((3,)),
            dma,
            dma((2,)),
            dma((6,)),
            dma((6,)),
            dma((6,)),
            dma((6,)),
            dma,
            dma,
        ],
        compiler_params=pltpu.CompilerParams(
            collective_id=0, has_side_effects=True, vmem_limit_bytes=60 * 1024 * 1024
        ),
        cost_estimate=pl.CostEstimate(
            flops=14_000_000_000, bytes_accessed=24_000_000, transcendentals=3_000_000
        ),
    )(tok, seg, eid, gate, lna, lne, wqkv, wao, win, wout)


def body(
    tokens, segment_ids, expert_ids, gate_values, ln_attn, w_qkv, w_attn_out, ln_expert, w_in, w_out
):
    out = layer(
        tokens[0],
        segment_ids,
        expert_ids[0].T,
        gate_values[0].T,
        ln_attn[None],
        ln_expert[None],
        w_qkv,
        w_attn_out,
        w_in[0],
        w_out[0],
    )
    return out[None]


def solution(mesh):
    placed = (
        P("dp", "seq", None),
        P("dp", "seq"),
        P("dp", "seq", None),
        P("dp", "seq", None),
        P(),
        P(),
        P(),
        P(),
        P("dp", None, "seq"),
        P("dp", "seq", None),
    )
    return jax.shard_map(
        body, mesh=mesh, in_specs=placed, out_specs=P("dp", "seq", None), check_vma=False
    )
```

```python
import functools

import jax
import jax.numpy as jnp
from jax import lax
from jax.experimental import pallas as pl
from jax.experimental.pallas import tpu as pltpu
from jax.sharding import PartitionSpec as P

F32 = jnp.float32
BF16 = jnp.bfloat16
I32 = jnp.int32
MESH = pl.DeviceIdType.MESH

D = 1280
HEADS = 16
HEAD = 80
TOK = 128
CAP = 9
NE = 32
COL = 256
NC = D // COL
MSG = 48
HALF = 16
CR = HALF * CAP
GS = 8
GM = GS * MSG
ALL = NE * MSG
EPS = 1e-06
NEG = -1e30

GROUPS = (((0, 1, 2), 0), ((3,), 128), ((4, 5), 256), ((6, 7), 384))


OFFSETS = sorted(
    [(dx, dy, dc) for dx in range(4) for dy in range(4) for dc in range(2)],
    key=lambda o: -(min(o[0], 4 - o[0]) + min(o[1], 4 - o[1]) + 0.5 * o[2]),
)

OUT = ((0, 64), (64, 80))
BACK = ((0, 80), (80, 64))


def normalize(rows, gain):
    mean = jnp.mean(rows, axis=-1, keepdims=True)
    centered = rows - mean
    spread = jnp.mean(centered * centered, axis=-1, keepdims=True)
    return centered * lax.rsqrt(spread + EPS) * gain


def gelu(x):
    return 0.5 * x * (1.0 + jnp.tanh(0.7978845608028654 * (x + 0.044715 * (x * x * x))))


def iota(shape, dim):
    return lax.broadcasted_iota(I32, shape, dim)


def dot(a, b):
    return jnp.dot(a, b, preferred_element_type=F32)


def cols(j):
    return pl.ds(pl.multiple_of(j * COL, COL), COL)


def kernel(
    tok, seg, eid, gate, lna, lne, wqkv_h, wao_h, win_h, wout_h, out,
    wqkv, wao, win, wout, xn, segs, q, k, v, ctx, ctxb, mid, xp, g, send, rcv, a, hid,
    part, keep, own, stage, back, rst, pack, ret, pick, unp0, unp1, pkm0, pkm1, gcol,
    w_sem, as_sem, ar_sem, ss_sem, sr_sem, ds_sem, dr_sem, zs_sem, zr_sem, bs_sem, br_sem,
    es_sem, er_sem,
):
    d = lax.axis_index("dp")
    z = lax.axis_index("seq")
    zl = lax.rem(z + 3, 4)
    zr = lax.rem(z + 1, 4)
    zo = lax.rem(z + 2, 4)
    x, y, c = d // 8, lax.rem(d // 2, 4), lax.rem(d, 2)

    xs = [lax.rem(x + i, 4) * 8 for i in range(4)]
    ys = [lax.rem(y + i, 4) * 2 for i in range(4)]
    cs = [c, 1 - c]

    def shifted(n, sign):
        dx, dy, dc = OFFSETS[n]
        return xs[sign * dx % 4] + ys[sign * dy % 4] + cs[dc]

    def rows48(j):
        return pl.ds(pl.multiple_of(j * MSG, MSG), MSG)

    loads = []
    for i in range(3):
        part_of = pl.ds(i * D, D)
        loads.append(pltpu.make_async_copy(wqkv_h.at[:, part_of], wqkv.at[:, part_of], w_sem.at[i]))
    loads.append(pltpu.make_async_copy(wao_h, wao, w_sem.at[3]))
    loads.append(pltpu.make_async_copy(win_h, win, w_sem.at[4]))
    loads.append(pltpu.make_async_copy(wout_h, wout, w_sem.at[5]))
    for load in loads[:3]:
        load.start()

    barrier = pltpu.get_barrier_semaphore()
    for other in (zl, zr, zo):
        pl.semaphore_signal(barrier, inc=1, device_id=(d, other), device_id_type=MESH)

    for n in range(NE - 1):
        pl.semaphore_signal(barrier, inc=1, device_id=(shifted(n, 1), z), device_id_type=MESH)
    xn[pl.ds(0, TOK), :] = normalize(tok[...].astype(F32), lna[...].reshape(1, D)).astype(BF16)
    segs[0] = jnp.broadcast_to(seg[...], (8, TOK))
    pl.semaphore_wait(barrier, NE - 1 + 3)

    def remote(src, dst, s_sem, r_sem, dev):
        return pltpu.make_async_remote_copy(
            src_ref=src, dst_ref=dst, send_sem=s_sem, recv_sem=r_sem,
            device_id=dev, device_id_type=MESH,
        )

    right, left, across = (d, zr), (d, zl), (d, zo)

    def xrows(slot, half):
        return xn.at[pl.ds(slot * TOK + half * 64, 64), :]

    seg_copies = [
        remote(segs.at[0], segs.at[1], ss_sem.at[0], sr_sem.at[0], right),
        remote(segs.at[0], segs.at[2], ss_sem.at[1], sr_sem.at[1], left),
        remote(segs.at[0], segs.at[3], ss_sem.at[2], sr_sem.at[2], across),
    ]
    r0 = remote(xrows(0, 0), xrows(1, 0), as_sem.at[0], ar_sem.at[0], right)
    r1 = remote(xrows(0, 1), xrows(1, 1), as_sem.at[1], ar_sem.at[1], right)
    l1 = remote(xrows(0, 1), xrows(2, 1), as_sem.at[2], ar_sem.at[2], left)
    l0 = remote(xrows(0, 0), xrows(2, 0), as_sem.at[3], ar_sem.at[3], left)
    ro = remote(xrows(1, 0), xrows(3, 0), as_sem.at[4], ar_sem.at[4], right)
    lo = remote(xrows(2, 1), xrows(3, 1), as_sem.at[5], ar_sem.at[5], left)
    r0.start()
    l1.start()
    r1.start()
    l0.start()
    for copy in seg_copies:
        copy.start()
    for load in loads[3:]:
        load.start()

    e0, e1 = eid[0:1, :], eid[1:2, :]
    ei = iota((NE, TOK), 0)
    named = jnp.where((ei == e0) | (ei == e1), 1.0, 0.0).astype(BF16)
    before = jnp.where(iota((TOK, TOK), 0) < iota((TOK, TOK), 1), 1.0, 0.0).astype(BF16)
    count = dot(named, before)
    s0 = jnp.sum(jnp.where(ei == e0, count, 0.0), axis=0, keepdims=True)
    s1 = jnp.sum(jnp.where(ei == e1, count, 0.0), axis=0, keepdims=True)
    t0 = e0.astype(F32) * MSG + s0
    t1 = e1.astype(F32) * MSG + s1
    ri = iota((TOK, TOK), 0)
    square = jnp.where(
        ri == 0, t0, jnp.where(ri == 1, t1, jnp.where(ri == 2, gate[0:1, :], gate[1:2, :]))
    )
    gcol[...] = jnp.transpose(square)
    t0, t1 = t0.astype(I32), t1.astype(I32)

    def make_g(i, _):
        rows = pl.ds(pl.multiple_of(i * 256, 256), 256)
        r = iota((256, TOK), 0) + i * 256
        for cc in range(NC):
            hit = (r == t0 + CAP * cc) | (r == t1 + CAP * cc)
            g[rows, cc * TOK : (cc + 1) * TOK] = jnp.where(hit, 1.0, 0.0).astype(BF16)
        return 0

    lax.fori_loop(0, ALL // 256, make_g, 0)

    def fixed(ref, q_dim, rows, first, base):
        q = iota(ref.shape, q_dim)
        r = iota(ref.shape, 1 - q_dim) + base
        if rows == 64:
            cc = lax.shift_right_logical(q, 6)
        else:
            cc = lax.shift_right_logical(q * 205, 14)
        i = q - cc * rows + first
        at = i + (MSG - CAP) * lax.shift_right_logical(i * 57, 9) + CAP * cc
        ref[...] = jnp.where(r == at, 1.0, 0.0).astype(BF16)

    fixed(unp0, 0, 64, 0, 0)
    fixed(unp1, 0, 80, 64, 7 * MSG)

    r0.wait_recv()
    ro.start()
    l1.wait_recv()
    lo.start()

    for load in loads[:3]:
        load.wait()

    def own_q(j, _):
        q[:, cols(j)] = dot(xn[pl.ds(0, TOK), :], wqkv[:, cols(j)]).astype(BF16)
        return 0

    lax.fori_loop(0, NC, own_q, 0)

    def keys_values(first, number):
        rows = pl.ds(first, number)

        def step(j, _):
            k[rows, cols(j)] = dot(xn[rows, :], wqkv[:, cols(j + NC)]).astype(BF16)
            v[rows, cols(j)] = dot(xn[rows, :], wqkv[:, cols(j + 2 * NC)]).astype(BF16)
            return 0

        lax.fori_loop(0, NC, step, 0)

    keys_values(0, TOK)
    fixed(pkm0, 1, 80, 0, 0)
    fixed(pkm1, 1, 80, 64, GM)

    r1.wait_recv()
    l0.wait_recv()
    keys_values(TOK, 2 * TOK)

    ri = iota((TOK, ALL), 1)
    c0, c1 = gcol[:, 0:1].astype(I32), gcol[:, 1:2].astype(I32)

    def make_pick(cc, _):
        base = pl.multiple_of(cc * 256, 256)
        pick[pl.ds(base, TOK), :] = jnp.where(ri == c0 + CAP * cc, 1.0, 0.0).astype(BF16)
        pick[pl.ds(base + TOK, TOK), :] = jnp.where(ri == c1 + CAP * cc, 1.0, 0.0).astype(BF16)
        return 0

    lax.fori_loop(0, NC, make_pick, 0)

    for copy in seg_copies:
        copy.wait_recv()
    eight = iota((8, TOK), 0)
    kinds = [jnp.where(eight == segs[s], 1.0, 0.0).astype(BF16) for s in range(4)]
    key_kind = jnp.concatenate(kinds, axis=1)
    same = lax.dot_general(kinds[0], key_kind, (((0,), (0,)), ((), ())), preferred_element_type=F32)
    bias = jnp.where(same > 0.5, 0.0, NEG)

    ro.wait_recv()
    lo.wait_recv()
    keys_values(3 * TOK, TOK)

    scale = HEAD ** (-0.5)
    ctx[...] = jnp.zeros((TOK, D), F32)
    for half in range(2):
        for heads, at in GROUPS:
            window = pl.ds(half * 640 + at, COL)
            lane = iota((TOK, COL), 1) + at
            masks = [(lane >= h * HEAD) & (lane < (h + 1) * HEAD) for h in heads]
            qw = q[:, window]
            zero = jnp.zeros_like(qw)
            stacked = jnp.concatenate([jnp.where(m, qw, zero) for m in masks], axis=0)
            scores = lax.dot_general(
                stacked, k[:, window], (((1,), (1,)), ((), ())), preferred_element_type=F32
            )
            probs, sums = [], []
            for n in range(len(heads)):
                s = scores[n * TOK : (n + 1) * TOK, :] * scale + bias
                w = jnp.exp(s - jnp.max(s, axis=-1, keepdims=True))
                sums.append(jnp.sum(w, axis=-1, keepdims=True))
                probs.append(w.astype(BF16))
            mixed = dot(jnp.concatenate(probs, axis=0), v[:, window])
            total = ctx[:, window]
            for n, m in enumerate(masks):
                total = jnp.where(m, mixed[n * TOK : (n + 1) * TOK, :] / sums[n], total)
            ctx[:, window] = total
    ctxb[...] = ctx[...].astype(BF16)

    loads[3].wait()

    def project(j, _):
        mid[:, cols(j)] = tok[:, cols(j)].astype(F32) + dot(ctxb[...], wao[:, cols(j)])
        return 0

    lax.fori_loop(0, NC, project, 0)
    expert_in = normalize(mid[...], lne[...].reshape(1, D)).astype(BF16)
    for cc in range(NC):
        xp[pl.ds(cc * TOK, TOK), :] = expert_in[:, cc * COL : (cc + 1) * COL]

    def fill(i, _):
        rows = pl.ds(pl.multiple_of(i * 256, 256), 256)
        send[rows, :] = dot(g[rows, :], xp[...]).astype(BF16)
        return 0

    lax.fori_loop(0, ALL // 256, fill, 0)

    for n in range(NE - 1):
        dest = shifted(n, 1)
        remote(
            send.at[rows48(dest), :], rcv.at[rows48(n), :], ds_sem, dr_sem.at[n // GS], (dest, z)
        ).start()
    rcv[pl.ds((NE - 1) * MSG, MSG), :] = send[rows48(d), :]

    def piece_of(slot, half, n):
        first, number = OUT[n]
        return a.at[slot, half, pl.ds(first, number)]

    def arrived(group):
        number = GS if group < 3 else GS - 1
        got = rcv.at[pl.ds(group * GM, number * MSG), :]
        remote(got, got, ds_sem, dr_sem.at[group], right).wait_recv()

    def unpack(half, n):
        first, number = OUT[n]
        arrived(2 * half + n)
        base = half * 2 * GM
        if n == 0:
            got = dot(unp0[...], rcv[pl.ds(base, GM), :])
        else:
            got = dot(unp1[...], rcv[pl.ds(base + 7 * MSG, 9 * MSG), :])
        for cc in range(NC):
            a[0, half, first : first + number, cc * COL : (cc + 1) * COL] = got[
                cc * number : (cc + 1) * number
            ].astype(BF16)

    zc = {}
    for half in range(2):
        for n in range(2):
            m = 2 * half + n
            zc["r", half, n] = remote(
                piece_of(0, half, n), piece_of(1, half, n), zs_sem.at[m], zr_sem.at[m], right
            )
            zc["l", half, n] = remote(
                piece_of(0, half, n), piece_of(2, half, n), zs_sem.at[4 + m], zr_sem.at[4 + m], left
            )
    for n in range(2):
        zc["ro", n] = remote(
            piece_of(1, 0, n), piece_of(3, 0, n), zs_sem.at[8 + n], zr_sem.at[8 + n], right
        )
        zc["lo", n] = remote(
            piece_of(2, 1, n), piece_of(3, 1, n), zs_sem.at[10 + n], zr_sem.at[10 + n], left
        )

    def expert(slot, half, store):
        def first(j, _):
            hid[:, cols(j)] = gelu(dot(a[slot, half], win[:, cols(j)])).astype(BF16)
            return 0

        lax.fori_loop(0, NC, first, 0)

        def second(j, _):
            store(cols(j), dot(hid[...], wout[:, cols(j)]))
            return 0

        lax.fori_loop(0, NC, second, 0)

    def into_own(half):
        def store(at, value):
            own[half, :, at] = value

        return store

    def into_part(n):
        def store(at, value):
            part[n, :, at] = value.astype(BF16)

        return store

    def into_keep(n):
        def store(at, value):
            keep[n, :, at] = value

        return store

    def back_of(ref, slot, n):
        first, number = BACK[n]
        return ref.at[slot, pl.ds(first, number)]

    b_left0 = remote(part.at[0], back.at[2], bs_sem.at[0], br_sem.at[0], left)
    b_right1 = remote(part.at[1], back.at[1], bs_sem.at[1], br_sem.at[1], right)
    bc = {}
    for n in range(2):
        for m, (key, src, dst, at, dev) in enumerate(
            (
                ("across0", 2, stage, 0, right),
                ("across1", 3, stage, 1, left),
                ("right0", 4, back, 0, right),
                ("left1", 5, back, 3, left),
            )
        ):
            bc[key, n] = remote(
                back_of(part, src, n), back_of(dst, at, n),
                bs_sem.at[2 + 2 * m + n], br_sem.at[2 + 2 * m + n], dev,
            )

    loads[4].wait()
    loads[5].wait()

    for half in range(2):
        for n in range(2):
            unpack(half, n)
            zc["r", half, n].start()
            zc["l", half, n].start()
    for n in range(2):
        zc["r", 0, n].wait_recv()
        zc["ro", n].start()
    expert(0, 0, into_own(0))
    for n in range(2):
        zc["l", 1, n].wait_recv()
        zc["lo", n].start()
    expert(1, 0, into_part(0))
    b_left0.start()
    expert(2, 1, into_part(1))
    b_right1.start()
    for n in range(2):
        zc["r", 1, n].wait_recv()
        zc["l", 0, n].wait_recv()
    expert(2, 0, into_keep(0))
    expert(1, 1, into_keep(1))
    expert(0, 1, into_own(1))
    for n in range(2):
        zc["ro", n].wait_recv()
    expert(3, 0, into_part(2))
    bc["across0", 0].start()
    bc["across0", 1].start()
    for n in range(2):
        zc["lo", n].wait_recv()
    expert(3, 1, into_part(3))
    bc["across1", 0].start()
    bc["across1", 1].start()
    for n in range(2):
        first, number = BACK[n]
        rows = pl.ds(first, number)
        bc["across0", n].wait_recv()
        part[4, rows] = (keep[0, rows] + stage[0, rows].astype(F32)).astype(BF16)
        bc["right0", n].start()
        bc["across1", n].wait_recv()
        part[5, rows] = (keep[1, rows] + stage[1, rows].astype(F32)).astype(BF16)
        bc["left1", n].start()

    b_left0.wait_recv()
    b_right1.wait_recv()
    for n in range(2):
        first, number = BACK[n]
        rows = pl.ds(first, number)
        for half in range(2):
            bc["right0" if half == 0 else "left1", n].wait_recv()
            for cc in range(NC):
                at = slice(cc * COL, (cc + 1) * COL)
                full = (
                    own[half, rows, at]
                    + back[half, rows, at].astype(F32)
                    + back[2 + half, rows, at].astype(F32)
                ).astype(BF16)
                if n == 0:
                    rst[half, 0, pl.ds(cc * 80, 80), :] = full
                    rst[half, 1, pl.ds(cc * 80, 16), :] = full[64:]
                else:
                    rst[half, 1, pl.ds(cc * 80 + 16, 64), :] = full
            packed = dot((pkm0 if n == 0 else pkm1)[...], rst[half, n])
            group = 2 * half + n
            pack[pl.ds(group * GM, GM), :] = packed.astype(BF16)
            for m in range(group * GS, min((group + 1) * GS, NE - 1)):
                dest = shifted(m, -1)
                remote(
                    pack.at[rows48(m), :], ret.at[rows48(d), :], es_sem, er_sem, (dest, z)
                ).start()
    ret[rows48(d), :] = pack[pl.ds((NE - 1) * MSG, MSG), :]

    others = ret.at[pl.ds(0, (NE - 1) * MSG), :]
    remote(others, others, es_sem, er_sem, right).wait_recv()
    g0, g1 = gcol[:, 2:3], gcol[:, 3:4]

    def final(cc, _):
        both = dot(pick[pl.ds(pl.multiple_of(cc * 256, 256), 256), :], ret[...])
        out[:, cols(cc)] = (mid[:, cols(cc)] + g0 * both[:TOK] + g1 * both[TOK:]).astype(BF16)
        return 0

    lax.fori_loop(0, NC, final, 0)

    for copy in seg_copies + [r0, r1, l0, l1, ro, lo] + list(zc.values()):
        copy.wait_send()
    for copy in [b_left0, b_right1] + list(bc.values()):
        copy.wait_send()
    gone = send.at[pl.ds(0, (NE - 1) * MSG), :]
    remote(gone, gone, ds_sem, dr_sem.at[0], right).wait_send()
    gone = pack.at[pl.ds(0, (NE - 1) * MSG), :]
    remote(gone, gone, es_sem, er_sem, right).wait_send()


def layer(tok, seg, eid, gate, lna, lne, wqkv, wao, win, wout):
    vm = pl.BlockSpec(memory_space=pltpu.VMEM)
    hbm = pl.BlockSpec(memory_space=pl.ANY)
    V = pltpu.VMEM
    dma = pltpu.SemaphoreType.DMA
    return pl.pallas_call(
        kernel,
        out_shape=jax.ShapeDtypeStruct((TOK, D), BF16),
        in_specs=[vm] * 6 + [hbm] * 4,
        out_specs=vm,
        scratch_shapes=[
            V((D, 3 * D), BF16),
            V((D, D), BF16),
            V((D, D), BF16),
            V((D, D), BF16),
            V((4 * TOK, D), BF16),
            V((4, 8, TOK), I32),
            V((TOK, D), BF16),
            V((4 * TOK, D), BF16),
            V((4 * TOK, D), BF16),
            V((TOK, D), F32),
            V((TOK, D), BF16),
            V((TOK, D), F32),
            V((NC * TOK, COL), BF16),
            V((ALL, NC * TOK), BF16),
            V((ALL, COL), BF16),
            V((ALL, COL), BF16),
            V((4, 2, CR, D), BF16),
            V((CR, D), BF16),
            V((6, CR, D), BF16),
            V((2, CR, D), F32),
            V((2, CR, D), F32),
            V((2, CR, D), BF16),
            V((4, CR, D), BF16),
            V((2, 2, NC * 80, COL), BF16),
            V((ALL, COL), BF16),
            V((ALL, COL), BF16),
            V((2 * NC * TOK, ALL), BF16),
            V((NC * 64, GM), BF16),
            V((NC * 80, 9 * MSG), BF16),
            V((GM, NC * 80), BF16),
            V((GM, NC * 80), BF16),
            V((TOK, TOK), F32),
            dma((6,)),
            dma((6,)),
            dma((6,)),
            dma((3,)),
            dma((3,)),
            dma,
            dma((4,)),
            dma((12,)),
            dma((12,)),
            dma((10,)),
            dma((10,)),
            dma,
            dma,
        ],
        compiler_params=pltpu.CompilerParams(
            collective_id=0, has_side_effects=True, vmem_limit_bytes=60 * 1024 * 1024
        ),
        cost_estimate=pl.CostEstimate(
            flops=14_000_000_000, bytes_accessed=24_000_000, transcendentals=3_000_000
        ),
    )(tok, seg, eid, gate, lna, lne, wqkv, wao, win, wout)


def body(
    tokens, segment_ids, expert_ids, gate_values, ln_attn, w_qkv, w_attn_out, ln_expert, w_in, w_out
):
    out = layer(
        tokens[0],
        segment_ids,
        expert_ids[0].T,
        gate_values[0].T,
        ln_attn,
        ln_expert,
        w_qkv,
        w_attn_out,
        w_in[0],
        w_out[0],
    )
    return out[None]


def solution(mesh):
    placed = (
        P("dp", "seq", None),
        P("dp", "seq"),
        P("dp", "seq", None),
        P("dp", "seq", None),
        P(),
        P(),
        P(),
        P(),
        P("dp", None, "seq"),
        P("dp", "seq", None),
    )
    return jax.shard_map(
        body, mesh=mesh, in_specs=placed, out_specs=P("dp", "seq", None), check_vma=False
    )
```

```python
import functools

import jax
import jax.numpy as jnp
from jax import lax
from jax.experimental import pallas as pl
from jax.experimental.pallas import tpu as pltpu
from jax.sharding import PartitionSpec as P

F32 = jnp.float32
BF16 = jnp.bfloat16
I32 = jnp.int32
MESH = pl.DeviceIdType.MESH

D = 1280
HEADS = 16
HEAD = 80
TOK = 128
CAP = 9
NE = 32
COL = 256
NC = D // COL
MSG = 48
HALF = 16
CR = HALF * CAP
GS = 8
GM = GS * MSG
ALL = NE * MSG
EPS = 1e-06
NEG = -1e30

GROUPS = (((0, 1, 2), 0), ((3,), 128), ((4, 5), 256), ((6, 7), 384))


OFFSETS = sorted(
    [(dx, dy, dc) for dx in range(4) for dy in range(4) for dc in range(2)],
    key=lambda o: -(min(o[0], 4 - o[0]) + min(o[1], 4 - o[1]) + 0.5 * o[2]),
)

OUT = ((0, 64), (64, 80))
BACK = ((0, 80), (80, 64))


def normalize(rows, gain):
    mean = jnp.mean(rows, axis=-1, keepdims=True)
    centered = rows - mean
    spread = jnp.mean(centered * centered, axis=-1, keepdims=True)
    return centered * lax.rsqrt(spread + EPS) * gain


def gelu(x):
    return 0.5 * x * (1.0 + jnp.tanh(0.7978845608028654 * (x + 0.044715 * (x * x * x))))


def iota(shape, dim):
    return lax.broadcasted_iota(I32, shape, dim)


def dot(a, b):
    return jnp.dot(a, b, preferred_element_type=F32)


def cols(j):
    return pl.ds(j * COL, COL)


def each(number, step):
    for i in range(number):
        step(i)


def kernel(
    tok, seg, eid, gate, lna, lne, wqkv_h, wao_h, win_h, wout_h, out,
    wqkv, wao, win, wout, xn, segs, q, k, v, ctx, ctxb, mid, xp, g, send, rcv, a, hid,
    part, keep, own, stage, back, rst, pack, ret, pick, unp0, unp1, pkm0, pkm1, gcol,
    w_sem, as_sem, ar_sem, ss_sem, sr_sem, ds_sem, dr_sem, zs_sem, zr_sem, bs_sem, br_sem,
    es_sem, er_sem,
):
    d = lax.axis_index("dp")
    z = lax.axis_index("seq")
    zl = lax.rem(z + 3, 4)
    zr = lax.rem(z + 1, 4)
    zo = lax.rem(z + 2, 4)
    x, y, c = d // 8, lax.rem(d // 2, 4), lax.rem(d, 2)

    xs = [lax.rem(x + i, 4) * 8 for i in range(4)]
    ys = [lax.rem(y + i, 4) * 2 for i in range(4)]
    cs = [c, 1 - c]

    def shifted(n, sign):
        dx, dy, dc = OFFSETS[n]
        return xs[sign * dx % 4] + ys[sign * dy % 4] + cs[dc]

    def rows48(j):
        return pl.ds(pl.multiple_of(j * MSG, MSG), MSG)

    loads = []
    for i in range(3):
        part_of = pl.ds(i * D, D)
        loads.append(pltpu.make_async_copy(wqkv_h.at[:, part_of], wqkv.at[:, part_of], w_sem.at[i]))
    loads.append(pltpu.make_async_copy(wao_h, wao, w_sem.at[3]))
    loads.append(pltpu.make_async_copy(win_h, win, w_sem.at[4]))
    loads.append(pltpu.make_async_copy(wout_h, wout, w_sem.at[5]))
    for load in loads[:3]:
        load.start()

    barrier = pltpu.get_barrier_semaphore()
    for other in (zl, zr, zo):
        pl.semaphore_signal(barrier, inc=1, device_id=(d, other), device_id_type=MESH)

    for n in range(NE - 1):
        pl.semaphore_signal(barrier, inc=1, device_id=(shifted(n, 1), z), device_id_type=MESH)
    xn[pl.ds(0, TOK), :] = normalize(tok[...].astype(F32), lna[...].reshape(1, D)).astype(BF16)
    segs[0] = jnp.broadcast_to(seg[...], (8, TOK))
    pl.semaphore_wait(barrier, NE - 1 + 3)

    def remote(src, dst, s_sem, r_sem, dev):
        return pltpu.make_async_remote_copy(
            src_ref=src, dst_ref=dst, send_sem=s_sem, recv_sem=r_sem,
            device_id=dev, device_id_type=MESH,
        )

    right, left, across = (d, zr), (d, zl), (d, zo)

    def xrows(slot, half):
        return xn.at[pl.ds(slot * TOK + half * 64, 64), :]

    seg_copies = [
        remote(segs.at[0], segs.at[1], ss_sem.at[0], sr_sem.at[0], right),
        remote(segs.at[0], segs.at[2], ss_sem.at[1], sr_sem.at[1], left),
        remote(segs.at[0], segs.at[3], ss_sem.at[2], sr_sem.at[2], across),
    ]
    r0 = remote(xrows(0, 0), xrows(1, 0), as_sem.at[0], ar_sem.at[0], right)
    r1 = remote(xrows(0, 1), xrows(1, 1), as_sem.at[1], ar_sem.at[1], right)
    l1 = remote(xrows(0, 1), xrows(2, 1), as_sem.at[2], ar_sem.at[2], left)
    l0 = remote(xrows(0, 0), xrows(2, 0), as_sem.at[3], ar_sem.at[3], left)
    ro = remote(xrows(1, 0), xrows(3, 0), as_sem.at[4], ar_sem.at[4], right)
    lo = remote(xrows(2, 1), xrows(3, 1), as_sem.at[5], ar_sem.at[5], left)
    r0.start()
    l1.start()
    r1.start()
    l0.start()
    for copy in seg_copies:
        copy.start()
    for load in loads[3:]:
        load.start()

    e0, e1 = eid[0:1, :], eid[1:2, :]
    ei = iota((NE, TOK), 0)
    named = jnp.where((ei == e0) | (ei == e1), 1.0, 0.0).astype(BF16)
    before = jnp.where(iota((TOK, TOK), 0) < iota((TOK, TOK), 1), 1.0, 0.0).astype(BF16)
    count = dot(named, before)
    s0 = jnp.sum(jnp.where(ei == e0, count, 0.0), axis=0, keepdims=True)
    s1 = jnp.sum(jnp.where(ei == e1, count, 0.0), axis=0, keepdims=True)
    t0 = e0.astype(F32) * MSG + s0
    t1 = e1.astype(F32) * MSG + s1
    ri = iota((TOK, TOK), 0)
    square = jnp.where(
        ri == 0, t0, jnp.where(ri == 1, t1, jnp.where(ri == 2, gate[0:1, :], gate[1:2, :]))
    )
    gcol[...] = jnp.transpose(square)
    t0, t1 = t0.astype(I32), t1.astype(I32)

    def make_g(i):
        rows = pl.ds(i * 256, 256)
        r = iota((256, TOK), 0) + i * 256
        for cc in range(NC):
            hit = (r == t0 + CAP * cc) | (r == t1 + CAP * cc)
            g[rows, cc * TOK : (cc + 1) * TOK] = jnp.where(hit, 1.0, 0.0).astype(BF16)

    each(ALL // 256, make_g)

    def fixed(ref, q_dim, rows, first, base):
        q = iota(ref.shape, q_dim)
        r = iota(ref.shape, 1 - q_dim) + base
        if rows == 64:
            cc = lax.shift_right_logical(q, 6)
        else:
            cc = lax.shift_right_logical(q * 205, 14)
        i = q - cc * rows + first
        at = i + (MSG - CAP) * lax.shift_right_logical(i * 57, 9) + CAP * cc
        ref[...] = jnp.where(r == at, 1.0, 0.0).astype(BF16)

    fixed(unp0, 0, 64, 0, 0)
    fixed(unp1, 0, 80, 64, 7 * MSG)

    r0.wait_recv()
    ro.start()
    l1.wait_recv()
    lo.start()

    for load in loads[:3]:
        load.wait()

    def own_q(j):
        q[:, cols(j)] = dot(xn[pl.ds(0, TOK), :], wqkv[:, cols(j)]).astype(BF16)

    each(NC, own_q)

    def keys_values(first, number):
        rows = pl.ds(first, number)

        def step(j):
            k[rows, cols(j)] = dot(xn[rows, :], wqkv[:, cols(j + NC)]).astype(BF16)
            v[rows, cols(j)] = dot(xn[rows, :], wqkv[:, cols(j + 2 * NC)]).astype(BF16)

        each(NC, step)

    keys_values(0, TOK)
    fixed(pkm0, 1, 80, 0, 0)
    fixed(pkm1, 1, 80, 64, GM)

    r1.wait_recv()
    l0.wait_recv()
    keys_values(TOK, 2 * TOK)

    ri = iota((TOK, ALL), 1)
    c0, c1 = gcol[:, 0:1].astype(I32), gcol[:, 1:2].astype(I32)

    def make_pick(cc):
        base = cc * 256
        pick[pl.ds(base, TOK), :] = jnp.where(ri == c0 + CAP * cc, 1.0, 0.0).astype(BF16)
        pick[pl.ds(base + TOK, TOK), :] = jnp.where(ri == c1 + CAP * cc, 1.0, 0.0).astype(BF16)

    each(NC, make_pick)

    for copy in seg_copies:
        copy.wait_recv()
    eight = iota((8, TOK), 0)
    kinds = [jnp.where(eight == segs[s], 1.0, 0.0).astype(BF16) for s in range(4)]
    key_kind = jnp.concatenate(kinds, axis=1)
    same = lax.dot_general(kinds[0], key_kind, (((0,), (0,)), ((), ())), preferred_element_type=F32)
    bias = jnp.where(same > 0.5, 0.0, NEG)

    ro.wait_recv()
    lo.wait_recv()
    keys_values(3 * TOK, TOK)

    scale = HEAD ** (-0.5)
    ctx[...] = jnp.zeros((TOK, D), F32)
    for half in range(2):
        for heads, at in GROUPS:
            window = pl.ds(half * 640 + at, COL)
            lane = iota((TOK, COL), 1) + at
            masks = [(lane >= h * HEAD) & (lane < (h + 1) * HEAD) for h in heads]
            qw = q[:, window]
            zero = jnp.zeros_like(qw)
            stacked = jnp.concatenate([jnp.where(m, qw, zero) for m in masks], axis=0)
            scores = lax.dot_general(
                stacked, k[:, window], (((1,), (1,)), ((), ())), preferred_element_type=F32
            )
            probs, sums = [], []
            for n in range(len(heads)):
                s = scores[n * TOK : (n + 1) * TOK, :] * scale + bias
                w = jnp.exp(s - jnp.max(s, axis=-1, keepdims=True))
                sums.append(jnp.sum(w, axis=-1, keepdims=True))
                probs.append(w.astype(BF16))
            mixed = dot(jnp.concatenate(probs, axis=0), v[:, window])
            total = ctx[:, window]
            for n, m in enumerate(masks):
                total = jnp.where(m, mixed[n * TOK : (n + 1) * TOK, :] / sums[n], total)
            ctx[:, window] = total
    ctxb[...] = ctx[...].astype(BF16)

    loads[3].wait()

    def project(j):
        mid[:, cols(j)] = tok[:, cols(j)].astype(F32) + dot(ctxb[...], wao[:, cols(j)])

    each(NC, project)
    expert_in = normalize(mid[...], lne[...].reshape(1, D)).astype(BF16)
    for cc in range(NC):
        xp[pl.ds(cc * TOK, TOK), :] = expert_in[:, cc * COL : (cc + 1) * COL]

    def fill(i):
        rows = pl.ds(i * 256, 256)
        send[rows, :] = dot(g[rows, :], xp[...]).astype(BF16)

    each(ALL // 256, fill)

    for n in range(NE - 1):
        dest = shifted(n, 1)
        remote(
            send.at[rows48(dest), :], rcv.at[rows48(n), :], ds_sem, dr_sem.at[n // GS], (dest, z)
        ).start()
    rcv[pl.ds((NE - 1) * MSG, MSG), :] = send[rows48(d), :]

    def piece_of(slot, half, n):
        first, number = OUT[n]
        return a.at[slot, half, pl.ds(first, number)]

    def arrived(group):
        number = GS if group < 3 else GS - 1
        got = rcv.at[pl.ds(group * GM, number * MSG), :]
        remote(got, got, ds_sem, dr_sem.at[group], right).wait_recv()

    def unpack(half, n):
        first, number = OUT[n]
        arrived(2 * half + n)
        base = half * 2 * GM
        if n == 0:
            got = dot(unp0[...], rcv[pl.ds(base, GM), :])
        else:
            got = dot(unp1[...], rcv[pl.ds(base + 7 * MSG, 9 * MSG), :])
        for cc in range(NC):
            a[0, half, first : first + number, cc * COL : (cc + 1) * COL] = got[
                cc * number : (cc + 1) * number
            ].astype(BF16)

    zc = {}
    for half in range(2):
        for n in range(2):
            m = 2 * half + n
            zc["r", half, n] = remote(
                piece_of(0, half, n), piece_of(1, half, n), zs_sem.at[m], zr_sem.at[m], right
            )
            zc["l", half, n] = remote(
                piece_of(0, half, n), piece_of(2, half, n), zs_sem.at[4 + m], zr_sem.at[4 + m], left
            )
    for n in range(2):
        zc["ro", n] = remote(
            piece_of(1, 0, n), piece_of(3, 0, n), zs_sem.at[8 + n], zr_sem.at[8 + n], right
        )
        zc["lo", n] = remote(
            piece_of(2, 1, n), piece_of(3, 1, n), zs_sem.at[10 + n], zr_sem.at[10 + n], left
        )

    def expert(slot, half, store):
        def first(j):
            hid[:, cols(j)] = gelu(dot(a[slot, half], win[:, cols(j)])).astype(BF16)

        each(NC, first)

        def second(j):
            store(cols(j), dot(hid[...], wout[:, cols(j)]))

        each(NC, second)

    def into_own(half):
        def store(at, value):
            own[half, :, at] = value

        return store

    def into_part(n):
        def store(at, value):
            part[n, :, at] = value.astype(BF16)

        return store

    def into_keep(n):
        def store(at, value):
            keep[n, :, at] = value

        return store

    def back_of(ref, slot, n):
        first, number = BACK[n]
        return ref.at[slot, pl.ds(first, number)]

    b_left0 = remote(part.at[0], back.at[2], bs_sem.at[0], br_sem.at[0], left)
    b_right1 = remote(part.at[1], back.at[1], bs_sem.at[1], br_sem.at[1], right)
    bc = {}
    for n in range(2):
        for m, (key, src, dst, at, dev) in enumerate(
            (
                ("across0", 2, stage, 0, right),
                ("across1", 3, stage, 1, left),
                ("right0", 4, back, 0, right),
                ("left1", 5, back, 3, left),
            )
        ):
            bc[key, n] = remote(
                back_of(part, src, n), back_of(dst, at, n),
                bs_sem.at[2 + 2 * m + n], br_sem.at[2 + 2 * m + n], dev,
            )

    loads[4].wait()
    loads[5].wait()

    for half in range(2):
        for n in range(2):
            unpack(half, n)
            zc["r", half, n].start()
            zc["l", half, n].start()
    for n in range(2):
        zc["r", 0, n].wait_recv()
        zc["ro", n].start()
    expert(0, 0, into_own(0))
    for n in range(2):
        zc["l", 1, n].wait_recv()
        zc["lo", n].start()
    expert(1, 0, into_part(0))
    b_left0.start()
    expert(2, 1, into_part(1))
    b_right1.start()
    for n in range(2):
        zc["r", 1, n].wait_recv()
        zc["l", 0, n].wait_recv()
    expert(2, 0, into_keep(0))
    expert(1, 1, into_keep(1))
    expert(0, 1, into_own(1))
    for n in range(2):
        zc["ro", n].wait_recv()
    expert(3, 0, into_part(2))
    bc["across0", 0].start()
    bc["across0", 1].start()
    for n in range(2):
        zc["lo", n].wait_recv()
    expert(3, 1, into_part(3))
    bc["across1", 0].start()
    bc["across1", 1].start()
    for n in range(2):
        first, number = BACK[n]
        rows = pl.ds(first, number)
        bc["across0", n].wait_recv()
        part[4, rows] = (keep[0, rows] + stage[0, rows].astype(F32)).astype(BF16)
        bc["right0", n].start()
        bc["across1", n].wait_recv()
        part[5, rows] = (keep[1, rows] + stage[1, rows].astype(F32)).astype(BF16)
        bc["left1", n].start()

    b_left0.wait_recv()
    b_right1.wait_recv()
    for n in range(2):
        first, number = BACK[n]
        rows = pl.ds(first, number)
        for half in range(2):
            bc["right0" if half == 0 else "left1", n].wait_recv()
            for cc in range(NC):
                at = slice(cc * COL, (cc + 1) * COL)
                full = (
                    own[half, rows, at]
                    + back[half, rows, at].astype(F32)
                    + back[2 + half, rows, at].astype(F32)
                ).astype(BF16)
                if n == 0:
                    rst[half, 0, pl.ds(cc * 80, 80), :] = full
                    rst[half, 1, pl.ds(cc * 80, 16), :] = full[64:]
                else:
                    rst[half, 1, pl.ds(cc * 80 + 16, 64), :] = full
            packed = dot((pkm0 if n == 0 else pkm1)[...], rst[half, n])
            group = 2 * half + n
            pack[pl.ds(group * GM, GM), :] = packed.astype(BF16)
            for m in range(group * GS, min((group + 1) * GS, NE - 1)):
                dest = shifted(m, -1)
                remote(
                    pack.at[rows48(m), :], ret.at[rows48(d), :], es_sem, er_sem, (dest, z)
                ).start()
    ret[rows48(d), :] = pack[pl.ds((NE - 1) * MSG, MSG), :]

    others = ret.at[pl.ds(0, (NE - 1) * MSG), :]
    remote(others, others, es_sem, er_sem, right).wait_recv()
    g0, g1 = gcol[:, 2:3], gcol[:, 3:4]

    def final(cc):
        both = dot(pick[pl.ds(cc * 256, 256), :], ret[...])
        out[:, cols(cc)] = (mid[:, cols(cc)] + g0 * both[:TOK] + g1 * both[TOK:]).astype(BF16)

    each(NC, final)

    for copy in seg_copies + [r0, r1, l0, l1, ro, lo] + list(zc.values()):
        copy.wait_send()
    for copy in [b_left0, b_right1] + list(bc.values()):
        copy.wait_send()
    gone = send.at[pl.ds(0, (NE - 1) * MSG), :]
    remote(gone, gone, ds_sem, dr_sem.at[0], right).wait_send()
    gone = pack.at[pl.ds(0, (NE - 1) * MSG), :]
    remote(gone, gone, es_sem, er_sem, right).wait_send()


def layer(tok, seg, eid, gate, lna, lne, wqkv, wao, win, wout):
    vm = pl.BlockSpec(memory_space=pltpu.VMEM)
    hbm = pl.BlockSpec(memory_space=pl.ANY)
    V = pltpu.VMEM
    dma = pltpu.SemaphoreType.DMA
    return pl.pallas_call(
        kernel,
        out_shape=jax.ShapeDtypeStruct((TOK, D), BF16),
        in_specs=[vm] * 6 + [hbm] * 4,
        out_specs=vm,
        scratch_shapes=[
            V((D, 3 * D), BF16),
            V((D, D), BF16),
            V((D, D), BF16),
            V((D, D), BF16),
            V((4 * TOK, D), BF16),
            V((4, 8, TOK), I32),
            V((TOK, D), BF16),
            V((4 * TOK, D), BF16),
            V((4 * TOK, D), BF16),
            V((TOK, D), F32),
            V((TOK, D), BF16),
            V((TOK, D), F32),
            V((NC * TOK, COL), BF16),
            V((ALL, NC * TOK), BF16),
            V((ALL, COL), BF16),
            V((ALL, COL), BF16),
            V((4, 2, CR, D), BF16),
            V((CR, D), BF16),
            V((6, CR, D), BF16),
            V((2, CR, D), F32),
            V((2, CR, D), F32),
            V((2, CR, D), BF16),
            V((4, CR, D), BF16),
            V((2, 2, NC * 80, COL), BF16),
            V((ALL, COL), BF16),
            V((ALL, COL), BF16),
            V((2 * NC * TOK, ALL), BF16),
            V((NC * 64, GM), BF16),
            V((NC * 80, 9 * MSG), BF16),
            V((GM, NC * 80), BF16),
            V((GM, NC * 80), BF16),
            V((TOK, TOK), F32),
            dma((6,)),
            dma((6,)),
            dma((6,)),
            dma((3,)),
            dma((3,)),
            dma,
            dma((4,)),
            dma((12,)),
            dma((12,)),
            dma((10,)),
            dma((10,)),
            dma,
            dma,
        ],
        compiler_params=pltpu.CompilerParams(
            collective_id=0, has_side_effects=True, vmem_limit_bytes=60 * 1024 * 1024
        ),
        cost_estimate=pl.CostEstimate(
            flops=14_000_000_000, bytes_accessed=24_000_000, transcendentals=3_000_000
        ),
    )(tok, seg, eid, gate, lna, lne, wqkv, wao, win, wout)


def body(
    tokens, segment_ids, expert_ids, gate_values, ln_attn, w_qkv, w_attn_out, ln_expert, w_in, w_out
):
    out = layer(
        tokens[0],
        segment_ids,
        expert_ids[0].T,
        gate_values[0].T,
        ln_attn,
        ln_expert,
        w_qkv,
        w_attn_out,
        w_in[0],
        w_out[0],
    )
    return out[None]


def solution(mesh):
    placed = (
        P("dp", "seq", None),
        P("dp", "seq"),
        P("dp", "seq", None),
        P("dp", "seq", None),
        P(),
        P(),
        P(),
        P(),
        P("dp", None, "seq"),
        P("dp", "seq", None),
    )
    return jax.shard_map(
        body, mesh=mesh, in_specs=placed, out_specs=P("dp", "seq", None), check_vma=False
    )
```

```python
import functools

import jax
import jax.numpy as jnp
from jax import lax
from jax.experimental import pallas as pl
from jax.experimental.pallas import tpu as pltpu
from jax.sharding import PartitionSpec as P

F32 = jnp.float32
BF16 = jnp.bfloat16
I32 = jnp.int32
MESH = pl.DeviceIdType.MESH

D = 1280
HEADS = 16
HEAD = 80
TOK = 128
CAP = 9
NE = 32
COL = 256
NC = D // COL
PW = 896
FW = D - PW
MSG = 32
FMSG = 48
HALF = 16
CR = HALF * CAP
GS = 8
GM = GS * MSG
FGM = GS * FMSG
ALLF = NE * FMSG
ALL = NE * MSG
EPS = 1e-06
NEG = -1e30

GROUPS = (((0, 1, 2), 0), ((3,), 128), ((4, 5), 256), ((6, 7), 384))


OFFSETS = sorted(
    [(dx, dy, dc) for dx in range(4) for dy in range(4) for dc in range(2)],
    key=lambda o: -(min(o[0], 4 - o[0]) + min(o[1], 4 - o[1]) + 0.5 * o[2]),
)

OUT = ((0, 64), (64, 80))
BACK = ((0, 80), (80, 64))


def normalize(rows, gain):
    mean = jnp.mean(rows, axis=-1, keepdims=True)
    centered = rows - mean
    spread = jnp.mean(centered * centered, axis=-1, keepdims=True)
    return centered * lax.rsqrt(spread + EPS) * gain


def gelu(x):
    return 0.5 * x * (1.0 + jnp.tanh(0.7978845608028654 * (x + 0.044715 * (x * x * x))))


def iota(shape, dim):
    return lax.broadcasted_iota(I32, shape, dim)


def dot(a, b):
    return jnp.dot(a, b, preferred_element_type=F32)


def cols(j):
    return pl.ds(j * COL, COL)


def each(number, step):
    for i in range(number):
        step(i)


def kernel(
    tok, seg, eid, gate, lna, lne, wqkv_h, wao_h, win_h, wout_h, out,
    wqkv, wao, win, wout, xn, info, q, k, v, ctx, ctxb, mid, xp, g, send, rcv, a, hid,
    part, keep, own, stage, back, rst, pack, ret, unp0, unp1, pkm0, pkm1, gcol,
    zx, gf, fsend, frcv, unf, pkf, frst, fpack, fret, fpart, fout, fown, fstage, fback,
    w_sem, as_sem, ar_sem, ss_sem, sr_sem, ds_sem, dr_sem, zs_sem, zr_sem, bs_sem, br_sem,
    es_sem, er_sem, xs_sem, xr_sem, fds_sem, fdr_sem, fes_sem, fer_sem, ys_sem, yr_sem,
):
    pick = wqkv.at[:, pl.ds(0, ALL)]
    fpick = wqkv.at[pl.ds(0, 4 * 256), pl.ds(ALL, ALLF)]
    d = lax.axis_index("dp")
    z = lax.axis_index("seq")
    zl = lax.rem(z + 3, 4)
    zr = lax.rem(z + 1, 4)
    zo = lax.rem(z + 2, 4)
    x, y, c = d // 8, lax.rem(d // 2, 4), lax.rem(d, 2)

    xs = [lax.rem(x + i, 4) * 8 for i in range(4)]
    ys = [lax.rem(y + i, 4) * 2 for i in range(4)]
    cs = [c, 1 - c]

    def shifted(n, sign):
        dx, dy, dc = OFFSETS[n]
        return xs[sign * dx % 4] + ys[sign * dy % 4] + cs[dc]

    def rows_of(j):
        return pl.ds(pl.multiple_of(j * MSG, MSG), MSG)

    def frows_of(j):
        return pl.ds(pl.multiple_of(j * FMSG, FMSG), FMSG)

    loads = []
    for i in range(3):
        part_of = pl.ds(i * D, D)
        loads.append(pltpu.make_async_copy(wqkv_h.at[:, part_of], wqkv.at[:, part_of], w_sem.at[i]))
    loads.append(pltpu.make_async_copy(wao_h, wao, w_sem.at[3]))
    loads.append(pltpu.make_async_copy(win_h, win, w_sem.at[4]))
    loads.append(pltpu.make_async_copy(wout_h, wout, w_sem.at[5]))
    for load in loads[:3]:
        load.start()

    barrier = pltpu.get_barrier_semaphore()
    for other in (zl, zr, zo):
        pl.semaphore_signal(barrier, inc=1, device_id=(d, other), device_id_type=MESH)

    for n in range(NE - 1):
        pl.semaphore_signal(barrier, inc=1, device_id=(shifted(n, 1), z), device_id_type=MESH)
    xn[pl.ds(0, TOK), :] = normalize(tok[...].astype(F32), lna[...].reshape(1, D)).astype(BF16)

    e0, e1 = eid[0:1, :], eid[1:2, :]
    ei = iota((NE, TOK), 0)
    named = jnp.where((ei == e0) | (ei == e1), 1.0, 0.0).astype(BF16)
    before = jnp.where(iota((TOK, TOK), 0) < iota((TOK, TOK), 1), 1.0, 0.0).astype(BF16)
    count = dot(named, before)
    chosen = []
    lines = [seg[...].astype(F32)]
    for e in (e0, e1):
        slot = jnp.sum(jnp.where(ei == e, count, 0.0), axis=0, keepdims=True).astype(I32)
        lines.append((e * FMSG + slot).astype(F32))
        odd = slot & 1
        pair = e * MSG + 3 * CAP + lax.shift_right_logical(slot, 1)
        chosen.append(
            (e * MSG + slot, jnp.where(odd == 0, pair, -1), jnp.where(odd == 1, pair, -1))
        )
    lines += [gate[0:1, :], gate[1:2, :]]
    ri = iota((8, TOK), 0)

    def stacked_lines(rows):
        total = jnp.zeros((8, TOK), F32)
        for n, row in enumerate(rows):
            total = jnp.where(ri == n, row, total)
        return total

    info[0] = stacked_lines(lines)
    pl.semaphore_wait(barrier, NE - 1 + 3)

    def remote(src, dst, s_sem, r_sem, dev):
        return pltpu.make_async_remote_copy(
            src_ref=src, dst_ref=dst, send_sem=s_sem, recv_sem=r_sem,
            device_id=dev, device_id_type=MESH,
        )

    right, left, across = (d, zr), (d, zl), (d, zo)

    def xrows(slot, half):
        return xn.at[pl.ds(slot * TOK + half * 64, 64), :]

    seg_copies = [
        remote(info.at[0], info.at[1], ss_sem.at[0], sr_sem.at[0], right),
        remote(info.at[0], info.at[2], ss_sem.at[1], sr_sem.at[1], left),
        remote(info.at[0], info.at[3], ss_sem.at[2], sr_sem.at[2], across),
    ]
    r0 = remote(xrows(0, 0), xrows(1, 0), as_sem.at[0], ar_sem.at[0], right)
    r1 = remote(xrows(0, 1), xrows(1, 1), as_sem.at[1], ar_sem.at[1], right)
    l1 = remote(xrows(0, 1), xrows(2, 1), as_sem.at[2], ar_sem.at[2], left)
    l0 = remote(xrows(0, 0), xrows(2, 0), as_sem.at[3], ar_sem.at[3], left)
    ro = remote(xrows(1, 0), xrows(3, 0), as_sem.at[4], ar_sem.at[4], right)
    lo = remote(xrows(2, 1), xrows(3, 1), as_sem.at[5], ar_sem.at[5], left)
    r0.start()
    l1.start()
    r1.start()
    l0.start()
    for copy in seg_copies:
        copy.start()
    for load in loads[3:]:
        load.start()

    def place(kind, cc):
        return chosen[kind][0] + CAP * cc if cc < 3 else chosen[kind][cc - 2]

    def make_g(i):
        rows = pl.ds(i * 256, 256)
        r = iota((256, TOK), 0) + i * 256
        for cc in range(NC):
            hit = (r == place(0, cc)) | (r == place(1, cc))
            g[rows, cc * TOK : (cc + 1) * TOK] = jnp.where(hit, 1.0, 0.0).astype(BF16)

    each(ALL // 256, make_g)

    def fixed(ref, q_dim, rows, first, base, msg):
        q = iota(ref.shape, q_dim)
        r = iota(ref.shape, 1 - q_dim) + base
        times, shift = {64: (1, 6), 80: (205, 14), CR: (1821, 18)}[rows]
        cc = lax.shift_right_logical(q * times, shift)
        i = q - cc * rows + first
        source = lax.shift_right_logical(i * 57, 9)
        slot = i - CAP * source
        at = source * msg + CAP * cc + slot
        if msg == MSG:
            pair = source * msg + 3 * CAP + lax.shift_right_logical(slot, 1)
            at = jnp.where(cc < 3, at, jnp.where((slot & 1) == cc - 3, pair, -1))
        ref[...] = jnp.where(r == at, 1.0, 0.0).astype(BF16)

    fixed(unp0, 0, 64, 0, 0, MSG)
    fixed(unp1, 0, 80, 64, 7 * MSG, MSG)

    r0.wait_recv()
    ro.start()
    l1.wait_recv()
    lo.start()

    for load in loads[:3]:
        load.wait()

    def own_q(j):
        q[:, cols(j)] = dot(xn[pl.ds(0, TOK), :], wqkv[:, cols(j)]).astype(BF16)

    each(NC, own_q)

    def keys_values(first, number):
        rows = pl.ds(first, number)

        def step(j):
            k[rows, cols(j)] = dot(xn[rows, :], wqkv[:, cols(j + NC)]).astype(BF16)
            v[rows, cols(j)] = dot(xn[rows, :], wqkv[:, cols(j + 2 * NC)]).astype(BF16)

        each(NC, step)

    keys_values(0, TOK)
    fixed(pkm0, 1, 80, 0, 0, MSG)
    fixed(pkm1, 1, 80, 64, GM, MSG)
    fixed(unf, 0, CR, 0, 0, FMSG)
    fixed(pkf, 1, CR, 0, 0, FMSG)

    r1.wait_recv()
    l0.wait_recv()
    keys_values(TOK, 2 * TOK)

    for copy in seg_copies:
        copy.wait_recv()
    eight = iota((8, TOK), 0).astype(F32)
    kinds = [jnp.where(eight == info[s, 0:1, :], 1.0, 0.0).astype(BF16) for s in range(4)]
    key_kind = jnp.concatenate(kinds, axis=1)
    same = lax.dot_general(kinds[0], key_kind, (((0,), (0,)), ((), ())), preferred_element_type=F32)
    bias = jnp.where(same > 0.5, 0.0, NEG)

    for s in range(4):
        more = jnp.zeros((8, TOK), F32)
        if s == 0:
            more = stacked_lines([row.astype(F32) for kind in chosen for row in kind])
        square = jnp.concatenate([info[s], more, jnp.zeros((TOK - 16, TOK), F32)], axis=0)
        gcol[s] = jnp.transpose(square)
        r = iota((ALLF, TOK), 0) - CAP * s
        f0, f1 = info[s, 1:2, :].astype(I32), info[s, 2:3, :].astype(I32)
        gf[:, s * TOK : (s + 1) * TOK] = jnp.where((r == f0) | (r == f1), 1.0, 0.0).astype(BF16)

    ro.wait_recv()
    lo.wait_recv()
    keys_values(3 * TOK, TOK)

    scale = HEAD ** (-0.5)
    ctx[...] = jnp.zeros((TOK, D), F32)
    for half in range(2):
        for heads, at in GROUPS:
            window = pl.ds(half * 640 + at, COL)
            lane = iota((TOK, COL), 1) + at
            masks = [(lane >= h * HEAD) & (lane < (h + 1) * HEAD) for h in heads]
            qw = q[:, window]
            zero = jnp.zeros_like(qw)
            stacked = jnp.concatenate([jnp.where(m, qw, zero) for m in masks], axis=0)
            scores = lax.dot_general(
                stacked, k[:, window], (((1,), (1,)), ((), ())), preferred_element_type=F32
            )
            probs, sums = [], []
            for n in range(len(heads)):
                s = scores[n * TOK : (n + 1) * TOK, :] * scale + bias
                w = jnp.exp(s - jnp.max(s, axis=-1, keepdims=True))
                sums.append(jnp.sum(w, axis=-1, keepdims=True))
                probs.append(w.astype(BF16))
            mixed = dot(jnp.concatenate(probs, axis=0), v[:, window])
            total = ctx[:, window]
            for n, m in enumerate(masks):
                total = jnp.where(m, mixed[n * TOK : (n + 1) * TOK, :] / sums[n], total)
            ctx[:, window] = total
    ctxb[...] = ctx[...].astype(BF16)

    loads[3].wait()

    def project(j):
        mid[:, cols(j)] = tok[:, cols(j)].astype(F32) + dot(ctxb[...], wao[:, cols(j)])

    each(NC, project)
    expert_in = normalize(mid[...], lne[...].reshape(1, D)).astype(BF16)
    zx[pl.ds(0, TOK), :] = expert_in[:, PW:]

    def zrows(slot, half):
        return zx.at[pl.ds(slot * TOK + half * 64, 64), :]

    xr0 = remote(zrows(0, 0), zrows(1, 0), xs_sem.at[0], xr_sem.at[0], right)
    xr1 = remote(zrows(0, 1), zrows(1, 1), xs_sem.at[1], xr_sem.at[1], right)
    xl1 = remote(zrows(0, 1), zrows(2, 1), xs_sem.at[2], xr_sem.at[2], left)
    xl0 = remote(zrows(0, 0), zrows(2, 0), xs_sem.at[3], xr_sem.at[3], left)
    xro = remote(zrows(1, 0), zrows(3, 0), xs_sem.at[4], xr_sem.at[4], right)
    xlo = remote(zrows(2, 1), zrows(3, 1), xs_sem.at[5], xr_sem.at[5], left)
    ring = [xr0, xr1, xl1, xl0, xro, xlo]
    for copy in ring[:4]:
        copy.start()

    for cc in range(3):
        xp[pl.ds(cc * TOK, TOK), :] = expert_in[:, cc * COL : (cc + 1) * COL]
    rest = expert_in[:, 3 * COL : PW]
    none = jnp.zeros_like(rest)
    xp[pl.ds(3 * TOK, TOK), :] = jnp.concatenate([rest, none], axis=1)
    xp[pl.ds(4 * TOK, TOK), :] = jnp.concatenate([none, rest], axis=1)

    def fill(i):
        rows = pl.ds(i * 256, 256)
        send[rows, :] = dot(g[rows, :], xp[...]).astype(BF16)

    each(ALL // 256, fill)

    for n in range(NE - 1):
        dest = shifted(n, 1)
        remote(
            send.at[rows_of(dest), :], rcv.at[rows_of(n), :], ds_sem, dr_sem.at[n // GS], (dest, z)
        ).start()
    rcv[pl.ds((NE - 1) * MSG, MSG), :] = send[rows_of(d), :]

    def piece_of(slot, half, n):
        first, number = OUT[n]
        return a.at[slot, half, pl.ds(first, number), pl.ds(0, PW)]

    def arrived(group):
        number = GS if group < 3 else GS - 1
        got = rcv.at[pl.ds(group * GM, number * MSG), :]
        remote(got, got, ds_sem, dr_sem.at[group], right).wait_recv()

    def unpack(half, n):
        first, number = OUT[n]
        arrived(2 * half + n)
        base = half * 2 * GM
        if n == 0:
            got = dot(unp0[...], rcv[pl.ds(base, GM), :])
        else:
            got = dot(unp1[...], rcv[pl.ds(base + 7 * MSG, 9 * MSG), :])
        rows = slice(first, first + number)
        for cc in range(3):
            a[0, half, rows, cc * COL : (cc + 1) * COL] = got[
                cc * number : (cc + 1) * number
            ].astype(BF16)
        a[0, half, rows, 3 * COL : PW] = (
            got[3 * number : 4 * number, :128] + got[4 * number :, 128:]
        ).astype(BF16)

    zc = {}
    for half in range(2):
        for n in range(2):
            m = 2 * half + n
            zc["r", half, n] = remote(
                piece_of(0, half, n), piece_of(1, half, n), zs_sem.at[m], zr_sem.at[m], right
            )
            zc["l", half, n] = remote(
                piece_of(0, half, n), piece_of(2, half, n), zs_sem.at[4 + m], zr_sem.at[4 + m], left
            )
    for n in range(2):
        zc["ro", n] = remote(
            piece_of(1, 0, n), piece_of(3, 0, n), zs_sem.at[8 + n], zr_sem.at[8 + n], right
        )
        zc["lo", n] = remote(
            piece_of(2, 1, n), piece_of(3, 1, n), zs_sem.at[10 + n], zr_sem.at[10 + n], left
        )

    def expert(slot, half, store):
        def first(j):
            hid[:, cols(j)] = gelu(dot(a[slot, half], win[:, cols(j)])).astype(BF16)

        each(NC, first)
        for j in range(3):
            store(cols(j), dot(hid[...], wout[:, cols(j)]))
        value = dot(hid[...], wout[:, 3 * COL :])
        store(pl.ds(3 * COL, 128), value[:, :128])
        frst[half, pl.ds(slot * CR, CR), :] = value[:, 128:].astype(BF16)

    def into_own(half):
        def store(at, value):
            own[half, :, at] = value

        return store

    def into_part(n):
        def store(at, value):
            part[n, :, at] = value.astype(BF16)

        return store

    def into_keep(n):
        def store(at, value):
            keep[n, :, at] = value

        return store

    def back_of(ref, slot, n):
        first, number = BACK[n]
        return ref.at[slot, pl.ds(first, number)]

    b_left0 = remote(part.at[0], back.at[2], bs_sem.at[0], br_sem.at[0], left)
    b_right1 = remote(part.at[1], back.at[1], bs_sem.at[1], br_sem.at[1], right)
    bc = {}
    for n in range(2):
        for m, (key, src, dst, at, dev) in enumerate(
            (
                ("across0", 2, stage, 0, right),
                ("across1", 3, stage, 1, left),
                ("right0", 4, back, 0, right),
                ("left1", 5, back, 3, left),
            )
        ):
            bc[key, n] = remote(
                back_of(part, src, n), back_of(dst, at, n),
                bs_sem.at[2 + 2 * m + n], br_sem.at[2 + 2 * m + n], dev,
            )

    loads[4].wait()
    loads[5].wait()

    xr0.wait_recv()
    xro.start()
    xl1.wait_recv()
    xlo.start()
    for n in range(2):
        unpack(0, n)
        zc["r", 0, n].start()
        zc["l", 0, n].start()
    for copy in (xr1, xl0, xro, xlo):
        copy.wait_recv()
    for i in range(ALLF // 256):
        rows = pl.ds(i * 256, 256)
        fsend[rows, :] = dot(gf[rows, :], zx[...]).astype(BF16)
    for n in range(NE - 1):
        dest = shifted(n, 1)
        remote(
            fsend.at[frows_of(dest), :], frcv.at[frows_of(n), :],
            fds_sem, fdr_sem.at[n // HALF], (dest, z),
        ).start()
    frcv[pl.ds((NE - 1) * FMSG, FMSG), :] = fsend[frows_of(d), :]
    for n in range(2):
        unpack(1, n)
        zc["r", 1, n].start()
        zc["l", 1, n].start()

    ri = iota((TOK, ALL), 1)
    for cc in range(NC):
        line = 8 if cc < 3 else 6 + cc
        for kind in range(2):
            at = gcol[0, :, line + 3 * kind : line + 3 * kind + 1].astype(I32)
            at = at + CAP * cc if cc < 3 else at
            pick[pl.ds(cc * 256 + kind * TOK, TOK), :] = jnp.where(ri == at, 1.0, 0.0).astype(BF16)
    for n in range(2):
        zc["r", 0, n].wait_recv()
        zc["ro", n].start()
    fi = iota((TOK, ALLF), 1)
    for s in range(4):
        for kind in range(2):
            at = gcol[s, :, 1 + kind : 2 + kind].astype(I32) + CAP * s
            fpick[pl.ds(s * 256 + kind * TOK, TOK), :] = jnp.where(fi == at, 1.0, 0.0).astype(BF16)
    for n in range(2):
        zc["l", 1, n].wait_recv()
        zc["lo", n].start()

    def funpack(half):
        number = HALF if half == 0 else HALF - 1
        got = frcv.at[pl.ds(half * HALF * FMSG, number * FMSG), :]
        remote(got, got, fds_sem, fdr_sem.at[half], right).wait_recv()
        rows = dot(unf[...], frcv[pl.ds(half * HALF * FMSG, HALF * FMSG), :]).astype(BF16)
        for s in range(4):
            a[s, half, :, PW:] = rows[s * CR : (s + 1) * CR]

    def freturn(half):
        fpack[pl.ds(half * HALF * FMSG, HALF * FMSG), :] = dot(pkf[...], frst[half]).astype(BF16)
        for m in range(half * HALF, min((half + 1) * HALF, NE - 1)):
            dest = shifted(m, -1)
            remote(
                fpack.at[frows_of(m), :], fret.at[frows_of(d), :], fes_sem, fer_sem, (dest, z)
            ).start()

    funpack(0)
    expert(1, 0, into_part(0))
    b_left0.start()
    for n in range(2):
        zc["l", 0, n].wait_recv()
    expert(2, 0, into_keep(0))
    expert(0, 0, into_own(0))
    for n in range(2):
        zc["ro", n].wait_recv()
    expert(3, 0, into_part(2))
    bc["across0", 0].start()
    bc["across0", 1].start()
    freturn(0)
    for n in range(2):
        zc["r", 1, n].wait_recv()
        zc["lo", n].wait_recv()
    funpack(1)
    expert(3, 1, into_part(3))
    bc["across1", 0].start()
    bc["across1", 1].start()
    expert(2, 1, into_part(1))
    b_right1.start()
    expert(1, 1, into_keep(1))
    expert(0, 1, into_own(1))
    freturn(1)
    fret[frows_of(d), :] = fpack[pl.ds((NE - 1) * FMSG, FMSG), :]
    for n in range(2):
        first, number = BACK[n]
        rows = pl.ds(first, number)
        bc["across0", n].wait_recv()
        part[4, rows] = (keep[0, rows] + stage[0, rows].astype(F32)).astype(BF16)
        bc["right0", n].start()
        bc["across1", n].wait_recv()
        part[5, rows] = (keep[1, rows] + stage[1, rows].astype(F32)).astype(BF16)
        bc["left1", n].start()

    def half_of(ref, slot, n):
        return ref.at[slot, pl.ds(n * 64, 64)]

    ya0 = remote(half_of(fout, 3, 0), fstage.at[0], ys_sem.at[0], yr_sem.at[0], right)
    ya1 = remote(half_of(fout, 3, 1), fstage.at[1], ys_sem.at[1], yr_sem.at[1], left)
    yl0 = remote(half_of(fout, 1, 0), half_of(fback, 1, 0), ys_sem.at[2], yr_sem.at[2], left)
    yr1 = remote(half_of(fout, 2, 1), half_of(fback, 0, 1), ys_sem.at[3], yr_sem.at[3], right)
    yr0 = remote(half_of(fout, 2, 0), half_of(fback, 0, 0), ys_sem.at[4], yr_sem.at[4], right)
    yl1 = remote(half_of(fout, 1, 1), half_of(fback, 1, 1), ys_sem.at[5], yr_sem.at[5], left)
    ring += [ya0, ya1, yl0, yr1, yr0, yl1]

    b_left0.wait_recv()
    b_right1.wait_recv()
    def finish(n):
        first, number = BACK[n]
        rows = pl.ds(first, number)
        for half in range(2):
            bc["right0" if half == 0 else "left1", n].wait_recv()
            for cc in range(4):
                at = slice(cc * COL, min((cc + 1) * COL, PW))
                full = (
                    own[half, rows, at]
                    + back[half, rows, at].astype(F32)
                    + back[2 + half, rows, at].astype(F32)
                ).astype(BF16)
                both = [full]
                if cc == 3:
                    none = jnp.zeros_like(full)
                    both = [
                        jnp.concatenate([full, none], axis=1),
                        jnp.concatenate([none, full], axis=1),
                    ]
                for m, value in enumerate(both):
                    if n == 0:
                        rst[half, 0, pl.ds((cc + m) * 80, 80), :] = value
                        rst[half, 1, pl.ds((cc + m) * 80, 16), :] = value[64:]
                    else:
                        rst[half, 1, pl.ds((cc + m) * 80 + 16, 64), :] = value
            packed = dot((pkm0 if n == 0 else pkm1)[...], rst[half, n])
            group = 2 * half + n
            pack[pl.ds(group * GM, GM), :] = packed.astype(BF16)
            for m in range(group * GS, min((group + 1) * GS, NE - 1)):
                dest = shifted(m, -1)
                remote(
                    pack.at[rows_of(m), :], ret.at[rows_of(d), :], es_sem, er_sem, (dest, z)
                ).start()
    finish(0)

    others = fret.at[pl.ds(0, (NE - 1) * FMSG), :]
    remote(others, others, fes_sem, fer_sem, right).wait_recv()
    for s in (3, 1, 2, 0):
        both = dot(fpick[pl.ds(s * 256, 256), :], fret[...])
        sums = gcol[s, :, 3:4] * both[:TOK] + gcol[s, :, 4:5] * both[TOK:]
        if s == 0:
            fown[...] = sums
        else:
            fpart[s] = sums
            for n in range(2):
                rows = pl.ds(n * 64, 64)
                fout[s, rows] = sums[n * 64 : (n + 1) * 64].astype(BF16)
        if s == 3:
            ya0.start()
            ya1.start()
        if s == 1:
            yl0.start()
        if s == 2:
            yr1.start()

    finish(1)
    ret[rows_of(d), :] = pack[pl.ds((NE - 1) * MSG, MSG), :]

    ya0.wait_recv()
    fout[2, pl.ds(0, 64)] = (fpart[2, pl.ds(0, 64)] + fstage[0].astype(F32)).astype(BF16)
    yr0.start()
    ya1.wait_recv()
    fout[1, pl.ds(64, 64)] = (fpart[1, pl.ds(64, 64)] + fstage[1].astype(F32)).astype(BF16)
    yl1.start()

    others = ret.at[pl.ds(0, (NE - 1) * MSG), :]
    remote(others, others, es_sem, er_sem, right).wait_recv()
    g0, g1 = gcol[0, :, 3:4], gcol[0, :, 4:5]
    for cc in range(3):
        both = dot(pick[pl.ds(cc * 256, 256), :], ret[...])
        out[:, cols(cc)] = (mid[:, cols(cc)] + g0 * both[:TOK] + g1 * both[TOK:]).astype(BF16)
    even = dot(pick[pl.ds(3 * 256, 256), :], ret[...])[:, :128]
    both = even + dot(pick[pl.ds(4 * 256, 256), :], ret[...])[:, 128:]
    out[:, 3 * COL : PW] = (
        mid[:, 3 * COL : PW] + g0 * both[:TOK] + g1 * both[TOK:]
    ).astype(BF16)
    for copy in (yl0, yr1, yr0, yl1):
        copy.wait_recv()
    out[:, PW:] = (
        mid[:, PW:] + fown[...] + fback[0].astype(F32) + fback[1].astype(F32)
    ).astype(BF16)

    for copy in seg_copies + [r0, r1, l0, l1, ro, lo] + ring + list(zc.values()):
        copy.wait_send()
    for copy in [b_left0, b_right1] + list(bc.values()):
        copy.wait_send()
    gone = send.at[pl.ds(0, (NE - 1) * MSG), :]
    remote(gone, gone, ds_sem, dr_sem.at[0], right).wait_send()
    gone = pack.at[pl.ds(0, (NE - 1) * MSG), :]
    remote(gone, gone, es_sem, er_sem, right).wait_send()
    gone = fsend.at[pl.ds(0, (NE - 1) * FMSG), :]
    remote(gone, gone, fds_sem, fdr_sem.at[0], right).wait_send()
    gone = fpack.at[pl.ds(0, (NE - 1) * FMSG), :]
    remote(gone, gone, fes_sem, fer_sem, right).wait_send()


def layer(tok, seg, eid, gate, lna, lne, wqkv, wao, win, wout):
    vm = pl.BlockSpec(memory_space=pltpu.VMEM)
    hbm = pl.BlockSpec(memory_space=pl.ANY)
    V = pltpu.VMEM
    dma = pltpu.SemaphoreType.DMA
    return pl.pallas_call(
        kernel,
        out_shape=jax.ShapeDtypeStruct((TOK, D), BF16),
        in_specs=[vm] * 6 + [hbm] * 4,
        out_specs=vm,
        scratch_shapes=[
            V((D, 3 * D), BF16),
            V((D, D), BF16),
            V((D, D), BF16),
            V((D, D), BF16),
            V((4 * TOK, D), BF16),
            V((4, 8, TOK), F32),
            V((TOK, D), BF16),
            V((4 * TOK, D), BF16),
            V((4 * TOK, D), BF16),
            V((TOK, D), F32),
            V((TOK, D), BF16),
            V((TOK, D), F32),
            V((NC * TOK, COL), BF16),
            V((ALL, NC * TOK), BF16),
            V((ALL, COL), BF16),
            V((ALL, COL), BF16),
            V((4, 2, CR, D), BF16),
            V((CR, D), BF16),
            V((6, CR, PW), BF16),
            V((2, CR, PW), F32),
            V((2, CR, PW), F32),
            V((2, CR, PW), BF16),
            V((4, CR, PW), BF16),
            V((2, 2, NC * 80, COL), BF16),
            V((ALL, COL), BF16),
            V((ALL, COL), BF16),
            V((NC * 64, GM), BF16),
            V((NC * 80, 9 * MSG), BF16),
            V((GM, NC * 80), BF16),
            V((GM, NC * 80), BF16),
            V((4, TOK, TOK), F32),
            V((4 * TOK, FW), BF16),
            V((ALLF, 4 * TOK), BF16),
            V((ALLF, FW), BF16),
            V((ALLF, FW), BF16),
            V((4 * CR, HALF * FMSG), BF16),
            V((HALF * FMSG, 4 * CR), BF16),
            V((2, 4 * CR, FW), BF16),
            V((ALLF, FW), BF16),
            V((ALLF, FW), BF16),
            V((4, TOK, FW), F32),
            V((4, TOK, FW), BF16),
            V((TOK, FW), F32),
            V((2, 64, FW), BF16),
            V((2, TOK, FW), BF16),
            dma((6,)),
            dma((6,)),
            dma((6,)),
            dma((3,)),
            dma((3,)),
            dma,
            dma((4,)),
            dma((12,)),
            dma((12,)),
            dma((10,)),
            dma((10,)),
            dma,
            dma,
            dma((6,)),
            dma((6,)),
            dma,
            dma((2,)),
            dma,
            dma,
            dma((6,)),
            dma((6,)),
        ],
        compiler_params=pltpu.CompilerParams(
            collective_id=0, has_side_effects=True, vmem_limit_bytes=60 * 1024 * 1024
        ),
        cost_estimate=pl.CostEstimate(
            flops=14_000_000_000, bytes_accessed=24_000_000, transcendentals=3_000_000
        ),
    )(tok, seg, eid, gate, lna, lne, wqkv, wao, win, wout)


def body(
    tokens, segment_ids, expert_ids, gate_values, ln_attn, w_qkv, w_attn_out, ln_expert, w_in, w_out
):
    out = layer(
        tokens[0],
        segment_ids,
        expert_ids[0].T,
        gate_values[0].T,
        ln_attn,
        ln_expert,
        w_qkv,
        w_attn_out,
        w_in[0],
        w_out[0],
    )
    return out[None]


def solution(mesh):
    placed = (
        P("dp", "seq", None),
        P("dp", "seq"),
        P("dp", "seq", None),
        P("dp", "seq", None),
        P(),
        P(),
        P(),
        P(),
        P("dp", None, "seq"),
        P("dp", "seq", None),
    )
    return jax.shard_map(
        body, mesh=mesh, in_specs=placed, out_specs=P("dp", "seq", None), check_vma=False
    )
```

```python
import functools

import jax
import jax.numpy as jnp
from jax import lax
from jax.experimental import pallas as pl
from jax.experimental.pallas import tpu as pltpu
from jax.sharding import PartitionSpec as P

F32 = jnp.float32
BF16 = jnp.bfloat16
I32 = jnp.int32
MESH = pl.DeviceIdType.MESH

D = 1280
HEADS = 16
HEAD = 80
TOK = 128
CAP = 9
NE = 32
COL = 256
NC = D // COL
PW = 896
FW = D - PW
MSG = 32
FMSG = 48
HALF = 16
CR = HALF * CAP
GS = 8
GM = GS * MSG
FGM = GS * FMSG
ALLF = NE * FMSG
ALL = NE * MSG
EPS = 1e-06
NEG = -1e30

GROUPS = (((0, 1, 2), 0), ((3,), 128), ((4, 5), 256), ((6, 7), 384))


OFFSETS = sorted(
    [(dx, dy, dc) for dx in range(4) for dy in range(4) for dc in range(2)],
    key=lambda o: -(min(o[0], 4 - o[0]) + min(o[1], 4 - o[1]) + 0.5 * o[2]),
)

OUT = ((0, 64), (64, 80))
BACK = ((0, 80), (80, 64))


def normalize(rows, gain):
    mean = jnp.mean(rows, axis=-1, keepdims=True)
    centered = rows - mean
    spread = jnp.mean(centered * centered, axis=-1, keepdims=True)
    return centered * lax.rsqrt(spread + EPS) * gain


def gelu(x):
    return 0.5 * x * (1.0 + jnp.tanh(0.7978845608028654 * (x + 0.044715 * (x * x * x))))


def iota(shape, dim):
    return lax.broadcasted_iota(I32, shape, dim)


def dot(a, b):
    return jnp.dot(a, b, preferred_element_type=F32)


def cols(j):
    return pl.ds(j * COL, COL)


def each(number, step):
    for i in range(number):
        step(i)


def kernel(
    tok, seg, eid, gate, lna, lne, wqkv_h, wao_h, win_h, wout_h, out,
    wqkv, wao, win, wout, xn, info, q, k, v, ctx, ctxb, mid, xp, g, send, rcv, a, hid,
    part, keep, own, stage, back, rst, pack, ret, unp0, unp1, pkm0, pkm1, gcol,
    zx, gf, fsend, frcv, unf, pkf, frst, fpack, fret, fpart, fout, fown, fstage, fback,
    w_sem, as_sem, ar_sem, ss_sem, sr_sem, ds_sem, dr_sem, zs_sem, zr_sem, bs_sem, br_sem,
    es_sem, er_sem, round_sem, xs_sem, xr_sem, fds_sem, fdr_sem, fes_sem, fer_sem, ys_sem, yr_sem,
):
    pick = wqkv.at[:, pl.ds(0, ALL)]
    fpick = wqkv.at[pl.ds(0, 4 * 256), pl.ds(ALL, ALLF)]
    d = lax.axis_index("dp")
    z = lax.axis_index("seq")
    zl = lax.rem(z + 3, 4)
    zr = lax.rem(z + 1, 4)
    zo = lax.rem(z + 2, 4)
    x, y, c = d // 8, lax.rem(d // 2, 4), lax.rem(d, 2)

    xs = [lax.rem(x + i, 4) * 8 for i in range(4)]
    ys = [lax.rem(y + i, 4) * 2 for i in range(4)]
    cs = [c, 1 - c]

    def shifted(n, sign):
        dx, dy, dc = OFFSETS[n]
        return xs[sign * dx % 4] + ys[sign * dy % 4] + cs[dc]

    def rows_of(j):
        return pl.ds(pl.multiple_of(j * MSG, MSG), MSG)

    def frows_of(j):
        return pl.ds(pl.multiple_of(j * FMSG, FMSG), FMSG)

    loads = []
    for i in range(3):
        part_of = pl.ds(i * D, D)
        loads.append(pltpu.make_async_copy(wqkv_h.at[:, part_of], wqkv.at[:, part_of], w_sem.at[i]))
    loads.append(pltpu.make_async_copy(wao_h, wao, w_sem.at[3]))
    loads.append(pltpu.make_async_copy(win_h, win, w_sem.at[4]))
    loads.append(pltpu.make_async_copy(wout_h, wout, w_sem.at[5]))
    for load in loads[:3]:
        load.start()

    barrier = pltpu.get_barrier_semaphore()
    for other in (zl, zr, zo):
        pl.semaphore_signal(barrier, inc=1, device_id=(d, other), device_id_type=MESH)

    x_line = [xs[i] + ys[0] + cs[0] for i in range(1, 4)]
    y_line = [xs[0] + ys[i] + cs[0] for i in range(1, 4)]
    twin = xs[0] + ys[0] + cs[1]
    for other in x_line + y_line + [twin]:
        pl.semaphore_signal(barrier, inc=1, device_id=(other, z), device_id_type=MESH)
    xn[pl.ds(0, TOK), :] = normalize(tok[...].astype(F32), lna[...].reshape(1, D)).astype(BF16)

    e0, e1 = eid[0:1, :], eid[1:2, :]
    ei = iota((NE, TOK), 0)
    named = jnp.where((ei == e0) | (ei == e1), 1.0, 0.0).astype(BF16)
    before = jnp.where(iota((TOK, TOK), 0) < iota((TOK, TOK), 1), 1.0, 0.0).astype(BF16)
    count = dot(named, before)
    chosen = []
    lines = [seg[...].astype(F32)]
    for e in (e0, e1):
        slot = jnp.sum(jnp.where(ei == e, count, 0.0), axis=0, keepdims=True).astype(I32)
        lines.append((e * FMSG + slot).astype(F32))
        odd = slot & 1
        pair = e * MSG + 3 * CAP + lax.shift_right_logical(slot, 1)
        chosen.append(
            (e * MSG + slot, jnp.where(odd == 0, pair, -1), jnp.where(odd == 1, pair, -1))
        )
    lines += [gate[0:1, :], gate[1:2, :]]
    ri = iota((8, TOK), 0)

    def stacked_lines(rows):
        total = jnp.zeros((8, TOK), F32)
        for n, row in enumerate(rows):
            total = jnp.where(ri == n, row, total)
        return total

    info[0] = stacked_lines(lines)
    pl.semaphore_wait(barrier, 10)

    def remote(src, dst, s_sem, r_sem, dev):
        return pltpu.make_async_remote_copy(
            src_ref=src, dst_ref=dst, send_sem=s_sem, recv_sem=r_sem,
            device_id=dev, device_id_type=MESH,
        )

    right, left, across = (d, zr), (d, zl), (d, zo)

    def xrows(slot, half):
        return xn.at[pl.ds(slot * TOK + half * 64, 64), :]

    seg_copies = [
        remote(info.at[0], info.at[1], ss_sem.at[0], sr_sem.at[0], right),
        remote(info.at[0], info.at[2], ss_sem.at[1], sr_sem.at[1], left),
        remote(info.at[0], info.at[3], ss_sem.at[2], sr_sem.at[2], across),
    ]
    r0 = remote(xrows(0, 0), xrows(1, 0), as_sem.at[0], ar_sem.at[0], right)
    r1 = remote(xrows(0, 1), xrows(1, 1), as_sem.at[1], ar_sem.at[1], right)
    l1 = remote(xrows(0, 1), xrows(2, 1), as_sem.at[2], ar_sem.at[2], left)
    l0 = remote(xrows(0, 0), xrows(2, 0), as_sem.at[3], ar_sem.at[3], left)
    ro = remote(xrows(1, 0), xrows(3, 0), as_sem.at[4], ar_sem.at[4], right)
    lo = remote(xrows(2, 1), xrows(3, 1), as_sem.at[5], ar_sem.at[5], left)
    r0.start()
    l1.start()
    r1.start()
    l0.start()
    for copy in seg_copies:
        copy.start()
    for load in loads[3:]:
        load.start()
    for other in x_line:
        pl.semaphore_signal(round_sem.at[0], inc=1, device_id=(other, z), device_id_type=MESH)

    def place(kind, cc):
        return chosen[kind][0] + CAP * cc if cc < 3 else chosen[kind][cc - 2]

    def make_g(i):
        rows = pl.ds(i * 256, 256)
        r = iota((256, TOK), 0) + i * 256
        for cc in range(NC):
            hit = (r == place(0, cc)) | (r == place(1, cc))
            g[rows, cc * TOK : (cc + 1) * TOK] = jnp.where(hit, 1.0, 0.0).astype(BF16)

    each(ALL // 256, make_g)

    def fixed(ref, q_dim, rows, first, base, msg):
        q = iota(ref.shape, q_dim)
        r = iota(ref.shape, 1 - q_dim) + base
        times, shift = {64: (1, 6), 80: (205, 14), CR: (1821, 18)}[rows]
        cc = lax.shift_right_logical(q * times, shift)
        i = q - cc * rows + first
        source = lax.shift_right_logical(i * 57, 9)
        slot = i - CAP * source
        at = source * msg + CAP * cc + slot
        if msg == MSG:
            pair = source * msg + 3 * CAP + lax.shift_right_logical(slot, 1)
            at = jnp.where(cc < 3, at, jnp.where((slot & 1) == cc - 3, pair, -1))
        ref[...] = jnp.where(r == at, 1.0, 0.0).astype(BF16)

    fixed(unp0, 0, 64, 0, 0, MSG)
    fixed(unp1, 0, 80, 64, 7 * MSG, MSG)

    r0.wait_recv()
    ro.start()
    l1.wait_recv()
    lo.start()

    pl.semaphore_wait(round_sem.at[0], 3)
    pl.semaphore_signal(round_sem.at[1], inc=1, device_id=(twin, z), device_id_type=MESH)

    for load in loads[:3]:
        load.wait()

    def own_q(j):
        q[:, cols(j)] = dot(xn[pl.ds(0, TOK), :], wqkv[:, cols(j)]).astype(BF16)

    each(NC, own_q)

    def keys_values(first, number):
        rows = pl.ds(first, number)

        def step(j):
            k[rows, cols(j)] = dot(xn[rows, :], wqkv[:, cols(j + NC)]).astype(BF16)
            v[rows, cols(j)] = dot(xn[rows, :], wqkv[:, cols(j + 2 * NC)]).astype(BF16)

        each(NC, step)

    keys_values(0, TOK)
    fixed(pkm0, 1, 80, 0, 0, MSG)
    fixed(pkm1, 1, 80, 64, GM, MSG)
    fixed(unf, 0, CR, 0, 0, FMSG)
    fixed(pkf, 1, CR, 0, 0, FMSG)

    r1.wait_recv()
    l0.wait_recv()
    keys_values(TOK, 2 * TOK)

    for copy in seg_copies:
        copy.wait_recv()
    eight = iota((8, TOK), 0).astype(F32)
    kinds = [jnp.where(eight == info[s, 0:1, :], 1.0, 0.0).astype(BF16) for s in range(4)]
    key_kind = jnp.concatenate(kinds, axis=1)
    same = lax.dot_general(kinds[0], key_kind, (((0,), (0,)), ((), ())), preferred_element_type=F32)
    bias = jnp.where(same > 0.5, 0.0, NEG)

    for s in range(4):
        more = jnp.zeros((8, TOK), F32)
        if s == 0:
            more = stacked_lines([row.astype(F32) for kind in chosen for row in kind])
        square = jnp.concatenate([info[s], more, jnp.zeros((TOK - 16, TOK), F32)], axis=0)
        gcol[s] = jnp.transpose(square)
        r = iota((ALLF, TOK), 0) - CAP * s
        f0, f1 = info[s, 1:2, :].astype(I32), info[s, 2:3, :].astype(I32)
        gf[:, s * TOK : (s + 1) * TOK] = jnp.where((r == f0) | (r == f1), 1.0, 0.0).astype(BF16)

    ro.wait_recv()
    lo.wait_recv()
    keys_values(3 * TOK, TOK)

    scale = HEAD ** (-0.5)
    ctx[...] = jnp.zeros((TOK, D), F32)
    for half in range(2):
        for heads, at in GROUPS:
            window = pl.ds(half * 640 + at, COL)
            lane = iota((TOK, COL), 1) + at
            masks = [(lane >= h * HEAD) & (lane < (h + 1) * HEAD) for h in heads]
            qw = q[:, window]
            zero = jnp.zeros_like(qw)
            stacked = jnp.concatenate([jnp.where(m, qw, zero) for m in masks], axis=0)
            scores = lax.dot_general(
                stacked, k[:, window], (((1,), (1,)), ((), ())), preferred_element_type=F32
            )
            probs, sums = [], []
            for n in range(len(heads)):
                s = scores[n * TOK : (n + 1) * TOK, :] * scale + bias
                w = jnp.exp(s - jnp.max(s, axis=-1, keepdims=True))
                sums.append(jnp.sum(w, axis=-1, keepdims=True))
                probs.append(w.astype(BF16))
            mixed = dot(jnp.concatenate(probs, axis=0), v[:, window])
            total = ctx[:, window]
            for n, m in enumerate(masks):
                total = jnp.where(m, mixed[n * TOK : (n + 1) * TOK, :] / sums[n], total)
            ctx[:, window] = total
    ctxb[...] = ctx[...].astype(BF16)

    loads[3].wait()

    def project(j):
        mid[:, cols(j)] = tok[:, cols(j)].astype(F32) + dot(ctxb[...], wao[:, cols(j)])

    each(NC, project)
    expert_in = normalize(mid[...], lne[...].reshape(1, D)).astype(BF16)
    zx[pl.ds(0, TOK), :] = expert_in[:, PW:]

    def zrows(slot, half):
        return zx.at[pl.ds(slot * TOK + half * 64, 64), :]

    xr0 = remote(zrows(0, 0), zrows(1, 0), xs_sem.at[0], xr_sem.at[0], right)
    xr1 = remote(zrows(0, 1), zrows(1, 1), xs_sem.at[1], xr_sem.at[1], right)
    xl1 = remote(zrows(0, 1), zrows(2, 1), xs_sem.at[2], xr_sem.at[2], left)
    xl0 = remote(zrows(0, 0), zrows(2, 0), xs_sem.at[3], xr_sem.at[3], left)
    xro = remote(zrows(1, 0), zrows(3, 0), xs_sem.at[4], xr_sem.at[4], right)
    xlo = remote(zrows(2, 1), zrows(3, 1), xs_sem.at[5], xr_sem.at[5], left)
    ring = [xr0, xr1, xl1, xl0, xro, xlo]
    for copy in ring[:4]:
        copy.start()

    for cc in range(3):
        xp[pl.ds(cc * TOK, TOK), :] = expert_in[:, cc * COL : (cc + 1) * COL]
    rest = expert_in[:, 3 * COL : PW]
    none = jnp.zeros_like(rest)
    xp[pl.ds(3 * TOK, TOK), :] = jnp.concatenate([rest, none], axis=1)
    xp[pl.ds(4 * TOK, TOK), :] = jnp.concatenate([none, rest], axis=1)

    def fill(i):
        rows = pl.ds(i * 256, 256)
        send[rows, :] = dot(g[rows, :], xp[...]).astype(BF16)

    each(ALL // 256, fill)

    pl.semaphore_wait(round_sem.at[1], 1)
    for n in range(NE - 1):
        dest = shifted(n, 1)
        remote(
            send.at[rows_of(dest), :], rcv.at[rows_of(n), :], ds_sem, dr_sem.at[n // GS], (dest, z)
        ).start()
    rcv[pl.ds((NE - 1) * MSG, MSG), :] = send[rows_of(d), :]

    def piece_of(slot, half, n):
        first, number = OUT[n]
        return a.at[slot, half, pl.ds(first, number), pl.ds(0, PW)]

    def arrived(group):
        number = GS if group < 3 else GS - 1
        got = rcv.at[pl.ds(group * GM, number * MSG), :]
        remote(got, got, ds_sem, dr_sem.at[group], right).wait_recv()

    def unpack(half, n):
        first, number = OUT[n]
        arrived(2 * half + n)
        base = half * 2 * GM
        if n == 0:
            got = dot(unp0[...], rcv[pl.ds(base, GM), :])
        else:
            got = dot(unp1[...], rcv[pl.ds(base + 7 * MSG, 9 * MSG), :])
        rows = slice(first, first + number)
        for cc in range(3):
            a[0, half, rows, cc * COL : (cc + 1) * COL] = got[
                cc * number : (cc + 1) * number
            ].astype(BF16)
        a[0, half, rows, 3 * COL : PW] = (
            got[3 * number : 4 * number, :128] + got[4 * number :, 128:]
        ).astype(BF16)

    zc = {}
    for half in range(2):
        for n in range(2):
            m = 2 * half + n
            zc["r", half, n] = remote(
                piece_of(0, half, n), piece_of(1, half, n), zs_sem.at[m], zr_sem.at[m], right
            )
            zc["l", half, n] = remote(
                piece_of(0, half, n), piece_of(2, half, n), zs_sem.at[4 + m], zr_sem.at[4 + m], left
            )
    for n in range(2):
        zc["ro", n] = remote(
            piece_of(1, 0, n), piece_of(3, 0, n), zs_sem.at[8 + n], zr_sem.at[8 + n], right
        )
        zc["lo", n] = remote(
            piece_of(2, 1, n), piece_of(3, 1, n), zs_sem.at[10 + n], zr_sem.at[10 + n], left
        )

    def expert(slot, half, store):
        def first(j):
            hid[:, cols(j)] = gelu(dot(a[slot, half], win[:, cols(j)])).astype(BF16)

        each(NC, first)
        for j in range(3):
            store(cols(j), dot(hid[...], wout[:, cols(j)]))
        value = dot(hid[...], wout[:, 3 * COL :])
        store(pl.ds(3 * COL, 128), value[:, :128])
        frst[half, pl.ds(slot * CR, CR), :] = value[:, 128:].astype(BF16)

    def into_own(half):
        def store(at, value):
            own[half, :, at] = value

        return store

    def into_part(n):
        def store(at, value):
            part[n, :, at] = value.astype(BF16)

        return store

    def into_keep(n):
        def store(at, value):
            keep[n, :, at] = value

        return store

    def back_of(ref, slot, n):
        first, number = BACK[n]
        return ref.at[slot, pl.ds(first, number)]

    b_left0 = remote(part.at[0], back.at[2], bs_sem.at[0], br_sem.at[0], left)
    b_right1 = remote(part.at[1], back.at[1], bs_sem.at[1], br_sem.at[1], right)
    bc = {}
    for n in range(2):
        for m, (key, src, dst, at, dev) in enumerate(
            (
                ("across0", 2, stage, 0, right),
                ("across1", 3, stage, 1, left),
                ("right0", 4, back, 0, right),
                ("left1", 5, back, 3, left),
            )
        ):
            bc[key, n] = remote(
                back_of(part, src, n), back_of(dst, at, n),
                bs_sem.at[2 + 2 * m + n], br_sem.at[2 + 2 * m + n], dev,
            )

    loads[4].wait()
    loads[5].wait()

    xr0.wait_recv()
    xro.start()
    xl1.wait_recv()
    xlo.start()
    for n in range(2):
        unpack(0, n)
        zc["r", 0, n].start()
        zc["l", 0, n].start()
    for copy in (xr1, xl0, xro, xlo):
        copy.wait_recv()
    for i in range(ALLF // 256):
        rows = pl.ds(i * 256, 256)
        fsend[rows, :] = dot(gf[rows, :], zx[...]).astype(BF16)
    for n in range(NE - 1):
        dest = shifted(n, 1)
        remote(
            fsend.at[frows_of(dest), :], frcv.at[frows_of(n), :],
            fds_sem, fdr_sem.at[n // HALF], (dest, z),
        ).start()
    frcv[pl.ds((NE - 1) * FMSG, FMSG), :] = fsend[frows_of(d), :]
    for n in range(2):
        unpack(1, n)
        zc["r", 1, n].start()
        zc["l", 1, n].start()

    ri = iota((TOK, ALL), 1)
    for cc in range(NC):
        line = 8 if cc < 3 else 6 + cc
        for kind in range(2):
            at = gcol[0, :, line + 3 * kind : line + 3 * kind + 1].astype(I32)
            at = at + CAP * cc if cc < 3 else at
            pick[pl.ds(cc * 256 + kind * TOK, TOK), :] = jnp.where(ri == at, 1.0, 0.0).astype(BF16)
    for n in range(2):
        zc["r", 0, n].wait_recv()
        zc["ro", n].start()
    fi = iota((TOK, ALLF), 1)
    for s in range(4):
        for kind in range(2):
            at = gcol[s, :, 1 + kind : 2 + kind].astype(I32) + CAP * s
            fpick[pl.ds(s * 256 + kind * TOK, TOK), :] = jnp.where(fi == at, 1.0, 0.0).astype(BF16)
    for n in range(2):
        zc["l", 1, n].wait_recv()
        zc["lo", n].start()

    def funpack(half):
        number = HALF if half == 0 else HALF - 1
        got = frcv.at[pl.ds(half * HALF * FMSG, number * FMSG), :]
        remote(got, got, fds_sem, fdr_sem.at[half], right).wait_recv()
        rows = dot(unf[...], frcv[pl.ds(half * HALF * FMSG, HALF * FMSG), :]).astype(BF16)
        for s in range(4):
            a[s, half, :, PW:] = rows[s * CR : (s + 1) * CR]

    def freturn(half):
        fpack[pl.ds(half * HALF * FMSG, HALF * FMSG), :] = dot(pkf[...], frst[half]).astype(BF16)
        for m in range(half * HALF, min((half + 1) * HALF, NE - 1)):
            dest = shifted(m, -1)
            remote(
                fpack.at[frows_of(m), :], fret.at[frows_of(d), :], fes_sem, fer_sem, (dest, z)
            ).start()

    funpack(0)
    expert(1, 0, into_part(0))
    b_left0.start()
    for n in range(2):
        zc["l", 0, n].wait_recv()
    expert(2, 0, into_keep(0))
    expert(0, 0, into_own(0))
    for n in range(2):
        zc["ro", n].wait_recv()
    expert(3, 0, into_part(2))
    bc["across0", 0].start()
    bc["across0", 1].start()
    freturn(0)
    for n in range(2):
        zc["r", 1, n].wait_recv()
        zc["lo", n].wait_recv()
    funpack(1)
    expert(3, 1, into_part(3))
    bc["across1", 0].start()
    bc["across1", 1].start()
    expert(2, 1, into_part(1))
    b_right1.start()
    expert(1, 1, into_keep(1))
    expert(0, 1, into_own(1))
    freturn(1)
    fret[frows_of(d), :] = fpack[pl.ds((NE - 1) * FMSG, FMSG), :]
    for n in range(2):
        first, number = BACK[n]
        rows = pl.ds(first, number)
        bc["across0", n].wait_recv()
        part[4, rows] = (keep[0, rows] + stage[0, rows].astype(F32)).astype(BF16)
        bc["right0", n].start()
        bc["across1", n].wait_recv()
        part[5, rows] = (keep[1, rows] + stage[1, rows].astype(F32)).astype(BF16)
        bc["left1", n].start()

    def half_of(ref, slot, n):
        return ref.at[slot, pl.ds(n * 64, 64)]

    ya0 = remote(half_of(fout, 3, 0), fstage.at[0], ys_sem.at[0], yr_sem.at[0], right)
    ya1 = remote(half_of(fout, 3, 1), fstage.at[1], ys_sem.at[1], yr_sem.at[1], left)
    yl0 = remote(half_of(fout, 1, 0), half_of(fback, 1, 0), ys_sem.at[2], yr_sem.at[2], left)
    yr1 = remote(half_of(fout, 2, 1), half_of(fback, 0, 1), ys_sem.at[3], yr_sem.at[3], right)
    yr0 = remote(half_of(fout, 2, 0), half_of(fback, 0, 0), ys_sem.at[4], yr_sem.at[4], right)
    yl1 = remote(half_of(fout, 1, 1), half_of(fback, 1, 1), ys_sem.at[5], yr_sem.at[5], left)
    ring += [ya0, ya1, yl0, yr1, yr0, yl1]

    b_left0.wait_recv()
    b_right1.wait_recv()
    def finish(n):
        first, number = BACK[n]
        rows = pl.ds(first, number)
        for half in range(2):
            bc["right0" if half == 0 else "left1", n].wait_recv()
            for cc in range(4):
                at = slice(cc * COL, min((cc + 1) * COL, PW))
                full = (
                    own[half, rows, at]
                    + back[half, rows, at].astype(F32)
                    + back[2 + half, rows, at].astype(F32)
                ).astype(BF16)
                both = [full]
                if cc == 3:
                    none = jnp.zeros_like(full)
                    both = [
                        jnp.concatenate([full, none], axis=1),
                        jnp.concatenate([none, full], axis=1),
                    ]
                for m, value in enumerate(both):
                    if n == 0:
                        rst[half, 0, pl.ds((cc + m) * 80, 80), :] = value
                        rst[half, 1, pl.ds((cc + m) * 80, 16), :] = value[64:]
                    else:
                        rst[half, 1, pl.ds((cc + m) * 80 + 16, 64), :] = value
            packed = dot((pkm0 if n == 0 else pkm1)[...], rst[half, n])
            group = 2 * half + n
            pack[pl.ds(group * GM, GM), :] = packed.astype(BF16)
            for m in range(group * GS, min((group + 1) * GS, NE - 1)):
                dest = shifted(m, -1)
                remote(
                    pack.at[rows_of(m), :], ret.at[rows_of(d), :], es_sem, er_sem, (dest, z)
                ).start()
    finish(0)

    others = fret.at[pl.ds(0, (NE - 1) * FMSG), :]
    remote(others, others, fes_sem, fer_sem, right).wait_recv()
    for s in (3, 1, 2, 0):
        both = dot(fpick[pl.ds(s * 256, 256), :], fret[...])
        sums = gcol[s, :, 3:4] * both[:TOK] + gcol[s, :, 4:5] * both[TOK:]
        if s == 0:
            fown[...] = sums
        else:
            fpart[s] = sums
            for n in range(2):
                rows = pl.ds(n * 64, 64)
                fout[s, rows] = sums[n * 64 : (n + 1) * 64].astype(BF16)
        if s == 3:
            ya0.start()
            ya1.start()
        if s == 1:
            yl0.start()
        if s == 2:
            yr1.start()

    finish(1)
    ret[rows_of(d), :] = pack[pl.ds((NE - 1) * MSG, MSG), :]

    ya0.wait_recv()
    fout[2, pl.ds(0, 64)] = (fpart[2, pl.ds(0, 64)] + fstage[0].astype(F32)).astype(BF16)
    yr0.start()
    ya1.wait_recv()
    fout[1, pl.ds(64, 64)] = (fpart[1, pl.ds(64, 64)] + fstage[1].astype(F32)).astype(BF16)
    yl1.start()

    others = ret.at[pl.ds(0, (NE - 1) * MSG), :]
    remote(others, others, es_sem, er_sem, right).wait_recv()
    g0, g1 = gcol[0, :, 3:4], gcol[0, :, 4:5]
    for cc in range(3):
        both = dot(pick[pl.ds(cc * 256, 256), :], ret[...])
        out[:, cols(cc)] = (mid[:, cols(cc)] + g0 * both[:TOK] + g1 * both[TOK:]).astype(BF16)
    even = dot(pick[pl.ds(3 * 256, 256), :], ret[...])[:, :128]
    both = even + dot(pick[pl.ds(4 * 256, 256), :], ret[...])[:, 128:]
    out[:, 3 * COL : PW] = (
        mid[:, 3 * COL : PW] + g0 * both[:TOK] + g1 * both[TOK:]
    ).astype(BF16)
    for copy in (yl0, yr1, yr0, yl1):
        copy.wait_recv()
    out[:, PW:] = (
        mid[:, PW:] + fown[...] + fback[0].astype(F32) + fback[1].astype(F32)
    ).astype(BF16)

    for copy in seg_copies + [r0, r1, l0, l1, ro, lo] + ring + list(zc.values()):
        copy.wait_send()
    for copy in [b_left0, b_right1] + list(bc.values()):
        copy.wait_send()
    gone = send.at[pl.ds(0, (NE - 1) * MSG), :]
    remote(gone, gone, ds_sem, dr_sem.at[0], right).wait_send()
    gone = pack.at[pl.ds(0, (NE - 1) * MSG), :]
    remote(gone, gone, es_sem, er_sem, right).wait_send()
    gone = fsend.at[pl.ds(0, (NE - 1) * FMSG), :]
    remote(gone, gone, fds_sem, fdr_sem.at[0], right).wait_send()
    gone = fpack.at[pl.ds(0, (NE - 1) * FMSG), :]
    remote(gone, gone, fes_sem, fer_sem, right).wait_send()


def layer(tok, seg, eid, gate, lna, lne, wqkv, wao, win, wout):
    vm = pl.BlockSpec(memory_space=pltpu.VMEM)
    hbm = pl.BlockSpec(memory_space=pl.ANY)
    V = pltpu.VMEM
    dma = pltpu.SemaphoreType.DMA
    return pl.pallas_call(
        kernel,
        out_shape=jax.ShapeDtypeStruct((TOK, D), BF16),
        in_specs=[vm] * 6 + [hbm] * 4,
        out_specs=vm,
        scratch_shapes=[
            V((D, 3 * D), BF16),
            V((D, D), BF16),
            V((D, D), BF16),
            V((D, D), BF16),
            V((4 * TOK, D), BF16),
            V((4, 8, TOK), F32),
            V((TOK, D), BF16),
            V((4 * TOK, D), BF16),
            V((4 * TOK, D), BF16),
            V((TOK, D), F32),
            V((TOK, D), BF16),
            V((TOK, D), F32),
            V((NC * TOK, COL), BF16),
            V((ALL, NC * TOK), BF16),
            V((ALL, COL), BF16),
            V((ALL, COL), BF16),
            V((4, 2, CR, D), BF16),
            V((CR, D), BF16),
            V((6, CR, PW), BF16),
            V((2, CR, PW), F32),
            V((2, CR, PW), F32),
            V((2, CR, PW), BF16),
            V((4, CR, PW), BF16),
            V((2, 2, NC * 80, COL), BF16),
            V((ALL, COL), BF16),
            V((ALL, COL), BF16),
            V((NC * 64, GM), BF16),
            V((NC * 80, 9 * MSG), BF16),
            V((GM, NC * 80), BF16),
            V((GM, NC * 80), BF16),
            V((4, TOK, TOK), F32),
            V((4 * TOK, FW), BF16),
            V((ALLF, 4 * TOK), BF16),
            V((ALLF, FW), BF16),
            V((ALLF, FW), BF16),
            V((4 * CR, HALF * FMSG), BF16),
            V((HALF * FMSG, 4 * CR), BF16),
            V((2, 4 * CR, FW), BF16),
            V((ALLF, FW), BF16),
            V((ALLF, FW), BF16),
            V((4, TOK, FW), F32),
            V((4, TOK, FW), BF16),
            V((TOK, FW), F32),
            V((2, 64, FW), BF16),
            V((2, TOK, FW), BF16),
            dma((6,)),
            dma((6,)),
            dma((6,)),
            dma((3,)),
            dma((3,)),
            dma,
            dma((4,)),
            dma((12,)),
            dma((12,)),
            dma((10,)),
            dma((10,)),
            dma,
            dma,
            pltpu.SemaphoreType.REGULAR((2,)),
            dma((6,)),
            dma((6,)),
            dma,
            dma((2,)),
            dma,
            dma,
            dma((6,)),
            dma((6,)),
        ],
        compiler_params=pltpu.CompilerParams(
            collective_id=0, has_side_effects=True, vmem_limit_bytes=50 * 1024 * 1024
        ),
        cost_estimate=pl.CostEstimate(
            flops=14_000_000_000, bytes_accessed=24_000_000, transcendentals=3_000_000
        ),
    )(tok, seg, eid, gate, lna, lne, wqkv, wao, win, wout)


def body(
    tokens, segment_ids, expert_ids, gate_values, ln_attn, w_qkv, w_attn_out, ln_expert, w_in, w_out
):
    out = layer(
        tokens[0],
        segment_ids,
        expert_ids[0].T,
        gate_values[0].T,
        ln_attn,
        ln_expert,
        w_qkv,
        w_attn_out,
        w_in[0],
        w_out[0],
    )
    return out[None]


def solution(mesh):
    placed = (
        P("dp", "seq", None),
        P("dp", "seq"),
        P("dp", "seq", None),
        P("dp", "seq", None),
        P(),
        P(),
        P(),
        P(),
        P("dp", None, "seq"),
        P("dp", "seq", None),
    )
    return jax.shard_map(
        body, mesh=mesh, in_specs=placed, out_specs=P("dp", "seq", None), check_vma=False
    )
```

```python
import functools

import jax
import jax.numpy as jnp
from jax import lax
from jax.experimental import pallas as pl
from jax.experimental.pallas import tpu as pltpu
from jax.sharding import PartitionSpec as P

F32 = jnp.float32
BF16 = jnp.bfloat16
I32 = jnp.int32
MESH = pl.DeviceIdType.MESH

D = 1280
HEADS = 16
HEAD = 80
TOK = 128
CAP = 9
NE = 32
COL = 256
NC = D // COL
PW = 896
FW = D - PW
MSG = 32
FMSG = 48
HALF = 16
CR = HALF * CAP
GS = 8
GM = GS * MSG
FGM = GS * FMSG
ALLF = NE * FMSG
ALL = NE * MSG
EPS = 1e-06
NEG = -1e30

GROUPS = (((0, 1, 2), 0), ((3,), 128), ((4, 5), 256), ((6, 7), 384))


OFFSETS = sorted(
    [(dx, dy, dc) for dx in range(4) for dy in range(4) for dc in range(2)],
    key=lambda o: -(min(o[0], 4 - o[0]) + min(o[1], 4 - o[1]) + 0.5 * o[2]),
)

OUT = ((0, 64), (64, 80))
BACK = ((0, 80), (80, 64))


def normalize(rows, gain):
    mean = jnp.mean(rows, axis=-1, keepdims=True)
    centered = rows - mean
    spread = jnp.mean(centered * centered, axis=-1, keepdims=True)
    return centered * lax.rsqrt(spread + EPS) * gain


def gelu(x):
    return 0.5 * x * (1.0 + jnp.tanh(0.7978845608028654 * (x + 0.044715 * (x * x * x))))


def iota(shape, dim):
    return lax.broadcasted_iota(I32, shape, dim)


def dot(a, b):
    return jnp.dot(a, b, preferred_element_type=F32)


def cols(j):
    return pl.ds(j * COL, COL)


def each(number, step):
    for i in range(number):
        step(i)


def kernel(
    tok_h, seg_h, eid_h, gate_h, lna_h, lne_h, wqkv_h, wao_h, win_h, wout_h, out,
    tok, seg, eid, gate, lna, lne, wqkv, wao, win, wout, xn, xraw, info, q, k, v, ctx, ctxb, mid, xp, g, send, rcv, a, hid,
    part, keep, own, stage, back, rst, pack, ret, unp0, unp1, pkm0, pkm1, gcol,
    zx, gf, fsend, frcv, unf, pkf, frst, fpack, fret, fpart, fout, fown, fstage, fback,
    i_sem, w_sem, as_sem, ar_sem, ss_sem, sr_sem, ds_sem, dr_sem, zs_sem, zr_sem, bs_sem, br_sem,
    es_sem, er_sem, round_sem, xs_sem, xr_sem, fds_sem, fdr_sem, fes_sem, fer_sem, ys_sem, yr_sem,
):
    pick = wqkv.at[:, pl.ds(0, ALL)]
    fpick = wqkv.at[pl.ds(0, 4 * 256), pl.ds(ALL, ALLF)]
    d = lax.axis_index("dp")
    z = lax.axis_index("seq")
    zl = lax.rem(z + 3, 4)
    zr = lax.rem(z + 1, 4)
    zo = lax.rem(z + 2, 4)
    x, y, c = d // 8, lax.rem(d // 2, 4), lax.rem(d, 2)

    xs = [lax.rem(x + i, 4) * 8 for i in range(4)]
    ys = [lax.rem(y + i, 4) * 2 for i in range(4)]
    cs = [c, 1 - c]

    def shifted(n, sign):
        dx, dy, dc = OFFSETS[n]
        return xs[sign * dx % 4] + ys[sign * dy % 4] + cs[dc]

    def rows_of(j):
        return pl.ds(pl.multiple_of(j * MSG, MSG), MSG)

    def frows_of(j):
        return pl.ds(pl.multiple_of(j * FMSG, FMSG), FMSG)

    small = [(tok_h, tok), (lna_h, lna), (eid_h, eid), (seg_h, seg), (gate_h, gate), (lne_h, lne)]
    small = [pltpu.make_async_copy(src, dst, i_sem.at[n]) for n, (src, dst) in enumerate(small)]
    for copy in small:
        copy.start()
    loads = []
    for i in range(3):
        part_of = pl.ds(i * D, D)
        loads.append(pltpu.make_async_copy(wqkv_h.at[:, part_of], wqkv.at[:, part_of], w_sem.at[i]))
    loads.append(pltpu.make_async_copy(wao_h, wao, w_sem.at[3]))
    loads.append(pltpu.make_async_copy(win_h, win, w_sem.at[4]))
    loads.append(pltpu.make_async_copy(wout_h, wout, w_sem.at[5]))
    barrier = pltpu.get_barrier_semaphore()
    for other in (zl, zr, zo):
        pl.semaphore_signal(barrier, inc=1, device_id=(d, other), device_id_type=MESH)

    x_line = [xs[i] + ys[0] + cs[0] for i in range(1, 4)]
    y_line = [xs[0] + ys[i] + cs[0] for i in range(1, 4)]
    twin = xs[0] + ys[0] + cs[1]
    for other in x_line + y_line + [twin]:
        pl.semaphore_signal(barrier, inc=1, device_id=(other, z), device_id_type=MESH)

    pl.semaphore_wait(barrier, 10)

    def remote(src, dst, s_sem, r_sem, dev):
        return pltpu.make_async_remote_copy(
            src_ref=src, dst_ref=dst, send_sem=s_sem, recv_sem=r_sem,
            device_id=dev, device_id_type=MESH,
        )

    right, left, across = (d, zr), (d, zl), (d, zo)

    def xrows(slot, half):
        rows = pl.ds(slot * TOK + half * 64, 64)
        return tok_h.at[pl.ds(half * 64, 64), :] if slot == 0 else xraw.at[rows, :]

    seg_copies = [
        remote(info.at[0], info.at[1], ss_sem.at[0], sr_sem.at[0], right),
        remote(info.at[0], info.at[2], ss_sem.at[1], sr_sem.at[1], left),
        remote(info.at[0], info.at[3], ss_sem.at[2], sr_sem.at[2], across),
    ]
    r0 = remote(xrows(0, 0), xrows(1, 0), as_sem.at[0], ar_sem.at[0], right)
    r1 = remote(xrows(0, 1), xrows(1, 1), as_sem.at[1], ar_sem.at[1], right)
    l1 = remote(xrows(0, 1), xrows(2, 1), as_sem.at[2], ar_sem.at[2], left)
    l0 = remote(xrows(0, 0), xrows(2, 0), as_sem.at[3], ar_sem.at[3], left)
    ro = remote(xrows(1, 0), xrows(3, 0), as_sem.at[4], ar_sem.at[4], right)
    lo = remote(xrows(2, 1), xrows(3, 1), as_sem.at[5], ar_sem.at[5], left)
    r0.start()
    l1.start()
    r1.start()
    l0.start()
    for load in loads:
        load.start()
    for copy in small:
        copy.wait()

    e0, e1 = eid[0:1, :], eid[1:2, :]
    ei = iota((NE, TOK), 0)
    named = jnp.where((ei == e0) | (ei == e1), 1.0, 0.0).astype(BF16)
    before = jnp.where(iota((TOK, TOK), 0) < iota((TOK, TOK), 1), 1.0, 0.0).astype(BF16)
    count = dot(named, before)
    chosen = []
    lines = [seg[...].astype(F32)]
    for e in (e0, e1):
        slot = jnp.sum(jnp.where(ei == e, count, 0.0), axis=0, keepdims=True).astype(I32)
        lines.append((e * FMSG + slot).astype(F32))
        odd = slot & 1
        pair = e * MSG + 3 * CAP + lax.shift_right_logical(slot, 1)
        chosen.append(
            (e * MSG + slot, jnp.where(odd == 0, pair, -1), jnp.where(odd == 1, pair, -1))
        )
    lines += [gate[0:1, :], gate[1:2, :]]
    ri = iota((8, TOK), 0)

    def stacked_lines(rows):
        total = jnp.zeros((8, TOK), F32)
        for n, row in enumerate(rows):
            total = jnp.where(ri == n, row, total)
        return total

    info[0] = stacked_lines(lines)
    for copy in seg_copies:
        copy.start()
    xn[pl.ds(0, TOK), :] = normalize(tok[...].astype(F32), lna[...].reshape(1, D)).astype(BF16)

    for other in x_line:
        pl.semaphore_signal(round_sem.at[0], inc=1, device_id=(other, z), device_id_type=MESH)

    def place(kind, cc):
        return chosen[kind][0] + CAP * cc if cc < 3 else chosen[kind][cc - 2]

    def make_g(i):
        rows = pl.ds(i * 256, 256)
        r = iota((256, TOK), 0) + i * 256
        for cc in range(NC):
            hit = (r == place(0, cc)) | (r == place(1, cc))
            g[rows, cc * TOK : (cc + 1) * TOK] = jnp.where(hit, 1.0, 0.0).astype(BF16)

    each(ALL // 256, make_g)

    def fixed(ref, q_dim, rows, first, base, msg):
        q = iota(ref.shape, q_dim)
        r = iota(ref.shape, 1 - q_dim) + base
        times, shift = {64: (1, 6), 80: (205, 14), CR: (1821, 18)}[rows]
        cc = lax.shift_right_logical(q * times, shift)
        i = q - cc * rows + first
        source = lax.shift_right_logical(i * 57, 9)
        slot = i - CAP * source
        at = source * msg + CAP * cc + slot
        if msg == MSG:
            pair = source * msg + 3 * CAP + lax.shift_right_logical(slot, 1)
            at = jnp.where(cc < 3, at, jnp.where((slot & 1) == cc - 3, pair, -1))
        ref[...] = jnp.where(r == at, 1.0, 0.0).astype(BF16)

    fixed(unp0, 0, 64, 0, 0, MSG)
    fixed(unp1, 0, 80, 64, 7 * MSG, MSG)

    r0.wait_recv()
    ro.start()
    l1.wait_recv()
    lo.start()

    pl.semaphore_wait(round_sem.at[0], 3)
    pl.semaphore_signal(round_sem.at[1], inc=1, device_id=(twin, z), device_id_type=MESH)

    for load in loads[:3]:
        load.wait()

    def own_q(j):
        q[:, cols(j)] = dot(xn[pl.ds(0, TOK), :], wqkv[:, cols(j)]).astype(BF16)

    each(NC, own_q)

    def keys_values(first, number):
        rows = pl.ds(first, number)
        if first:
            xn[rows, :] = normalize(xraw[rows, :].astype(F32), lna[...].reshape(1, D)).astype(BF16)

        def step(j):
            k[rows, cols(j)] = dot(xn[rows, :], wqkv[:, cols(j + NC)]).astype(BF16)
            v[rows, cols(j)] = dot(xn[rows, :], wqkv[:, cols(j + 2 * NC)]).astype(BF16)

        each(NC, step)

    keys_values(0, TOK)
    fixed(pkm0, 1, 80, 0, 0, MSG)
    fixed(pkm1, 1, 80, 64, GM, MSG)
    fixed(unf, 0, CR, 0, 0, FMSG)
    fixed(pkf, 1, CR, 0, 0, FMSG)

    r1.wait_recv()
    l0.wait_recv()
    keys_values(TOK, 2 * TOK)

    for copy in seg_copies:
        copy.wait_recv()
    eight = iota((8, TOK), 0).astype(F32)
    kinds = [jnp.where(eight == info[s, 0:1, :], 1.0, 0.0).astype(BF16) for s in range(4)]
    key_kind = jnp.concatenate(kinds, axis=1)
    same = lax.dot_general(kinds[0], key_kind, (((0,), (0,)), ((), ())), preferred_element_type=F32)
    bias = jnp.where(same > 0.5, 0.0, NEG)

    for s in range(4):
        more = jnp.zeros((8, TOK), F32)
        if s == 0:
            more = stacked_lines([row.astype(F32) for kind in chosen for row in kind])
        square = jnp.concatenate([info[s], more, jnp.zeros((TOK - 16, TOK), F32)], axis=0)
        gcol[s] = jnp.transpose(square)
        r = iota((ALLF, TOK), 0) - CAP * s
        f0, f1 = info[s, 1:2, :].astype(I32), info[s, 2:3, :].astype(I32)
        gf[:, s * TOK : (s + 1) * TOK] = jnp.where((r == f0) | (r == f1), 1.0, 0.0).astype(BF16)

    ro.wait_recv()
    lo.wait_recv()
    keys_values(3 * TOK, TOK)

    scale = HEAD ** (-0.5)
    ctx[...] = jnp.zeros((TOK, D), F32)
    for half in range(2):
        for heads, at in GROUPS:
            window = pl.ds(half * 640 + at, COL)
            lane = iota((TOK, COL), 1) + at
            masks = [(lane >= h * HEAD) & (lane < (h + 1) * HEAD) for h in heads]
            qw = q[:, window]
            zero = jnp.zeros_like(qw)
            stacked = jnp.concatenate([jnp.where(m, qw, zero) for m in masks], axis=0)
            scores = lax.dot_general(
                stacked, k[:, window], (((1,), (1,)), ((), ())), preferred_element_type=F32
            )
            probs, sums = [], []
            for n in range(len(heads)):
                s = scores[n * TOK : (n + 1) * TOK, :] * scale + bias
                w = jnp.exp(s - jnp.max(s, axis=-1, keepdims=True))
                sums.append(jnp.sum(w, axis=-1, keepdims=True))
                probs.append(w.astype(BF16))
            mixed = dot(jnp.concatenate(probs, axis=0), v[:, window])
            total = ctx[:, window]
            for n, m in enumerate(masks):
                total = jnp.where(m, mixed[n * TOK : (n + 1) * TOK, :] / sums[n], total)
            ctx[:, window] = total
    ctxb[...] = ctx[...].astype(BF16)

    loads[3].wait()

    def project(j):
        mid[:, cols(j)] = tok[:, cols(j)].astype(F32) + dot(ctxb[...], wao[:, cols(j)])

    each(NC, project)
    expert_in = normalize(mid[...], lne[...].reshape(1, D)).astype(BF16)
    zx[pl.ds(0, TOK), :] = expert_in[:, PW:]

    def zrows(slot, half):
        return zx.at[pl.ds(slot * TOK + half * 64, 64), :]

    xr0 = remote(zrows(0, 0), zrows(1, 0), xs_sem.at[0], xr_sem.at[0], right)
    xr1 = remote(zrows(0, 1), zrows(1, 1), xs_sem.at[1], xr_sem.at[1], right)
    xl1 = remote(zrows(0, 1), zrows(2, 1), xs_sem.at[2], xr_sem.at[2], left)
    xl0 = remote(zrows(0, 0), zrows(2, 0), xs_sem.at[3], xr_sem.at[3], left)
    xro = remote(zrows(1, 0), zrows(3, 0), xs_sem.at[4], xr_sem.at[4], right)
    xlo = remote(zrows(2, 1), zrows(3, 1), xs_sem.at[5], xr_sem.at[5], left)
    ring = [xr0, xr1, xl1, xl0, xro, xlo]
    for copy in ring[:4]:
        copy.start()

    for cc in range(3):
        xp[pl.ds(cc * TOK, TOK), :] = expert_in[:, cc * COL : (cc + 1) * COL]
    rest = expert_in[:, 3 * COL : PW]
    none = jnp.zeros_like(rest)
    xp[pl.ds(3 * TOK, TOK), :] = jnp.concatenate([rest, none], axis=1)
    xp[pl.ds(4 * TOK, TOK), :] = jnp.concatenate([none, rest], axis=1)

    def fill(i):
        rows = pl.ds(i * 256, 256)
        send[rows, :] = dot(g[rows, :], xp[...]).astype(BF16)

    each(ALL // 256, fill)

    pl.semaphore_wait(round_sem.at[1], 1)

    def to_experts(first, last):
        for n in range(first, last):
            dest = shifted(n, 1)
            remote(
                send.at[rows_of(dest), :], rcv.at[rows_of(n), :],
                ds_sem, dr_sem.at[n // GS], (dest, z),
            ).start()

    to_experts(0, HALF)
    xr0.wait_recv()
    xro.start()
    xl1.wait_recv()
    xlo.start()
    to_experts(HALF, NE - 1)
    rcv[pl.ds((NE - 1) * MSG, MSG), :] = send[rows_of(d), :]

    def piece_of(slot, half, n):
        first, number = OUT[n]
        return a.at[slot, half, pl.ds(first, number), pl.ds(0, PW)]

    def arrived(group):
        number = GS if group < 3 else GS - 1
        got = rcv.at[pl.ds(group * GM, number * MSG), :]
        remote(got, got, ds_sem, dr_sem.at[group], right).wait_recv()

    def unpack(half, n):
        first, number = OUT[n]
        arrived(2 * half + n)
        base = half * 2 * GM
        if n == 0:
            got = dot(unp0[...], rcv[pl.ds(base, GM), :])
        else:
            got = dot(unp1[...], rcv[pl.ds(base + 7 * MSG, 9 * MSG), :])
        rows = slice(first, first + number)
        for cc in range(3):
            a[0, half, rows, cc * COL : (cc + 1) * COL] = got[
                cc * number : (cc + 1) * number
            ].astype(BF16)
        a[0, half, rows, 3 * COL : PW] = (
            got[3 * number : 4 * number, :128] + got[4 * number :, 128:]
        ).astype(BF16)

    zc = {}
    for half in range(2):
        for n in range(2):
            m = 2 * half + n
            zc["r", half, n] = remote(
                piece_of(0, half, n), piece_of(1, half, n), zs_sem.at[m], zr_sem.at[m], right
            )
            zc["l", half, n] = remote(
                piece_of(0, half, n), piece_of(2, half, n), zs_sem.at[4 + m], zr_sem.at[4 + m], left
            )
    for n in range(2):
        zc["ro", n] = remote(
            piece_of(1, 0, n), piece_of(3, 0, n), zs_sem.at[8 + n], zr_sem.at[8 + n], right
        )
        zc["lo", n] = remote(
            piece_of(2, 1, n), piece_of(3, 1, n), zs_sem.at[10 + n], zr_sem.at[10 + n], left
        )

    def expert(slot, half, store):
        def first(j):
            hid[:, cols(j)] = gelu(dot(a[slot, half], win[:, cols(j)])).astype(BF16)

        each(NC, first)
        for j in range(3):
            store(cols(j), dot(hid[...], wout[:, cols(j)]))
        value = dot(hid[...], wout[:, 3 * COL :])
        store(pl.ds(3 * COL, 128), value[:, :128])
        frst[half, pl.ds(slot * CR, CR), :] = value[:, 128:].astype(BF16)

    def into_own(half):
        def store(at, value):
            own[half, :, at] = value

        return store

    def into_part(n):
        def store(at, value):
            part[n, :, at] = value.astype(BF16)

        return store

    def into_keep(n):
        def store(at, value):
            keep[n, :, at] = value

        return store

    def back_of(ref, slot, n):
        first, number = BACK[n]
        return ref.at[slot, pl.ds(first, number)]

    b_left0 = remote(part.at[0], back.at[2], bs_sem.at[0], br_sem.at[0], left)
    b_right1 = remote(part.at[1], back.at[1], bs_sem.at[1], br_sem.at[1], right)
    bc = {}
    for n in range(2):
        for m, (key, src, dst, at, dev) in enumerate(
            (
                ("across0", 2, stage, 0, right),
                ("across1", 3, stage, 1, left),
                ("right0", 4, back, 0, right),
                ("left1", 5, back, 3, left),
            )
        ):
            bc[key, n] = remote(
                back_of(part, src, n), back_of(dst, at, n),
                bs_sem.at[2 + 2 * m + n], br_sem.at[2 + 2 * m + n], dev,
            )

    loads[4].wait()
    loads[5].wait()

    for n in range(2):
        unpack(0, n)
        zc["r", 0, n].start()
        zc["l", 0, n].start()
    for copy in (xr1, xl0, xro, xlo):
        copy.wait_recv()
    for i in range(ALLF // 256):
        rows = pl.ds(i * 256, 256)
        fsend[rows, :] = dot(gf[rows, :], zx[...]).astype(BF16)
    for n in range(NE - 1):
        dest = shifted(n, 1)
        remote(
            fsend.at[frows_of(dest), :], frcv.at[frows_of(n), :],
            fds_sem, fdr_sem.at[n // HALF], (dest, z),
        ).start()
    frcv[pl.ds((NE - 1) * FMSG, FMSG), :] = fsend[frows_of(d), :]
    for n in range(2):
        unpack(1, n)
        zc["r", 1, n].start()
        zc["l", 1, n].start()

    ri = iota((TOK, ALL), 1)
    for cc in range(NC):
        line = 8 if cc < 3 else 6 + cc
        for kind in range(2):
            at = gcol[0, :, line + 3 * kind : line + 3 * kind + 1].astype(I32)
            at = at + CAP * cc if cc < 3 else at
            pick[pl.ds(cc * 256 + kind * TOK, TOK), :] = jnp.where(ri == at, 1.0, 0.0).astype(BF16)
    for n in range(2):
        zc["r", 0, n].wait_recv()
        zc["ro", n].start()
    fi = iota((TOK, ALLF), 1)
    for s in range(4):
        for kind in range(2):
            at = gcol[s, :, 1 + kind : 2 + kind].astype(I32) + CAP * s
            fpick[pl.ds(s * 256 + kind * TOK, TOK), :] = jnp.where(fi == at, 1.0, 0.0).astype(BF16)
    for n in range(2):
        zc["l", 1, n].wait_recv()
        zc["lo", n].start()

    def funpack(half):
        number = HALF if half == 0 else HALF - 1
        got = frcv.at[pl.ds(half * HALF * FMSG, number * FMSG), :]
        remote(got, got, fds_sem, fdr_sem.at[half], right).wait_recv()
        rows = dot(unf[...], frcv[pl.ds(half * HALF * FMSG, HALF * FMSG), :]).astype(BF16)
        for s in range(4):
            a[s, half, :, PW:] = rows[s * CR : (s + 1) * CR]

    def freturn(half):
        fpack[pl.ds(half * HALF * FMSG, HALF * FMSG), :] = dot(pkf[...], frst[half]).astype(BF16)
        for m in range(half * HALF, min((half + 1) * HALF, NE - 1)):
            dest = shifted(m, -1)
            remote(
                fpack.at[frows_of(m), :], fret.at[frows_of(d), :], fes_sem, fer_sem, (dest, z)
            ).start()

    funpack(0)
    expert(1, 0, into_part(0))
    b_left0.start()
    for n in range(2):
        zc["l", 0, n].wait_recv()
    expert(2, 0, into_keep(0))
    expert(0, 0, into_own(0))
    for n in range(2):
        zc["ro", n].wait_recv()
    expert(3, 0, into_part(2))
    bc["across0", 0].start()
    bc["across0", 1].start()
    freturn(0)
    for n in range(2):
        zc["r", 1, n].wait_recv()
        zc["lo", n].wait_recv()
    funpack(1)
    expert(3, 1, into_part(3))
    bc["across1", 0].start()
    bc["across1", 1].start()
    expert(2, 1, into_part(1))
    b_right1.start()
    expert(1, 1, into_keep(1))
    expert(0, 1, into_own(1))
    freturn(1)
    fret[frows_of(d), :] = fpack[pl.ds((NE - 1) * FMSG, FMSG), :]
    for n in range(2):
        first, number = BACK[n]
        rows = pl.ds(first, number)
        bc["across0", n].wait_recv()
        part[4, rows] = (keep[0, rows] + stage[0, rows].astype(F32)).astype(BF16)
        bc["right0", n].start()
        bc["across1", n].wait_recv()
        part[5, rows] = (keep[1, rows] + stage[1, rows].astype(F32)).astype(BF16)
        bc["left1", n].start()

    def half_of(ref, slot, n):
        return ref.at[slot, pl.ds(n * 64, 64)]

    ya0 = remote(half_of(fout, 3, 0), fstage.at[0], ys_sem.at[0], yr_sem.at[0], right)
    ya1 = remote(half_of(fout, 3, 1), fstage.at[1], ys_sem.at[1], yr_sem.at[1], left)
    yl0 = remote(half_of(fout, 1, 0), half_of(fback, 1, 0), ys_sem.at[2], yr_sem.at[2], left)
    yr1 = remote(half_of(fout, 2, 1), half_of(fback, 0, 1), ys_sem.at[3], yr_sem.at[3], right)
    yr0 = remote(half_of(fout, 2, 0), half_of(fback, 0, 0), ys_sem.at[4], yr_sem.at[4], right)
    yl1 = remote(half_of(fout, 1, 1), half_of(fback, 1, 1), ys_sem.at[5], yr_sem.at[5], left)
    ring += [ya0, ya1, yl0, yr1, yr0, yl1]

    b_left0.wait_recv()
    b_right1.wait_recv()
    def finish(n):
        first, number = BACK[n]
        rows = pl.ds(first, number)
        for half in range(2):
            bc["right0" if half == 0 else "left1", n].wait_recv()
            for cc in range(4):
                at = slice(cc * COL, min((cc + 1) * COL, PW))
                full = (
                    own[half, rows, at]
                    + back[half, rows, at].astype(F32)
                    + back[2 + half, rows, at].astype(F32)
                ).astype(BF16)
                both = [full]
                if cc == 3:
                    none = jnp.zeros_like(full)
                    both = [
                        jnp.concatenate([full, none], axis=1),
                        jnp.concatenate([none, full], axis=1),
                    ]
                for m, value in enumerate(both):
                    if n == 0:
                        rst[half, 0, pl.ds((cc + m) * 80, 80), :] = value
                        rst[half, 1, pl.ds((cc + m) * 80, 16), :] = value[64:]
                    else:
                        rst[half, 1, pl.ds((cc + m) * 80 + 16, 64), :] = value
            packed = dot((pkm0 if n == 0 else pkm1)[...], rst[half, n])
            group = 2 * half + n
            pack[pl.ds(group * GM, GM), :] = packed.astype(BF16)
            for m in range(group * GS, min((group + 1) * GS, NE - 1)):
                dest = shifted(m, -1)
                remote(
                    pack.at[rows_of(m), :], ret.at[rows_of(d), :], es_sem, er_sem, (dest, z)
                ).start()
    finish(0)

    others = fret.at[pl.ds(0, (NE - 1) * FMSG), :]
    remote(others, others, fes_sem, fer_sem, right).wait_recv()
    for s in (3, 1, 2, 0):
        both = dot(fpick[pl.ds(s * 256, 256), :], fret[...])
        sums = gcol[s, :, 3:4] * both[:TOK] + gcol[s, :, 4:5] * both[TOK:]
        if s == 0:
            fown[...] = sums
        else:
            fpart[s] = sums
            for n in range(2):
                rows = pl.ds(n * 64, 64)
                fout[s, rows] = sums[n * 64 : (n + 1) * 64].astype(BF16)
        if s == 3:
            ya0.start()
            ya1.start()
        if s == 1:
            yl0.start()
        if s == 2:
            yr1.start()

    finish(1)
    ret[rows_of(d), :] = pack[pl.ds((NE - 1) * MSG, MSG), :]

    ya0.wait_recv()
    fout[2, pl.ds(0, 64)] = (fpart[2, pl.ds(0, 64)] + fstage[0].astype(F32)).astype(BF16)
    yr0.start()
    ya1.wait_recv()
    fout[1, pl.ds(64, 64)] = (fpart[1, pl.ds(64, 64)] + fstage[1].astype(F32)).astype(BF16)
    yl1.start()

    others = ret.at[pl.ds(0, (NE - 1) * MSG), :]
    remote(others, others, es_sem, er_sem, right).wait_recv()
    g0, g1 = gcol[0, :, 3:4], gcol[0, :, 4:5]
    for cc in range(3):
        both = dot(pick[pl.ds(cc * 256, 256), :], ret[...])
        out[:, cols(cc)] = (mid[:, cols(cc)] + g0 * both[:TOK] + g1 * both[TOK:]).astype(BF16)
    even = dot(pick[pl.ds(3 * 256, 256), :], ret[...])[:, :128]
    both = even + dot(pick[pl.ds(4 * 256, 256), :], ret[...])[:, 128:]
    out[:, 3 * COL : PW] = (
        mid[:, 3 * COL : PW] + g0 * both[:TOK] + g1 * both[TOK:]
    ).astype(BF16)
    for copy in (yl0, yr1, yr0, yl1):
        copy.wait_recv()
    out[:, PW:] = (
        mid[:, PW:] + fown[...] + fback[0].astype(F32) + fback[1].astype(F32)
    ).astype(BF16)

    for copy in seg_copies + [r0, r1, l0, l1, ro, lo] + ring + list(zc.values()):
        copy.wait_send()
    for copy in [b_left0, b_right1] + list(bc.values()):
        copy.wait_send()
    gone = send.at[pl.ds(0, (NE - 1) * MSG), :]
    remote(gone, gone, ds_sem, dr_sem.at[0], right).wait_send()
    gone = pack.at[pl.ds(0, (NE - 1) * MSG), :]
    remote(gone, gone, es_sem, er_sem, right).wait_send()
    gone = fsend.at[pl.ds(0, (NE - 1) * FMSG), :]
    remote(gone, gone, fds_sem, fdr_sem.at[0], right).wait_send()
    gone = fpack.at[pl.ds(0, (NE - 1) * FMSG), :]
    remote(gone, gone, fes_sem, fer_sem, right).wait_send()


def layer(tok, seg, eid, gate, lna, lne, wqkv, wao, win, wout):
    vm = pl.BlockSpec(memory_space=pltpu.VMEM)
    hbm = pl.BlockSpec(memory_space=pl.ANY)
    V = pltpu.VMEM
    dma = pltpu.SemaphoreType.DMA
    return pl.pallas_call(
        kernel,
        out_shape=jax.ShapeDtypeStruct((TOK, D), BF16),
        in_specs=[hbm] * 10,
        out_specs=vm,
        scratch_shapes=[
            V((TOK, D), BF16),
            V((1, TOK), I32),
            V((2, TOK), I32),
            V((2, TOK), F32),
            V((D,), F32),
            V((D,), F32),
            V((D, 3 * D), BF16),
            V((D, D), BF16),
            V((D, D), BF16),
            V((D, D), BF16),
            V((4 * TOK, D), BF16),
            V((4 * TOK, D), BF16),
            V((4, 8, TOK), F32),
            V((TOK, D), BF16),
            V((4 * TOK, D), BF16),
            V((4 * TOK, D), BF16),
            V((TOK, D), F32),
            V((TOK, D), BF16),
            V((TOK, D), F32),
            V((NC * TOK, COL), BF16),
            V((ALL, NC * TOK), BF16),
            V((ALL, COL), BF16),
            V((ALL, COL), BF16),
            V((4, 2, CR, D), BF16),
            V((CR, D), BF16),
            V((6, CR, PW), BF16),
            V((2, CR, PW), F32),
            V((2, CR, PW), F32),
            V((2, CR, PW), BF16),
            V((4, CR, PW), BF16),
            V((2, 2, NC * 80, COL), BF16),
            V((ALL, COL), BF16),
            V((ALL, COL), BF16),
            V((NC * 64, GM), BF16),
            V((NC * 80, 9 * MSG), BF16),
            V((GM, NC * 80), BF16),
            V((GM, NC * 80), BF16),
            V((4, TOK, TOK), F32),
            V((4 * TOK, FW), BF16),
            V((ALLF, 4 * TOK), BF16),
            V((ALLF, FW), BF16),
            V((ALLF, FW), BF16),
            V((4 * CR, HALF * FMSG), BF16),
            V((HALF * FMSG, 4 * CR), BF16),
            V((2, 4 * CR, FW), BF16),
            V((ALLF, FW), BF16),
            V((ALLF, FW), BF16),
            V((4, TOK, FW), F32),
            V((4, TOK, FW), BF16),
            V((TOK, FW), F32),
            V((2, 64, FW), BF16),
            V((2, TOK, FW), BF16),
            dma((6,)),
            dma((6,)),
            dma((6,)),
            dma((6,)),
            dma((3,)),
            dma((3,)),
            dma,
            dma((4,)),
            dma((12,)),
            dma((12,)),
            dma((10,)),
            dma((10,)),
            dma,
            dma,
            pltpu.SemaphoreType.REGULAR((2,)),
            dma((6,)),
            dma((6,)),
            dma,
            dma((2,)),
            dma,
            dma,
            dma((6,)),
            dma((6,)),
        ],
        compiler_params=pltpu.CompilerParams(
            collective_id=0, has_side_effects=True, vmem_limit_bytes=60 * 1024 * 1024
        ),
        cost_estimate=pl.CostEstimate(
            flops=14_000_000_000, bytes_accessed=24_000_000, transcendentals=3_000_000
        ),
    )(tok, seg, eid, gate, lna, lne, wqkv, wao, win, wout)


def body(
    tokens, segment_ids, expert_ids, gate_values, ln_attn, w_qkv, w_attn_out, ln_expert, w_in, w_out
):
    out = layer(
        tokens[0],
        segment_ids,
        expert_ids[0].T,
        gate_values[0].T,
        ln_attn,
        ln_expert,
        w_qkv,
        w_attn_out,
        w_in[0],
        w_out[0],
    )
    return out[None]


def solution(mesh):
    placed = (
        P("dp", "seq", None),
        P("dp", "seq"),
        P("dp", "seq", None),
        P("dp", "seq", None),
        P(),
        P(),
        P(),
        P(),
        P("dp", None, "seq"),
        P("dp", "seq", None),
    )
    return jax.shard_map(
        body, mesh=mesh, in_specs=placed, out_specs=P("dp", "seq", None), check_vma=False
    )
```

```python
import functools

import jax
import jax.numpy as jnp
from jax import lax
from jax.experimental import pallas as pl
from jax.experimental.pallas import tpu as pltpu
from jax.sharding import PartitionSpec as P

F32 = jnp.float32
BF16 = jnp.bfloat16
I32 = jnp.int32
MESH = pl.DeviceIdType.MESH

D = 1280
HEADS = 16
HEAD = 80
TOK = 128
CAP = 9
NE = 32
COL = 256
NC = D // COL
PW = 896
FW = D - PW
MSG = 32
FMSG = 48
HALF = 16
CR = HALF * CAP
GS = 8
GM = GS * MSG
FGM = GS * FMSG
ALLF = NE * FMSG
ALL = NE * MSG
EPS = 1e-06
NEG = -1e30

GROUPS = (((0, 1, 2), 0), ((3,), 128), ((4, 5), 256), ((6, 7), 384))


OFFSETS = sorted(
    [(dx, dy, dc) for dx in range(4) for dy in range(4) for dc in range(2)],
    key=lambda o: -(min(o[0], 4 - o[0]) + min(o[1], 4 - o[1]) + 0.5 * o[2]),
)

OUT = ((0, 64), (64, 80))
BACK = ((0, 80), (80, 64))


def normalize(rows, gain):
    mean = jnp.mean(rows, axis=-1, keepdims=True)
    centered = rows - mean
    spread = jnp.mean(centered * centered, axis=-1, keepdims=True)
    return centered * lax.rsqrt(spread + EPS) * gain


def gelu(x):
    return 0.5 * x * (1.0 + jnp.tanh(0.7978845608028654 * (x + 0.044715 * (x * x * x))))


def iota(shape, dim):
    return lax.broadcasted_iota(I32, shape, dim)


def dot(a, b):
    return jnp.dot(a, b, preferred_element_type=F32)


def cols(j):
    return pl.ds(j * COL, COL)


def each(number, step):
    for i in range(number):
        step(i)


def kernel(
    tok_h, seg_h, eid_h, gate_h, lna_h, lne_h, wqkv_h, wao_h, win_h, wout_h, out,
    tok, seg, eid, gate, lna, lne, wqkv, wao, win, wout, xn, xraw, info, q, k, v, ctx, ctxb, mid, xp, g, send, rcv, a, hid,
    part, keep, own, stage, back, rst, pack, ret, unp0, unp1, pkm0, pkm1, gcol,
    zx, gf, fsend, frcv, unf, pkf, frst, fpack, fret, facc, pacc, fpart, fout, fown, fstage, fback,
    i_sem, w_sem, as_sem, ar_sem, ss_sem, sr_sem, ds_sem, dr_sem, zs_sem, zr_sem, bs_sem, br_sem,
    es_sem, er_sem, round_sem, xs_sem, xr_sem, fds_sem, fdr_sem, fes_sem, fer_sem, ys_sem, yr_sem,
):
    pick = wqkv.at[:, pl.ds(0, ALL)]
    fpick = wqkv.at[pl.ds(0, 4 * 256), pl.ds(ALL, ALLF)]
    d = lax.axis_index("dp")
    z = lax.axis_index("seq")
    zl = lax.rem(z + 3, 4)
    zr = lax.rem(z + 1, 4)
    zo = lax.rem(z + 2, 4)
    x, y, c = d // 8, lax.rem(d // 2, 4), lax.rem(d, 2)

    xs = [lax.rem(x + i, 4) * 8 for i in range(4)]
    ys = [lax.rem(y + i, 4) * 2 for i in range(4)]
    cs = [c, 1 - c]

    def shifted(n, sign):
        dx, dy, dc = OFFSETS[n]
        return xs[sign * dx % 4] + ys[sign * dy % 4] + cs[dc]

    def rows_of(j):
        return pl.ds(j * MSG, MSG)

    def frows_of(j):
        return pl.ds(j * FMSG, FMSG)

    small = [(tok_h, tok), (lna_h, lna), (eid_h, eid), (seg_h, seg), (gate_h, gate), (lne_h, lne)]
    small = [pltpu.make_async_copy(src, dst, i_sem.at[n]) for n, (src, dst) in enumerate(small)]
    for copy in small:
        copy.start()
    loads = []
    for i in range(3):
        part_of = pl.ds(i * D, D)
        loads.append(pltpu.make_async_copy(wqkv_h.at[:, part_of], wqkv.at[:, part_of], w_sem.at[i]))
    loads.append(pltpu.make_async_copy(wao_h, wao, w_sem.at[3]))
    loads.append(pltpu.make_async_copy(win_h, win, w_sem.at[4]))
    loads.append(pltpu.make_async_copy(wout_h, wout, w_sem.at[5]))
    barrier = pltpu.get_barrier_semaphore()
    for other in (zl, zr, zo):
        pl.semaphore_signal(barrier, inc=1, device_id=(d, other), device_id_type=MESH)

    x_line = [xs[i] + ys[0] + cs[0] for i in range(1, 4)]
    y_line = [xs[0] + ys[i] + cs[0] for i in range(1, 4)]
    twin = xs[0] + ys[0] + cs[1]
    for other in x_line + y_line + [twin]:
        pl.semaphore_signal(barrier, inc=1, device_id=(other, z), device_id_type=MESH)

    pl.semaphore_wait(barrier, 10)

    def remote(src, dst, s_sem, r_sem, dev):
        return pltpu.make_async_remote_copy(
            src_ref=src, dst_ref=dst, send_sem=s_sem, recv_sem=r_sem,
            device_id=dev, device_id_type=MESH,
        )

    right, left, across = (d, zr), (d, zl), (d, zo)

    def xrows(slot, half):
        rows = pl.ds(slot * TOK + half * 64, 64)
        return tok_h.at[pl.ds(half * 64, 64), :] if slot == 0 else xraw.at[rows, :]

    seg_copies = [
        remote(info.at[0], info.at[1], ss_sem.at[0], sr_sem.at[0], right),
        remote(info.at[0], info.at[2], ss_sem.at[1], sr_sem.at[1], left),
        remote(info.at[0], info.at[3], ss_sem.at[2], sr_sem.at[2], across),
    ]
    r0 = remote(xrows(0, 0), xrows(1, 0), as_sem.at[0], ar_sem.at[0], right)
    r1 = remote(xrows(0, 1), xrows(1, 1), as_sem.at[1], ar_sem.at[1], right)
    l1 = remote(xrows(0, 1), xrows(2, 1), as_sem.at[2], ar_sem.at[2], left)
    l0 = remote(xrows(0, 0), xrows(2, 0), as_sem.at[3], ar_sem.at[3], left)
    ro = remote(xrows(1, 0), xrows(3, 0), as_sem.at[4], ar_sem.at[4], right)
    lo = remote(xrows(2, 1), xrows(3, 1), as_sem.at[5], ar_sem.at[5], left)
    r0.start()
    l1.start()
    r1.start()
    l0.start()
    for load in loads:
        load.start()
    for copy in small:
        copy.wait()

    e0, e1 = eid[0:1, :], eid[1:2, :]
    ei = iota((NE, TOK), 0)
    named = jnp.where((ei == e0) | (ei == e1), 1.0, 0.0).astype(BF16)
    before = jnp.where(iota((TOK, TOK), 0) < iota((TOK, TOK), 1), 1.0, 0.0).astype(BF16)
    count = dot(named, before)
    order = jnp.full((NE, TOK), NE - 1, I32)
    for n in range(NE - 1):
        order = jnp.where(ei == shifted(n, 1), n, order)
    chosen = []
    lines = [seg[...].astype(F32)]
    for e in (e0, e1):
        slot = jnp.sum(jnp.where(ei == e, count, 0.0), axis=0, keepdims=True).astype(I32)
        e = jnp.sum(jnp.where(ei == e, order, 0), axis=0, keepdims=True)
        lines.append((e * FMSG + slot).astype(F32))
        odd = slot & 1
        pair = e * MSG + 3 * CAP + lax.shift_right_logical(slot, 1)
        chosen.append(
            (e * MSG + slot, jnp.where(odd == 0, pair, -1), jnp.where(odd == 1, pair, -1))
        )
    lines += [gate[0:1, :], gate[1:2, :]]
    ri = iota((8, TOK), 0)

    def stacked_lines(rows):
        total = jnp.zeros((8, TOK), F32)
        for n, row in enumerate(rows):
            total = jnp.where(ri == n, row, total)
        return total

    info[0] = stacked_lines(lines)
    for copy in seg_copies:
        copy.start()
    xn[pl.ds(0, TOK), :] = normalize(tok[...].astype(F32), lna[...].reshape(1, D)).astype(BF16)

    for other in x_line:
        pl.semaphore_signal(round_sem.at[0], inc=1, device_id=(other, z), device_id_type=MESH)

    def place(kind, cc):
        return chosen[kind][0] + CAP * cc if cc < 3 else chosen[kind][cc - 2]

    def make_g(i):
        rows = pl.ds(i * 256, 256)
        r = iota((256, TOK), 0) + i * 256
        for cc in range(NC):
            hit = (r == place(0, cc)) | (r == place(1, cc))
            g[rows, cc * TOK : (cc + 1) * TOK] = jnp.where(hit, 1.0, 0.0).astype(BF16)

    each(ALL // 256, make_g)

    def fixed(ref, q_dim, rows, first, base, msg):
        q = iota(ref.shape, q_dim)
        r = iota(ref.shape, 1 - q_dim) + base
        times, shift = {64: (1, 6), 80: (205, 14), CR: (1821, 18)}[rows]
        cc = lax.shift_right_logical(q * times, shift)
        i = q - cc * rows + first
        source = lax.shift_right_logical(i * 57, 9)
        slot = i - CAP * source
        at = source * msg + CAP * cc + slot
        if msg == MSG:
            pair = source * msg + 3 * CAP + lax.shift_right_logical(slot, 1)
            at = jnp.where(cc < 3, at, jnp.where((slot & 1) == cc - 3, pair, -1))
        ref[...] = jnp.where(r == at, 1.0, 0.0).astype(BF16)


    r0.wait_recv()
    ro.start()
    l1.wait_recv()
    lo.start()

    pl.semaphore_wait(round_sem.at[0], 3)
    pl.semaphore_signal(round_sem.at[1], inc=1, device_id=(twin, z), device_id_type=MESH)

    for load in loads[:3]:
        load.wait()

    def own_q(j):
        q[:, cols(j)] = dot(xn[pl.ds(0, TOK), :], wqkv[:, cols(j)]).astype(BF16)

    each(NC, own_q)

    def keys_values(first, number):
        rows = pl.ds(first, number)
        if first:
            xn[rows, :] = normalize(xraw[rows, :].astype(F32), lna[...].reshape(1, D)).astype(BF16)

        def step(j):
            k[rows, cols(j)] = dot(xn[rows, :], wqkv[:, cols(j + NC)]).astype(BF16)
            v[rows, cols(j)] = dot(xn[rows, :], wqkv[:, cols(j + 2 * NC)]).astype(BF16)

        each(NC, step)

    keys_values(0, TOK)

    r1.wait_recv()
    l0.wait_recv()
    keys_values(TOK, 2 * TOK)

    for copy in seg_copies:
        copy.wait_recv()
    eight = iota((8, TOK), 0).astype(F32)
    kinds = [jnp.where(eight == info[s, 0:1, :], 1.0, 0.0).astype(BF16) for s in range(4)]
    key_kind = jnp.concatenate(kinds, axis=1)
    same = lax.dot_general(kinds[0], key_kind, (((0,), (0,)), ((), ())), preferred_element_type=F32)
    bias = jnp.where(same > 0.5, 0.0, NEG)

    ro.wait_recv()
    lo.wait_recv()
    keys_values(3 * TOK, TOK)

    scale = HEAD ** (-0.5)
    ctx[...] = jnp.zeros((TOK, D), F32)
    for half in range(2):
        for heads, at in GROUPS:
            window = pl.ds(half * 640 + at, COL)
            lane = iota((TOK, COL), 1) + at
            masks = [(lane >= h * HEAD) & (lane < (h + 1) * HEAD) for h in heads]
            qw = q[:, window]
            zero = jnp.zeros_like(qw)
            stacked = jnp.concatenate([jnp.where(m, qw, zero) for m in masks], axis=0)
            scores = lax.dot_general(
                stacked, k[:, window], (((1,), (1,)), ((), ())), preferred_element_type=F32
            )
            probs, sums = [], []
            for n in range(len(heads)):
                s = scores[n * TOK : (n + 1) * TOK, :] * scale + bias
                w = jnp.exp(s - jnp.max(s, axis=-1, keepdims=True))
                sums.append(jnp.sum(w, axis=-1, keepdims=True))
                probs.append(w.astype(BF16))
            mixed = dot(jnp.concatenate(probs, axis=0), v[:, window])
            total = ctx[:, window]
            for n, m in enumerate(masks):
                total = jnp.where(m, mixed[n * TOK : (n + 1) * TOK, :] / sums[n], total)
            ctx[:, window] = total
    ctxb[...] = ctx[...].astype(BF16)

    loads[3].wait()

    def project(j):
        mid[:, cols(j)] = tok[:, cols(j)].astype(F32) + dot(ctxb[...], wao[:, cols(j)])

    each(NC, project)
    expert_in = normalize(mid[...], lne[...].reshape(1, D)).astype(BF16)
    zx[pl.ds(0, TOK), :] = expert_in[:, PW:]

    def zrows(slot, half):
        return zx.at[pl.ds(slot * TOK + half * 64, 64), :]

    xr0 = remote(zrows(0, 0), zrows(1, 0), xs_sem.at[0], xr_sem.at[0], right)
    xr1 = remote(zrows(0, 1), zrows(1, 1), xs_sem.at[1], xr_sem.at[1], right)
    xl1 = remote(zrows(0, 1), zrows(2, 1), xs_sem.at[2], xr_sem.at[2], left)
    xl0 = remote(zrows(0, 0), zrows(2, 0), xs_sem.at[3], xr_sem.at[3], left)
    xro = remote(zrows(1, 0), zrows(3, 0), xs_sem.at[4], xr_sem.at[4], right)
    xlo = remote(zrows(2, 1), zrows(3, 1), xs_sem.at[5], xr_sem.at[5], left)
    ring = [xr0, xr1, xl1, xl0, xro, xlo]
    for copy in ring[:4]:
        copy.start()

    for cc in range(3):
        xp[pl.ds(cc * TOK, TOK), :] = expert_in[:, cc * COL : (cc + 1) * COL]
    rest = expert_in[:, 3 * COL : PW]
    none = jnp.zeros_like(rest)
    xp[pl.ds(3 * TOK, TOK), :] = jnp.concatenate([rest, none], axis=1)
    xp[pl.ds(4 * TOK, TOK), :] = jnp.concatenate([none, rest], axis=1)

    def fill(i):
        rows = pl.ds(i * 256, 256)
        send[rows, :] = dot(g[rows, :], xp[...]).astype(BF16)


    pl.semaphore_wait(round_sem.at[1], 1)

    def to_experts(first, last):
        for n in range(first, last):
            dest = shifted(n, 1)
            remote(
                send.at[rows_of(n), :], rcv.at[rows_of(n), :],
                ds_sem, dr_sem.at[n // GS], (dest, z),
            ).start()

    for i in range(2):
        fill(i)
        to_experts(i * GS, (i + 1) * GS)
    xr0.wait_recv()
    xro.start()
    xl1.wait_recv()
    xlo.start()
    for i in range(2, 4):
        fill(i)
        to_experts(i * GS, min((i + 1) * GS, NE - 1))
    rcv[rows_of(NE - 1), :] = send[rows_of(NE - 1), :]

    fixed(unp0, 0, 64, 0, 0, MSG)
    fixed(unp1, 0, 80, 64, 7 * MSG, MSG)
    for s in range(4):
        r = iota((ALLF, TOK), 0) - CAP * s
        f0, f1 = info[s, 1:2, :].astype(I32), info[s, 2:3, :].astype(I32)
        gf[:, s * TOK : (s + 1) * TOK] = jnp.where((r == f0) | (r == f1), 1.0, 0.0).astype(BF16)

    def piece_of(slot, half, n):
        first, number = OUT[n]
        return a.at[slot, half, pl.ds(first, number), pl.ds(0, PW)]

    def arrived(group):
        number = GS if group < 3 else GS - 1
        got = rcv.at[pl.ds(group * GM, number * MSG), :]
        remote(got, got, ds_sem, dr_sem.at[group], right).wait_recv()

    def unpack(half, n):
        first, number = OUT[n]
        arrived(2 * half + n)
        base = half * 2 * GM
        if n == 0:
            got = dot(unp0[...], rcv[pl.ds(base, GM), :])
        else:
            got = dot(unp1[...], rcv[pl.ds(base + 7 * MSG, 9 * MSG), :])
        rows = slice(first, first + number)
        for cc in range(3):
            a[0, half, rows, cc * COL : (cc + 1) * COL] = got[
                cc * number : (cc + 1) * number
            ].astype(BF16)
        a[0, half, rows, 3 * COL : PW] = (
            got[3 * number : 4 * number, :128] + got[4 * number :, 128:]
        ).astype(BF16)

    zc = {}
    for half in range(2):
        for n in range(2):
            m = 2 * half + n
            zc["r", half, n] = remote(
                piece_of(0, half, n), piece_of(1, half, n), zs_sem.at[m], zr_sem.at[m], right
            )
            zc["l", half, n] = remote(
                piece_of(0, half, n), piece_of(2, half, n), zs_sem.at[4 + m], zr_sem.at[4 + m], left
            )
    for n in range(2):
        zc["ro", n] = remote(
            piece_of(1, 0, n), piece_of(3, 0, n), zs_sem.at[8 + n], zr_sem.at[8 + n], right
        )
        zc["lo", n] = remote(
            piece_of(2, 1, n), piece_of(3, 1, n), zs_sem.at[10 + n], zr_sem.at[10 + n], left
        )

    def expert(slot, half, store):
        def first(j):
            hid[:, cols(j)] = gelu(dot(a[slot, half], win[:, cols(j)])).astype(BF16)

        each(NC, first)
        for j in range(3):
            store(cols(j), dot(hid[...], wout[:, cols(j)]))
        value = dot(hid[...], wout[:, 3 * COL :])
        store(pl.ds(3 * COL, 128), value[:, :128])
        frst[half, pl.ds(slot * CR, CR), :] = value[:, 128:].astype(BF16)

    def into_own(half):
        def store(at, value):
            own[half, :, at] = value

        return store

    def into_part(n):
        def store(at, value):
            part[n, :, at] = value.astype(BF16)

        return store

    def into_keep(n):
        def store(at, value):
            keep[n, :, at] = value

        return store

    def back_of(ref, slot, n):
        first, number = BACK[n]
        return ref.at[slot, pl.ds(first, number)]

    b_left0 = remote(part.at[0], back.at[2], bs_sem.at[0], br_sem.at[0], left)
    b_right1 = remote(part.at[1], back.at[1], bs_sem.at[1], br_sem.at[1], right)
    bc = {}
    for n in range(2):
        for m, (key, src, dst, at, dev) in enumerate(
            (
                ("across0", 2, stage, 0, right),
                ("across1", 3, stage, 1, left),
                ("right0", 4, back, 0, right),
                ("left1", 5, back, 3, left),
            )
        ):
            bc[key, n] = remote(
                back_of(part, src, n), back_of(dst, at, n),
                bs_sem.at[2 + 2 * m + n], br_sem.at[2 + 2 * m + n], dev,
            )

    loads[4].wait()
    loads[5].wait()

    for n in range(2):
        unpack(0, n)
        zc["r", 0, n].start()
        zc["l", 0, n].start()
    for copy in (xr1, xl0, xro, xlo):
        copy.wait_recv()
    for half in range(2):
        rows = pl.ds(half * HALF * FMSG, HALF * FMSG)
        fsend[rows, :] = dot(gf[rows, :], zx[...]).astype(BF16)
        for n in range(half * HALF, min((half + 1) * HALF, NE - 1)):
            dest = shifted(n, 1)
            remote(
                fsend.at[frows_of(n), :], frcv.at[frows_of(n), :],
                fds_sem, fdr_sem.at[half], (dest, z),
            ).start()
    frcv[frows_of(NE - 1), :] = fsend[frows_of(NE - 1), :]
    for n in range(2):
        unpack(1, n)
        zc["r", 1, n].start()
        zc["l", 1, n].start()

    for s in range(4):
        more = jnp.zeros((8, TOK), F32)
        if s == 0:
            more = stacked_lines([row.astype(F32) for kind in chosen for row in kind])
        square = jnp.concatenate([info[s], more, jnp.zeros((TOK - 16, TOK), F32)], axis=0)
        gcol[s] = jnp.transpose(square)
    fixed(unf, 0, CR, 0, 0, FMSG)

    ri = iota((TOK, ALL), 1)
    for cc in range(NC):
        line = 8 if cc < 3 else 6 + cc
        for kind in range(2):
            at = gcol[0, :, line + 3 * kind : line + 3 * kind + 1].astype(I32)
            at = at + CAP * cc if cc < 3 else at
            pick[pl.ds(cc * 256 + kind * TOK, TOK), :] = jnp.where(ri == at, 1.0, 0.0).astype(BF16)
    for n in range(2):
        zc["r", 0, n].wait_recv()
        zc["ro", n].start()
    fi = iota((TOK, ALLF), 1)
    for s in range(4):
        for kind in range(2):
            at = gcol[s, :, 1 + kind : 2 + kind].astype(I32) + CAP * s
            fpick[pl.ds(s * 256 + kind * TOK, TOK), :] = jnp.where(fi == at, 1.0, 0.0).astype(BF16)
    fixed(pkf, 1, CR, 0, 0, FMSG)
    for n in range(2):
        zc["l", 1, n].wait_recv()
        zc["lo", n].start()
    fixed(pkm0, 1, 80, 0, 0, MSG)
    fixed(pkm1, 1, 80, 64, GM, MSG)

    def funpack(half):
        number = HALF if half == 0 else HALF - 1
        got = frcv.at[pl.ds(half * HALF * FMSG, number * FMSG), :]
        remote(got, got, fds_sem, fdr_sem.at[half], right).wait_recv()
        rows = dot(unf[...], frcv[pl.ds(half * HALF * FMSG, HALF * FMSG), :]).astype(BF16)
        for s in range(4):
            a[s, half, :, PW:] = rows[s * CR : (s + 1) * CR]

    def freturn(half):
        fpack[pl.ds(half * HALF * FMSG, HALF * FMSG), :] = dot(pkf[...], frst[half]).astype(BF16)
        for m in range(half * HALF, min((half + 1) * HALF, NE - 1)):
            dest = shifted(m, -1)
            remote(
                fpack.at[frows_of(m), :], fret.at[frows_of(m), :],
                fes_sem, fer_sem.at[half], (dest, z),
            ).start()

    funpack(0)
    expert(1, 0, into_part(0))
    b_left0.start()
    for n in range(2):
        zc["l", 0, n].wait_recv()
    expert(2, 0, into_keep(0))
    expert(0, 0, into_own(0))
    for n in range(2):
        zc["ro", n].wait_recv()
    expert(3, 0, into_part(2))
    bc["across0", 0].start()
    bc["across0", 1].start()
    freturn(0)
    for n in range(2):
        zc["r", 1, n].wait_recv()
        zc["lo", n].wait_recv()
    funpack(1)
    expert(3, 1, into_part(3))
    bc["across1", 0].start()
    bc["across1", 1].start()
    expert(2, 1, into_part(1))
    b_right1.start()
    expert(1, 1, into_keep(1))
    expert(0, 1, into_own(1))
    freturn(1)
    fret[frows_of(NE - 1), :] = fpack[frows_of(NE - 1), :]
    for n in range(2):
        first, number = BACK[n]
        rows = pl.ds(first, number)
        bc["across0", n].wait_recv()
        part[4, rows] = (keep[0, rows] + stage[0, rows].astype(F32)).astype(BF16)
        bc["right0", n].start()
        bc["across1", n].wait_recv()
        part[5, rows] = (keep[1, rows] + stage[1, rows].astype(F32)).astype(BF16)
        bc["left1", n].start()

    def half_of(ref, slot, n):
        return ref.at[slot, pl.ds(n * 64, 64)]

    ya0 = remote(half_of(fout, 3, 0), fstage.at[0], ys_sem.at[0], yr_sem.at[0], right)
    ya1 = remote(half_of(fout, 3, 1), fstage.at[1], ys_sem.at[1], yr_sem.at[1], left)
    yl0 = remote(half_of(fout, 1, 0), half_of(fback, 1, 0), ys_sem.at[2], yr_sem.at[2], left)
    yr1 = remote(half_of(fout, 2, 1), half_of(fback, 0, 1), ys_sem.at[3], yr_sem.at[3], right)
    yr0 = remote(half_of(fout, 2, 0), half_of(fback, 0, 0), ys_sem.at[4], yr_sem.at[4], right)
    yl1 = remote(half_of(fout, 1, 1), half_of(fback, 1, 1), ys_sem.at[5], yr_sem.at[5], left)
    ring += [ya0, ya1, yl0, yr1, yr0, yl1]

    b_left0.wait_recv()
    b_right1.wait_recv()
    def finish(n):
        first, number = BACK[n]
        rows = pl.ds(first, number)
        for half in range(2):
            bc["right0" if half == 0 else "left1", n].wait_recv()
            for cc in range(4):
                at = slice(cc * COL, min((cc + 1) * COL, PW))
                full = (
                    own[half, rows, at]
                    + back[half, rows, at].astype(F32)
                    + back[2 + half, rows, at].astype(F32)
                ).astype(BF16)
                both = [full]
                if cc == 3:
                    none = jnp.zeros_like(full)
                    both = [
                        jnp.concatenate([full, none], axis=1),
                        jnp.concatenate([none, full], axis=1),
                    ]
                for m, value in enumerate(both):
                    if n == 0:
                        rst[half, 0, pl.ds((cc + m) * 80, 80), :] = value
                        rst[half, 1, pl.ds((cc + m) * 80, 16), :] = value[64:]
                    else:
                        rst[half, 1, pl.ds((cc + m) * 80 + 16, 64), :] = value
            packed = dot((pkm0 if n == 0 else pkm1)[...], rst[half, n])
            group = 2 * half + n
            pack[pl.ds(group * GM, GM), :] = packed.astype(BF16)
            for m in range(group * GS, min((group + 1) * GS, NE - 1)):
                dest = shifted(m, -1)
                remote(
                    pack.at[rows_of(m), :], ret.at[rows_of(m), :],
                    es_sem, er_sem.at[group], (dest, z),
                ).start()
    def fhalf(half):
        number = HALF if half == 0 else HALF - 1
        got = fret.at[pl.ds(half * HALF * FMSG, number * FMSG), :]
        remote(got, got, fes_sem, fer_sem.at[half], right).wait_recv()

    early = pl.ds(0, HALF * FMSG)
    late = pl.ds(HALF * FMSG, HALF * FMSG)
    fhalf(0)
    facc[...] = dot(fpick[:, early], fret[early, :])
    finish(0)
    fhalf(1)

    def weighted(both, s):
        return gcol[s, :, 3:4] * both[:TOK] + gcol[s, :, 4:5] * both[TOK:]

    rows = pl.ds(3 * 256, 256)
    fout[3] = weighted(facc[rows, :] + dot(fpick[rows, late], fret[late, :]), 3).astype(BF16)
    ya0.start()
    ya1.start()
    rows = pl.ds(0, 3 * 256)
    both = facc[rows, :] + dot(fpick[rows, late], fret[late, :])
    for s in range(3):
        sums = weighted(both[s * 256 : (s + 1) * 256], s)
        if s == 0:
            fown[...] = sums
        else:
            fpart[s] = sums
            fout[s] = sums.astype(BF16)
    yl0.start()
    yr1.start()

    finish(1)
    ret[rows_of(NE - 1), :] = pack[rows_of(NE - 1), :]

    ya0.wait_recv()
    fout[2, pl.ds(0, 64)] = (fpart[2, pl.ds(0, 64)] + fstage[0].astype(F32)).astype(BF16)
    yr0.start()
    ya1.wait_recv()
    fout[1, pl.ds(64, 64)] = (fpart[1, pl.ds(64, 64)] + fstage[1].astype(F32)).astype(BF16)
    yl1.start()

    def returned(group):
        number = GS if group < 3 else GS - 1
        got = ret.at[pl.ds(group * GM, number * MSG), :]
        remote(got, got, es_sem, er_sem.at[group], right).wait_recv()
        return pl.ds(group * GM, GM)

    first, second = returned(0), returned(2)
    pacc[...] = dot(pick[:, first], ret[first, :]) + dot(pick[:, second], ret[second, :])
    first, second = returned(1), returned(3)
    picked = dot(pick[:, first], ret[first, :]) + dot(pick[:, second], ret[second, :])
    picked = pacc[...] + picked
    g0, g1 = gcol[0, :, 3:4], gcol[0, :, 4:5]
    for cc in range(3):
        both = picked[cc * 256 : (cc + 1) * 256]
        out[:, cols(cc)] = (mid[:, cols(cc)] + g0 * both[:TOK] + g1 * both[TOK:]).astype(BF16)
    both = picked[3 * 256 : 4 * 256, :128] + picked[4 * 256 :, 128:]
    out[:, 3 * COL : PW] = (
        mid[:, 3 * COL : PW] + g0 * both[:TOK] + g1 * both[TOK:]
    ).astype(BF16)
    for copy in (yl0, yr1, yr0, yl1):
        copy.wait_recv()
    out[:, PW:] = (
        mid[:, PW:] + fown[...] + fback[0].astype(F32) + fback[1].astype(F32)
    ).astype(BF16)

    for copy in seg_copies + [r0, r1, l0, l1, ro, lo] + ring + list(zc.values()):
        copy.wait_send()
    for copy in [b_left0, b_right1] + list(bc.values()):
        copy.wait_send()
    gone = send.at[pl.ds(0, (NE - 1) * MSG), :]
    remote(gone, gone, ds_sem, dr_sem.at[0], right).wait_send()
    gone = pack.at[pl.ds(0, (NE - 1) * MSG), :]
    remote(gone, gone, es_sem, er_sem.at[0], right).wait_send()
    gone = fsend.at[pl.ds(0, (NE - 1) * FMSG), :]
    remote(gone, gone, fds_sem, fdr_sem.at[0], right).wait_send()
    gone = fpack.at[pl.ds(0, (NE - 1) * FMSG), :]
    remote(gone, gone, fes_sem, fer_sem.at[0], right).wait_send()


def layer(tok, seg, eid, gate, lna, lne, wqkv, wao, win, wout):
    vm = pl.BlockSpec(memory_space=pltpu.VMEM)
    hbm = pl.BlockSpec(memory_space=pl.ANY)
    V = pltpu.VMEM
    dma = pltpu.SemaphoreType.DMA
    return pl.pallas_call(
        kernel,
        out_shape=jax.ShapeDtypeStruct((TOK, D), BF16),
        in_specs=[hbm] * 10,
        out_specs=vm,
        scratch_shapes=[
            V((TOK, D), BF16),
            V((1, TOK), I32),
            V((2, TOK), I32),
            V((2, TOK), F32),
            V((D,), F32),
            V((D,), F32),
            V((D, 3 * D), BF16),
            V((D, D), BF16),
            V((D, D), BF16),
            V((D, D), BF16),
            V((4 * TOK, D), BF16),
            V((4 * TOK, D), BF16),
            V((4, 8, TOK), F32),
            V((TOK, D), BF16),
            V((4 * TOK, D), BF16),
            V((4 * TOK, D), BF16),
            V((TOK, D), F32),
            V((TOK, D), BF16),
            V((TOK, D), F32),
            V((NC * TOK, COL), BF16),
            V((ALL, NC * TOK), BF16),
            V((ALL, COL), BF16),
            V((ALL, COL), BF16),
            V((4, 2, CR, D), BF16),
            V((CR, D), BF16),
            V((6, CR, PW), BF16),
            V((2, CR, PW), F32),
            V((2, CR, PW), F32),
            V((2, CR, PW), BF16),
            V((4, CR, PW), BF16),
            V((2, 2, NC * 80, COL), BF16),
            V((ALL, COL), BF16),
            V((ALL, COL), BF16),
            V((NC * 64, GM), BF16),
            V((NC * 80, 9 * MSG), BF16),
            V((GM, NC * 80), BF16),
            V((GM, NC * 80), BF16),
            V((4, TOK, TOK), F32),
            V((4 * TOK, FW), BF16),
            V((ALLF, 4 * TOK), BF16),
            V((ALLF, FW), BF16),
            V((ALLF, FW), BF16),
            V((4 * CR, HALF * FMSG), BF16),
            V((HALF * FMSG, 4 * CR), BF16),
            V((2, 4 * CR, FW), BF16),
            V((ALLF, FW), BF16),
            V((ALLF, FW), BF16),
            V((4 * 256, FW), F32),
            V((NC * 256, COL), F32),
            V((4, TOK, FW), F32),
            V((4, TOK, FW), BF16),
            V((TOK, FW), F32),
            V((2, 64, FW), BF16),
            V((2, TOK, FW), BF16),
            dma((6,)),
            dma((6,)),
            dma((6,)),
            dma((6,)),
            dma((3,)),
            dma((3,)),
            dma,
            dma((4,)),
            dma((12,)),
            dma((12,)),
            dma((10,)),
            dma((10,)),
            dma,
            dma((4,)),
            pltpu.SemaphoreType.REGULAR((2,)),
            dma((6,)),
            dma((6,)),
            dma,
            dma((2,)),
            dma,
            dma((2,)),
            dma((6,)),
            dma((6,)),
        ],
        compiler_params=pltpu.CompilerParams(
            collective_id=0, has_side_effects=True, vmem_limit_bytes=60 * 1024 * 1024
        ),
        cost_estimate=pl.CostEstimate(
            flops=14_000_000_000, bytes_accessed=24_000_000, transcendentals=3_000_000
        ),
    )(tok, seg, eid, gate, lna, lne, wqkv, wao, win, wout)


def body(
    tokens, segment_ids, expert_ids, gate_values, ln_attn, w_qkv, w_attn_out, ln_expert, w_in, w_out
):
    out = layer(
        tokens[0],
        segment_ids,
        expert_ids[0].T,
        gate_values[0].T,
        ln_attn,
        ln_expert,
        w_qkv,
        w_attn_out,
        w_in[0],
        w_out[0],
    )
    return out[None]


def solution(mesh):
    placed = (
        P("dp", "seq", None),
        P("dp", "seq"),
        P("dp", "seq", None),
        P("dp", "seq", None),
        P(),
        P(),
        P(),
        P(),
        P("dp", None, "seq"),
        P("dp", "seq", None),
    )
    return jax.shard_map(
        body, mesh=mesh, in_specs=placed, out_specs=P("dp", "seq", None), check_vma=False
    )
```

```python
import functools

import jax
import jax.numpy as jnp
from jax import lax
from jax.experimental import pallas as pl
from jax.experimental.pallas import tpu as pltpu
from jax.sharding import PartitionSpec as P

F32 = jnp.float32
BF16 = jnp.bfloat16
I32 = jnp.int32
MESH = pl.DeviceIdType.MESH

D = 1280
HEADS = 16
HEAD = 80
TOK = 128
CAP = 9
NE = 32
COL = 256
NC = D // COL
PW = 896
FW = D - PW
MSG = 32
FMSG = 48
HALF = 16
CR = HALF * CAP
GS = 8
GM = GS * MSG
FGM = GS * FMSG
ALLF = NE * FMSG
ALL = NE * MSG
EPS = 1e-06
NEG = -1e30

GROUPS = (((0, 1, 2), 0), ((3,), 128), ((4, 5), 256), ((6, 7), 384))


OFFSETS = sorted(
    [(dx, dy, dc) for dx in range(4) for dy in range(4) for dc in range(2)],
    key=lambda o: -(min(o[0], 4 - o[0]) + min(o[1], 4 - o[1]) + 0.5 * o[2]),
)

OUT = ((0, 64), (64, 80))
BACK = ((0, 80), (80, 64))


def normalize(rows, gain):
    mean = jnp.mean(rows, axis=-1, keepdims=True)
    centered = rows - mean
    spread = jnp.mean(centered * centered, axis=-1, keepdims=True)
    return centered * lax.rsqrt(spread + EPS) * gain


def gelu(x):
    return 0.5 * x * (1.0 + jnp.tanh(0.7978845608028654 * (x + 0.044715 * (x * x * x))))


def iota(shape, dim):
    return lax.broadcasted_iota(I32, shape, dim)


def dot(a, b):
    return jnp.dot(a, b, preferred_element_type=F32)


def cols(j):
    return pl.ds(j * COL, COL)


def each(number, step):
    for i in range(number):
        step(i)


def kernel(
    tok_h, seg_h, eid_h, gate_h, lna_h, lne_h, wqkv_h, wao_h, win_h, wout_h, out_h,
    out,    tok, seg, eid, gate, lna, lne, wqkv, wao, win, wout, xn, xraw, info, q, k, v, ctx, ctxb, mid, xp, g, send, rcv, a, hid,
    part, keep, own, stage, back, rst, pack, ret, unp0, unp1, pkm0, pkm1, gcol,
    zx, gf, fsend, frcv, unf, pkf, frst, fpack, fret, facc, pacc, fpart, fout, fown, fstage, fback,
    i_sem, o_sem, w_sem, as_sem, ar_sem, ss_sem, sr_sem, ds_sem, dr_sem, zs_sem, zr_sem, bs_sem, br_sem,
    es_sem, er_sem, round_sem, xs_sem, xr_sem, fds_sem, fdr_sem, fes_sem, fer_sem, ys_sem, yr_sem,
):
    pick = wqkv.at[:, pl.ds(0, ALL)]
    fpick = wqkv.at[pl.ds(0, 4 * 256), pl.ds(ALL, ALLF)]
    d = lax.axis_index("dp")
    z = lax.axis_index("seq")
    zl = lax.rem(z + 3, 4)
    zr = lax.rem(z + 1, 4)
    zo = lax.rem(z + 2, 4)
    x, y, c = d // 8, lax.rem(d // 2, 4), lax.rem(d, 2)

    xs = [lax.rem(x + i, 4) * 8 for i in range(4)]
    ys = [lax.rem(y + i, 4) * 2 for i in range(4)]
    cs = [c, 1 - c]

    def shifted(n, sign):
        dx, dy, dc = OFFSETS[n]
        return xs[sign * dx % 4] + ys[sign * dy % 4] + cs[dc]

    def rows_of(j):
        return pl.ds(j * MSG, MSG)

    def frows_of(j):
        return pl.ds(j * FMSG, FMSG)

    small = [(tok_h, tok), (lna_h, lna), (eid_h, eid), (seg_h, seg), (gate_h, gate), (lne_h, lne)]
    small = [pltpu.make_async_copy(src, dst, i_sem.at[n]) for n, (src, dst) in enumerate(small)]
    for copy in small:
        copy.start()
    loads = []
    for i in range(3):
        part_of = pl.ds(i * D, D)
        loads.append(pltpu.make_async_copy(wqkv_h.at[:, part_of], wqkv.at[:, part_of], w_sem.at[i]))
    loads.append(pltpu.make_async_copy(wao_h, wao, w_sem.at[3]))
    loads.append(pltpu.make_async_copy(win_h, win, w_sem.at[4]))
    loads.append(pltpu.make_async_copy(wout_h, wout, w_sem.at[5]))
    barrier = pltpu.get_barrier_semaphore()
    for other in (zl, zr, zo):
        pl.semaphore_signal(barrier, inc=1, device_id=(d, other), device_id_type=MESH)

    x_line = [xs[i] + ys[0] + cs[0] for i in range(1, 4)]
    y_line = [xs[0] + ys[i] + cs[0] for i in range(1, 4)]
    twin = xs[0] + ys[0] + cs[1]
    for other in x_line + y_line + [twin]:
        pl.semaphore_signal(barrier, inc=1, device_id=(other, z), device_id_type=MESH)

    pl.semaphore_wait(barrier, 10)

    def remote(src, dst, s_sem, r_sem, dev):
        return pltpu.make_async_remote_copy(
            src_ref=src, dst_ref=dst, send_sem=s_sem, recv_sem=r_sem,
            device_id=dev, device_id_type=MESH,
        )

    right, left, across = (d, zr), (d, zl), (d, zo)

    def xrows(slot, half):
        rows = pl.ds(slot * TOK + half * 64, 64)
        return tok_h.at[pl.ds(half * 64, 64), :] if slot == 0 else xraw.at[rows, :]

    seg_copies = [
        remote(info.at[0], info.at[1], ss_sem.at[0], sr_sem.at[0], right),
        remote(info.at[0], info.at[2], ss_sem.at[1], sr_sem.at[1], left),
        remote(info.at[0], info.at[3], ss_sem.at[2], sr_sem.at[2], across),
    ]
    r0 = remote(xrows(0, 0), xrows(1, 0), as_sem.at[0], ar_sem.at[0], right)
    r1 = remote(xrows(0, 1), xrows(1, 1), as_sem.at[1], ar_sem.at[1], right)
    l1 = remote(xrows(0, 1), xrows(2, 1), as_sem.at[2], ar_sem.at[2], left)
    l0 = remote(xrows(0, 0), xrows(2, 0), as_sem.at[3], ar_sem.at[3], left)
    ro = remote(xrows(1, 0), xrows(3, 0), as_sem.at[4], ar_sem.at[4], right)
    lo = remote(xrows(2, 1), xrows(3, 1), as_sem.at[5], ar_sem.at[5], left)
    r0.start()
    l1.start()
    r1.start()
    l0.start()
    for load in loads:
        load.start()
    for copy in small:
        copy.wait()

    e0, e1 = eid[0:1, :], eid[1:2, :]
    ei = iota((NE, TOK), 0)
    named = jnp.where((ei == e0) | (ei == e1), 1.0, 0.0).astype(BF16)
    before = jnp.where(iota((TOK, TOK), 0) < iota((TOK, TOK), 1), 1.0, 0.0).astype(BF16)
    count = dot(named, before)
    order = jnp.full((NE, TOK), NE - 1, I32)
    for n in range(NE - 1):
        order = jnp.where(ei == shifted(n, 1), n, order)
    chosen = []
    lines = [seg[...].astype(F32)]
    for e in (e0, e1):
        slot = jnp.sum(jnp.where(ei == e, count, 0.0), axis=0, keepdims=True).astype(I32)
        e = jnp.sum(jnp.where(ei == e, order, 0), axis=0, keepdims=True)
        lines.append((e * FMSG + slot).astype(F32))
        odd = slot & 1
        pair = e * MSG + 3 * CAP + lax.shift_right_logical(slot, 1)
        chosen.append(
            (e * MSG + slot, jnp.where(odd == 0, pair, -1), jnp.where(odd == 1, pair, -1))
        )
    lines += [gate[0:1, :], gate[1:2, :]]
    ri = iota((8, TOK), 0)

    def stacked_lines(rows):
        total = jnp.zeros((8, TOK), F32)
        for n, row in enumerate(rows):
            total = jnp.where(ri == n, row, total)
        return total

    info[0] = stacked_lines(lines)
    for copy in seg_copies:
        copy.start()
    xn[pl.ds(0, TOK), :] = normalize(tok[...].astype(F32), lna[...].reshape(1, D)).astype(BF16)

    for other in x_line:
        pl.semaphore_signal(round_sem.at[0], inc=1, device_id=(other, z), device_id_type=MESH)

    def place(kind, cc):
        return chosen[kind][0] + CAP * cc if cc < 3 else chosen[kind][cc - 2]

    def make_g(i):
        rows = pl.ds(i * 256, 256)
        r = iota((256, TOK), 0) + i * 256
        for cc in range(NC):
            hit = (r == place(0, cc)) | (r == place(1, cc))
            g[rows, cc * TOK : (cc + 1) * TOK] = jnp.where(hit, 1.0, 0.0).astype(BF16)

    each(ALL // 256, make_g)

    def fixed(ref, q_dim, rows, first, base, msg):
        q = iota(ref.shape, q_dim)
        r = iota(ref.shape, 1 - q_dim) + base
        times, shift = {64: (1, 6), 80: (205, 14), CR: (1821, 18)}[rows]
        cc = lax.shift_right_logical(q * times, shift)
        i = q - cc * rows + first
        source = lax.shift_right_logical(i * 57, 9)
        slot = i - CAP * source
        at = source * msg + CAP * cc + slot
        if msg == MSG:
            pair = source * msg + 3 * CAP + lax.shift_right_logical(slot, 1)
            at = jnp.where(cc < 3, at, jnp.where((slot & 1) == cc - 3, pair, -1))
        ref[...] = jnp.where(r == at, 1.0, 0.0).astype(BF16)


    r0.wait_recv()
    ro.start()
    l1.wait_recv()
    lo.start()

    pl.semaphore_wait(round_sem.at[0], 3)
    pl.semaphore_signal(round_sem.at[1], inc=1, device_id=(twin, z), device_id_type=MESH)

    for load in loads[:3]:
        load.wait()

    def own_q(j):
        q[:, cols(j)] = dot(xn[pl.ds(0, TOK), :], wqkv[:, cols(j)]).astype(BF16)

    each(NC, own_q)

    def keys_values(first, number):
        rows = pl.ds(first, number)
        if first:
            xn[rows, :] = normalize(xraw[rows, :].astype(F32), lna[...].reshape(1, D)).astype(BF16)

        def step(j):
            k[rows, cols(j)] = dot(xn[rows, :], wqkv[:, cols(j + NC)]).astype(BF16)
            v[rows, cols(j)] = dot(xn[rows, :], wqkv[:, cols(j + 2 * NC)]).astype(BF16)

        each(NC, step)

    keys_values(0, TOK)

    r1.wait_recv()
    l0.wait_recv()
    keys_values(TOK, 2 * TOK)

    for copy in seg_copies:
        copy.wait_recv()
    eight = iota((8, TOK), 0).astype(F32)
    kinds = [jnp.where(eight == info[s, 0:1, :], 1.0, 0.0).astype(BF16) for s in range(4)]
    key_kind = jnp.concatenate(kinds, axis=1)
    same = lax.dot_general(kinds[0], key_kind, (((0,), (0,)), ((), ())), preferred_element_type=F32)
    bias = jnp.where(same > 0.5, 0.0, NEG)

    ro.wait_recv()
    lo.wait_recv()
    keys_values(3 * TOK, TOK)

    scale = HEAD ** (-0.5)
    ctx[...] = jnp.zeros((TOK, D), F32)
    for half in range(2):
        for heads, at in GROUPS:
            window = pl.ds(half * 640 + at, COL)
            lane = iota((TOK, COL), 1) + at
            masks = [(lane >= h * HEAD) & (lane < (h + 1) * HEAD) for h in heads]
            qw = q[:, window]
            zero = jnp.zeros_like(qw)
            stacked = jnp.concatenate([jnp.where(m, qw, zero) for m in masks], axis=0)
            scores = lax.dot_general(
                stacked, k[:, window], (((1,), (1,)), ((), ())), preferred_element_type=F32
            )
            probs, sums = [], []
            for n in range(len(heads)):
                s = scores[n * TOK : (n + 1) * TOK, :] * scale + bias
                w = jnp.exp(s - jnp.max(s, axis=-1, keepdims=True))
                sums.append(jnp.sum(w, axis=-1, keepdims=True))
                probs.append(w.astype(BF16))
            mixed = dot(jnp.concatenate(probs, axis=0), v[:, window])
            total = ctx[:, window]
            for n, m in enumerate(masks):
                total = jnp.where(m, mixed[n * TOK : (n + 1) * TOK, :] / sums[n], total)
            ctx[:, window] = total
    ctxb[...] = ctx[...].astype(BF16)

    loads[3].wait()

    def project(j):
        mid[:, cols(j)] = tok[:, cols(j)].astype(F32) + dot(ctxb[...], wao[:, cols(j)])

    each(NC, project)
    expert_in = normalize(mid[...], lne[...].reshape(1, D)).astype(BF16)
    zx[pl.ds(0, TOK), :] = expert_in[:, PW:]

    def zrows(slot, half):
        return zx.at[pl.ds(slot * TOK + half * 64, 64), :]

    xr0 = remote(zrows(0, 0), zrows(1, 0), xs_sem.at[0], xr_sem.at[0], right)
    xr1 = remote(zrows(0, 1), zrows(1, 1), xs_sem.at[1], xr_sem.at[1], right)
    xl1 = remote(zrows(0, 1), zrows(2, 1), xs_sem.at[2], xr_sem.at[2], left)
    xl0 = remote(zrows(0, 0), zrows(2, 0), xs_sem.at[3], xr_sem.at[3], left)
    xro = remote(zrows(1, 0), zrows(3, 0), xs_sem.at[4], xr_sem.at[4], right)
    xlo = remote(zrows(2, 1), zrows(3, 1), xs_sem.at[5], xr_sem.at[5], left)
    ring = [xr0, xr1, xl1, xl0, xro, xlo]
    for copy in ring[:4]:
        copy.start()

    for cc in range(3):
        xp[pl.ds(cc * TOK, TOK), :] = expert_in[:, cc * COL : (cc + 1) * COL]
    rest = expert_in[:, 3 * COL : PW]
    none = jnp.zeros_like(rest)
    xp[pl.ds(3 * TOK, TOK), :] = jnp.concatenate([rest, none], axis=1)
    xp[pl.ds(4 * TOK, TOK), :] = jnp.concatenate([none, rest], axis=1)

    def fill(i):
        rows = pl.ds(i * 256, 256)
        send[rows, :] = dot(g[rows, :], xp[...]).astype(BF16)


    pl.semaphore_wait(round_sem.at[1], 1)

    def to_experts(first, last):
        for n in range(first, last):
            dest = shifted(n, 1)
            remote(
                send.at[rows_of(n), :], rcv.at[rows_of(n), :],
                ds_sem, dr_sem.at[n // GS], (dest, z),
            ).start()

    for i in range(2):
        fill(i)
        to_experts(i * GS, (i + 1) * GS)
    xr0.wait_recv()
    xro.start()
    xl1.wait_recv()
    xlo.start()
    for i in range(2, 4):
        fill(i)
        to_experts(i * GS, min((i + 1) * GS, NE - 1))
    rcv[rows_of(NE - 1), :] = send[rows_of(NE - 1), :]

    fixed(unp0, 0, 64, 0, 0, MSG)
    fixed(unp1, 0, 80, 64, 7 * MSG, MSG)
    for s in range(4):
        r = iota((ALLF, TOK), 0) - CAP * s
        f0, f1 = info[s, 1:2, :].astype(I32), info[s, 2:3, :].astype(I32)
        gf[:, s * TOK : (s + 1) * TOK] = jnp.where((r == f0) | (r == f1), 1.0, 0.0).astype(BF16)

    def piece_of(slot, half, n):
        first, number = OUT[n]
        return a.at[slot, half, pl.ds(first, number), pl.ds(0, PW)]

    def arrived(group):
        number = GS if group < 3 else GS - 1
        got = rcv.at[pl.ds(group * GM, number * MSG), :]
        remote(got, got, ds_sem, dr_sem.at[group], right).wait_recv()

    def unpack(half, n):
        first, number = OUT[n]
        arrived(2 * half + n)
        base = half * 2 * GM
        if n == 0:
            got = dot(unp0[...], rcv[pl.ds(base, GM), :])
        else:
            got = dot(unp1[...], rcv[pl.ds(base + 7 * MSG, 9 * MSG), :])
        rows = slice(first, first + number)
        for cc in range(3):
            a[0, half, rows, cc * COL : (cc + 1) * COL] = got[
                cc * number : (cc + 1) * number
            ].astype(BF16)
        a[0, half, rows, 3 * COL : PW] = (
            got[3 * number : 4 * number, :128] + got[4 * number :, 128:]
        ).astype(BF16)

    zc = {}
    for half in range(2):
        for n in range(2):
            m = 2 * half + n
            zc["r", half, n] = remote(
                piece_of(0, half, n), piece_of(1, half, n), zs_sem.at[m], zr_sem.at[m], right
            )
            zc["l", half, n] = remote(
                piece_of(0, half, n), piece_of(2, half, n), zs_sem.at[4 + m], zr_sem.at[4 + m], left
            )
    for n in range(2):
        zc["ro", n] = remote(
            piece_of(1, 0, n), piece_of(3, 0, n), zs_sem.at[8 + n], zr_sem.at[8 + n], right
        )
        zc["lo", n] = remote(
            piece_of(2, 1, n), piece_of(3, 1, n), zs_sem.at[10 + n], zr_sem.at[10 + n], left
        )

    def expert(slot, half, store):
        def first(j):
            hid[:, cols(j)] = gelu(dot(a[slot, half], win[:, cols(j)])).astype(BF16)

        each(NC, first)
        for j in range(3):
            store(cols(j), dot(hid[...], wout[:, cols(j)]))
        value = dot(hid[...], wout[:, 3 * COL :])
        store(pl.ds(3 * COL, 128), value[:, :128])
        frst[half, pl.ds(slot * CR, CR), :] = value[:, 128:].astype(BF16)

    def into_own(half):
        def store(at, value):
            own[half, :, at] = value

        return store

    def into_part(n):
        def store(at, value):
            part[n, :, at] = value.astype(BF16)

        return store

    def into_keep(n):
        def store(at, value):
            keep[n, :, at] = value

        return store

    def back_of(ref, slot, n):
        first, number = BACK[n]
        return ref.at[slot, pl.ds(first, number)]

    b_left0 = remote(part.at[0], back.at[2], bs_sem.at[0], br_sem.at[0], left)
    b_right1 = remote(part.at[1], back.at[1], bs_sem.at[1], br_sem.at[1], right)
    bc = {}
    for n in range(2):
        for m, (key, src, dst, at, dev) in enumerate(
            (
                ("across0", 2, stage, 0, right),
                ("across1", 3, stage, 1, left),
                ("right0", 4, back, 0, right),
                ("left1", 5, back, 3, left),
            )
        ):
            bc[key, n] = remote(
                back_of(part, src, n), back_of(dst, at, n),
                bs_sem.at[2 + 2 * m + n], br_sem.at[2 + 2 * m + n], dev,
            )

    loads[4].wait()
    loads[5].wait()

    for n in range(2):
        unpack(0, n)
        zc["r", 0, n].start()
        zc["l", 0, n].start()
    for copy in (xr1, xl0, xro, xlo):
        copy.wait_recv()
    for half in range(2):
        rows = pl.ds(half * HALF * FMSG, HALF * FMSG)
        fsend[rows, :] = dot(gf[rows, :], zx[...]).astype(BF16)
        for n in range(half * HALF, min((half + 1) * HALF, NE - 1)):
            dest = shifted(n, 1)
            remote(
                fsend.at[frows_of(n), :], frcv.at[frows_of(n), :],
                fds_sem, fdr_sem.at[half], (dest, z),
            ).start()
    frcv[frows_of(NE - 1), :] = fsend[frows_of(NE - 1), :]
    for n in range(2):
        unpack(1, n)
        zc["r", 1, n].start()
        zc["l", 1, n].start()

    for s in range(4):
        more = jnp.zeros((8, TOK), F32)
        if s == 0:
            more = stacked_lines([row.astype(F32) for kind in chosen for row in kind])
        square = jnp.concatenate([info[s], more, jnp.zeros((TOK - 16, TOK), F32)], axis=0)
        gcol[s] = jnp.transpose(square)
    fixed(unf, 0, CR, 0, 0, FMSG)

    ri = iota((TOK, ALL), 1)
    for cc in range(NC):
        line = 8 if cc < 3 else 6 + cc
        for kind in range(2):
            at = gcol[0, :, line + 3 * kind : line + 3 * kind + 1].astype(I32)
            at = at + CAP * cc if cc < 3 else at
            pick[pl.ds(cc * 256 + kind * TOK, TOK), :] = jnp.where(ri == at, 1.0, 0.0).astype(BF16)
    for n in range(2):
        zc["r", 0, n].wait_recv()
        zc["ro", n].start()
    fi = iota((TOK, ALLF), 1)
    for s in range(4):
        for kind in range(2):
            at = gcol[s, :, 1 + kind : 2 + kind].astype(I32) + CAP * s
            fpick[pl.ds(s * 256 + kind * TOK, TOK), :] = jnp.where(fi == at, 1.0, 0.0).astype(BF16)
    fixed(pkf, 1, CR, 0, 0, FMSG)
    for n in range(2):
        zc["l", 1, n].wait_recv()
        zc["lo", n].start()
    fixed(pkm0, 1, 80, 0, 0, MSG)
    fixed(pkm1, 1, 80, 64, GM, MSG)

    def funpack(half):
        number = HALF if half == 0 else HALF - 1
        got = frcv.at[pl.ds(half * HALF * FMSG, number * FMSG), :]
        remote(got, got, fds_sem, fdr_sem.at[half], right).wait_recv()
        rows = dot(unf[...], frcv[pl.ds(half * HALF * FMSG, HALF * FMSG), :]).astype(BF16)
        for s in range(4):
            a[s, half, :, PW:] = rows[s * CR : (s + 1) * CR]

    def freturn(half):
        for group in (2 * half, 2 * half + 1):
            rows = pl.ds((group - 2 * half) * FGM, FGM)
            fpack[pl.ds(group * FGM, FGM), :] = dot(pkf[rows, :], frst[half]).astype(BF16)
            for m in range(group * GS, min((group + 1) * GS, NE - 1)):
                dest = shifted(m, -1)
                remote(
                    fpack.at[frows_of(m), :], fret.at[frows_of(m), :],
                    fes_sem, fer_sem.at[half], (dest, z),
                ).start()

    funpack(0)
    expert(1, 0, into_part(0))
    b_left0.start()
    for n in range(2):
        zc["l", 0, n].wait_recv()
    expert(2, 0, into_keep(0))
    expert(0, 0, into_own(0))
    for n in range(2):
        zc["ro", n].wait_recv()
    expert(3, 0, into_part(2))
    bc["across0", 0].start()
    bc["across0", 1].start()
    freturn(0)
    for n in range(2):
        zc["r", 1, n].wait_recv()
        zc["lo", n].wait_recv()
    funpack(1)
    expert(3, 1, into_part(3))
    bc["across1", 0].start()
    bc["across1", 1].start()
    expert(2, 1, into_part(1))
    b_right1.start()
    expert(1, 1, into_keep(1))
    expert(0, 1, into_own(1))
    freturn(1)
    fret[frows_of(NE - 1), :] = fpack[frows_of(NE - 1), :]
    for n in range(2):
        first, number = BACK[n]
        rows = pl.ds(first, number)
        bc["across0", n].wait_recv()
        part[4, rows] = (keep[0, rows] + stage[0, rows].astype(F32)).astype(BF16)
        bc["right0", n].start()
        bc["across1", n].wait_recv()
        part[5, rows] = (keep[1, rows] + stage[1, rows].astype(F32)).astype(BF16)
        bc["left1", n].start()

    def half_of(ref, slot, n):
        return ref.at[slot, pl.ds(n * 64, 64)]

    ya0 = remote(half_of(fout, 3, 0), fstage.at[0], ys_sem.at[0], yr_sem.at[0], right)
    ya1 = remote(half_of(fout, 3, 1), fstage.at[1], ys_sem.at[1], yr_sem.at[1], left)
    yl0 = remote(half_of(fout, 1, 0), half_of(fback, 1, 0), ys_sem.at[2], yr_sem.at[2], left)
    yr1 = remote(half_of(fout, 2, 1), half_of(fback, 0, 1), ys_sem.at[3], yr_sem.at[3], right)
    yr0 = remote(half_of(fout, 2, 0), half_of(fback, 0, 0), ys_sem.at[4], yr_sem.at[4], right)
    yl1 = remote(half_of(fout, 1, 1), half_of(fback, 1, 1), ys_sem.at[5], yr_sem.at[5], left)
    ring += [ya0, ya1, yl0, yr1, yr0, yl1]

    b_left0.wait_recv()
    b_right1.wait_recv()
    def finish(n):
        first, number = BACK[n]
        rows = pl.ds(first, number)
        for half in range(2):
            bc["right0" if half == 0 else "left1", n].wait_recv()
            for cc in range(4):
                at = slice(cc * COL, min((cc + 1) * COL, PW))
                full = (
                    own[half, rows, at]
                    + back[half, rows, at].astype(F32)
                    + back[2 + half, rows, at].astype(F32)
                ).astype(BF16)
                both = [full]
                if cc == 3:
                    none = jnp.zeros_like(full)
                    both = [
                        jnp.concatenate([full, none], axis=1),
                        jnp.concatenate([none, full], axis=1),
                    ]
                for m, value in enumerate(both):
                    if n == 0:
                        rst[half, 0, pl.ds((cc + m) * 80, 80), :] = value
                        rst[half, 1, pl.ds((cc + m) * 80, 16), :] = value[64:]
                    else:
                        rst[half, 1, pl.ds((cc + m) * 80 + 16, 64), :] = value
            packed = dot((pkm0 if n == 0 else pkm1)[...], rst[half, n])
            group = 2 * half + n
            pack[pl.ds(group * GM, GM), :] = packed.astype(BF16)
            for m in range(group * GS, min((group + 1) * GS, NE - 1)):
                dest = shifted(m, -1)
                remote(
                    pack.at[rows_of(m), :], ret.at[rows_of(m), :],
                    es_sem, er_sem.at[group], (dest, z),
                ).start()
    def fhalf(half):
        number = HALF if half == 0 else HALF - 1
        got = fret.at[pl.ds(half * HALF * FMSG, number * FMSG), :]
        remote(got, got, fes_sem, fer_sem.at[half], right).wait_recv()

    early = pl.ds(0, HALF * FMSG)
    late = pl.ds(HALF * FMSG, HALF * FMSG)
    fhalf(0)
    facc[...] = dot(fpick[:, early], fret[early, :])
    finish(0)
    fhalf(1)

    def weighted(both, s):
        return gcol[s, :, 3:4] * both[:TOK] + gcol[s, :, 4:5] * both[TOK:]

    rows = pl.ds(3 * 256, 256)
    fout[3] = weighted(facc[rows, :] + dot(fpick[rows, late], fret[late, :]), 3).astype(BF16)
    ya0.start()
    ya1.start()
    rows = pl.ds(0, 3 * 256)
    both = facc[rows, :] + dot(fpick[rows, late], fret[late, :])
    for s in range(3):
        sums = weighted(both[s * 256 : (s + 1) * 256], s)
        if s == 0:
            fown[...] = sums
        else:
            fpart[s] = sums
            fout[s] = sums.astype(BF16)
    yl0.start()
    yr1.start()

    finish(1)
    ret[rows_of(NE - 1), :] = pack[rows_of(NE - 1), :]

    ya0.wait_recv()
    fout[2, pl.ds(0, 64)] = (fpart[2, pl.ds(0, 64)] + fstage[0].astype(F32)).astype(BF16)
    yr0.start()
    ya1.wait_recv()
    fout[1, pl.ds(64, 64)] = (fpart[1, pl.ds(64, 64)] + fstage[1].astype(F32)).astype(BF16)
    yl1.start()

    def returned(group):
        number = GS if group < 3 else GS - 1
        got = ret.at[pl.ds(group * GM, number * MSG), :]
        remote(got, got, es_sem, er_sem.at[group], right).wait_recv()
        return pl.ds(group * GM, GM)

    first, second = returned(0), returned(2)
    pacc[...] = dot(pick[:, first], ret[first, :]) + dot(pick[:, second], ret[second, :])
    first, second = returned(1), returned(3)
    picked = dot(pick[:, first], ret[first, :]) + dot(pick[:, second], ret[second, :])
    picked = pacc[...] + picked
    g0, g1 = gcol[0, :, 3:4], gcol[0, :, 4:5]
    for cc in range(3):
        both = picked[cc * 256 : (cc + 1) * 256]
        out[:, cols(cc)] = (mid[:, cols(cc)] + g0 * both[:TOK] + g1 * both[TOK:]).astype(BF16)
    both = picked[3 * 256 : 4 * 256, :128] + picked[4 * 256 :, 128:]
    out[:, 3 * COL : PW] = (
        mid[:, 3 * COL : PW] + g0 * both[:TOK] + g1 * both[TOK:]
    ).astype(BF16)
    leave = [
        pltpu.make_async_copy(out.at[:, at], out_h.at[:, at], o_sem.at[n])
        for n, at in enumerate((pl.ds(0, PW), pl.ds(PW, FW)))
    ]
    leave[0].start()
    for copy in (yl0, yr1, yr0, yl1):
        copy.wait_recv()
    out[:, PW:] = (
        mid[:, PW:] + fown[...] + fback[0].astype(F32) + fback[1].astype(F32)
    ).astype(BF16)

    leave[1].start()

    for copy in seg_copies + [r0, r1, l0, l1, ro, lo] + ring + list(zc.values()):
        copy.wait_send()
    for copy in [b_left0, b_right1] + list(bc.values()):
        copy.wait_send()
    gone = send.at[pl.ds(0, (NE - 1) * MSG), :]
    remote(gone, gone, ds_sem, dr_sem.at[0], right).wait_send()
    gone = pack.at[pl.ds(0, (NE - 1) * MSG), :]
    remote(gone, gone, es_sem, er_sem.at[0], right).wait_send()
    gone = fsend.at[pl.ds(0, (NE - 1) * FMSG), :]
    remote(gone, gone, fds_sem, fdr_sem.at[0], right).wait_send()
    gone = fpack.at[pl.ds(0, (NE - 1) * FMSG), :]
    remote(gone, gone, fes_sem, fer_sem.at[0], right).wait_send()
    for copy in leave:
        copy.wait()


def layer(tok, seg, eid, gate, lna, lne, wqkv, wao, win, wout):
    hbm = pl.BlockSpec(memory_space=pl.ANY)
    V = pltpu.VMEM
    dma = pltpu.SemaphoreType.DMA
    return pl.pallas_call(
        kernel,
        out_shape=jax.ShapeDtypeStruct((TOK, D), BF16),
        in_specs=[hbm] * 10,
        out_specs=hbm,
        scratch_shapes=[
            V((TOK, D), BF16),
            V((TOK, D), BF16),
            V((1, TOK), I32),
            V((2, TOK), I32),
            V((2, TOK), F32),
            V((D,), F32),
            V((D,), F32),
            V((D, 3 * D), BF16),
            V((D, D), BF16),
            V((D, D), BF16),
            V((D, D), BF16),
            V((4 * TOK, D), BF16),
            V((4 * TOK, D), BF16),
            V((4, 8, TOK), F32),
            V((TOK, D), BF16),
            V((4 * TOK, D), BF16),
            V((4 * TOK, D), BF16),
            V((TOK, D), F32),
            V((TOK, D), BF16),
            V((TOK, D), F32),
            V((NC * TOK, COL), BF16),
            V((ALL, NC * TOK), BF16),
            V((ALL, COL), BF16),
            V((ALL, COL), BF16),
            V((4, 2, CR, D), BF16),
            V((CR, D), BF16),
            V((6, CR, PW), BF16),
            V((2, CR, PW), F32),
            V((2, CR, PW), F32),
            V((2, CR, PW), BF16),
            V((4, CR, PW), BF16),
            V((2, 2, NC * 80, COL), BF16),
            V((ALL, COL), BF16),
            V((ALL, COL), BF16),
            V((NC * 64, GM), BF16),
            V((NC * 80, 9 * MSG), BF16),
            V((GM, NC * 80), BF16),
            V((GM, NC * 80), BF16),
            V((4, TOK, TOK), F32),
            V((4 * TOK, FW), BF16),
            V((ALLF, 4 * TOK), BF16),
            V((ALLF, FW), BF16),
            V((ALLF, FW), BF16),
            V((4 * CR, HALF * FMSG), BF16),
            V((HALF * FMSG, 4 * CR), BF16),
            V((2, 4 * CR, FW), BF16),
            V((ALLF, FW), BF16),
            V((ALLF, FW), BF16),
            V((4 * 256, FW), F32),
            V((NC * 256, COL), F32),
            V((4, TOK, FW), F32),
            V((4, TOK, FW), BF16),
            V((TOK, FW), F32),
            V((2, 64, FW), BF16),
            V((2, TOK, FW), BF16),
            dma((6,)),
            dma((2,)),
            dma((6,)),
            dma((6,)),
            dma((6,)),
            dma((3,)),
            dma((3,)),
            dma,
            dma((4,)),
            dma((12,)),
            dma((12,)),
            dma((10,)),
            dma((10,)),
            dma,
            dma((4,)),
            pltpu.SemaphoreType.REGULAR((2,)),
            dma((6,)),
            dma((6,)),
            dma,
            dma((2,)),
            dma,
            dma((2,)),
            dma((6,)),
            dma((6,)),
        ],
        compiler_params=pltpu.CompilerParams(
            collective_id=0, has_side_effects=True, vmem_limit_bytes=60 * 1024 * 1024
        ),
        cost_estimate=pl.CostEstimate(
            flops=14_000_000_000, bytes_accessed=24_000_000, transcendentals=3_000_000
        ),
    )(tok, seg, eid, gate, lna, lne, wqkv, wao, win, wout)


def body(
    tokens, segment_ids, expert_ids, gate_values, ln_attn, w_qkv, w_attn_out, ln_expert, w_in, w_out
):
    out = layer(
        tokens[0],
        segment_ids,
        expert_ids[0].T,
        gate_values[0].T,
        ln_attn,
        ln_expert,
        w_qkv,
        w_attn_out,
        w_in[0],
        w_out[0],
    )
    return out[None]


def solution(mesh):
    placed = (
        P("dp", "seq", None),
        P("dp", "seq"),
        P("dp", "seq", None),
        P("dp", "seq", None),
        P(),
        P(),
        P(),
        P(),
        P("dp", None, "seq"),
        P("dp", "seq", None),
    )
    return jax.shard_map(
        body, mesh=mesh, in_specs=placed, out_specs=P("dp", "seq", None), check_vma=False
    )
```
